256 devices in a mesh: wide: 64 (over y, z, core), narrow: 4 (over x).
Axes of the slice: x: 4, y: 4, z: 8, core: 2. Of those that a mesh axis runs over, the one named last changes fastest.
Arguments:
- item_owner: int32 [512, 512, 1], P(('wide', 'narrow')), may hold values from 0 to 63; in each aligned block of 1024 rows (0 to 1023, 1024 to 2047, ..., all dimensions but the last counted through in order) at most 24 rows name the same one
- item_row: int32 [512, 512], P(('wide', 'narrow')), may hold values from 0 to 1023
- hot_row: int32 [512, 512], P(('wide', 'narrow')), may hold values from 0 to 1023
- hot_flag: int32 [512, 512], P(('wide', 'narrow')), may hold values from 0 to 1, as said below
- seq_length: int32 [512], P(('wide', 'narrow')), may hold values from 256 to 512, as said below
- cold_table: bfloat16 [65536, 512], P('wide'), may hold values from -6 to 6
- hot_table: bfloat16 [1024, 512], replicated, may hold values from -6 to 6
- proj_weight: bfloat16 [512, 2048], replicated, may hold values from -0.25 to 0.25
- out_weight: bfloat16 [512, 512], replicated, may hold values from -0.25 to 0.25
- norm_gain: float32 [1, 512], replicated, may hold values from 0.5 to 1.5
- cotangent: bfloat16 [512, 512, 512], P(('wide', 'narrow')), may hold values from -6 to 6
Outputs:
- proj_grad: float32 [512, 2048], P(None, 'wide')
- out_grad: float32 [512, 512], P(None, 'wide')
- gain_grad: float32 [1, 512], P(None, 'wide')
- cold_grad: float32 [65536, 512], P(('wide', 'narrow'))
- hot_grad: float32 [1024, 512], P(('wide', 'narrow'))
The draws below stay inside these ranges and needn't reach their ends.
Inputs may be any that keep to these rules, and one draw needn't show every extreme that they name: `item_owner`: at most 24 of the token slots of one device (padding and hot ones included) name one owner; in every draw some device's slots name some owner exactly 24 times. `seq_length`: each is a multiple of 128; some history has the full 512. `hot_flag`: in every draw all token slots of some device are hot; that device's slots name 1024 different hot rows.
All inputs are finite; a program needn't handle non-finite values.
Results may differ from the reference program's by a relative error of at most 0.014.
Values may be sent and summed in bfloat16 or wider, within the bound.
A program may use at most 128 MiB of HBM per device.

```python
import math
import jax
import jax.numpy as jnp
import numpy as np
from jax import lax

D = 512
HEADS = 4
LEN = 512
BLOCK = 128
SEQ_DEV = 2
TOK_DEV = 1024
SEQS = 512
OWNERS = 64
CAP = 24
ROWS_DEV = 1024
ROWS = 65536
HOT = 1024


def hot_layout(key):
    flag_key, first_key, second_key, order_key, device_key, spread_key = jax.random.split(key, 6)
    blocks = SEQS // SEQ_DEV
    chosen = jax.random.randint(device_key, (), 0, blocks)
    device_ids = jnp.arange(blocks, dtype=jnp.int32)[:, None]
    full = device_ids == chosen
    sparse_flag = (jax.random.randint(flag_key, (blocks, TOK_DEV), 0, 8) == 0).astype(jnp.int32)
    flags = jnp.where(full, 1, sparse_flag)
    order = jax.random.permutation(order_key, HOT).astype(jnp.int32)
    first = jax.random.randint(first_key, (blocks, TOK_DEV), 0, HOT)
    second = jax.random.randint(second_key, (blocks, TOK_DEV), 0, HOT)
    skewed = order[jnp.minimum(first, second)]
    spread = jax.random.permutation(spread_key, HOT).astype(jnp.int32)
    distinct = spread[jnp.arange(TOK_DEV, dtype=jnp.int32) % HOT]
    rows = jnp.where(full, distinct[None, :], skewed)
    return (flags.reshape(SEQS, LEN).astype(jnp.int32), rows.reshape(SEQS, LEN).astype(jnp.int32))


def draw_hot_flag(key, part):
    return hot_layout(key)[0]


def draw_hot_row(key, part):
    return hot_layout(key)[1]


def draw_seq_length(key, part):
    key = jax.random.fold_in(key, 7)
    first, second = jax.random.split(key)
    blocks = jax.random.randint(first, (SEQS,), LEN // BLOCK // 2, LEN // BLOCK + 1)
    chosen = jax.random.randint(second, (), 0, SEQS)
    blocks = blocks.at[chosen].set(LEN // BLOCK)
    return (blocks * BLOCK).astype(jnp.int32)


def with_ends(array, rng, least, high):
    spot = [jax.random.randint(jax.random.fold_in(rng, axis), (), 0, length) for axis, length in enumerate(array.shape)]
    widest = array.shape.index(max(array.shape))
    neighbour = spot[:widest] + [(spot[widest] + 1) % array.shape[widest]] + spot[widest + 1:]
    return array.at[tuple(spot)].set(least).at[tuple(neighbour)].set(high)


def block_levels(own_key, extent, shards, low, largest):
    level = 1.0
    for dim, blocks in shards:
        steps = jax.random.uniform(jax.random.fold_in(jax.random.fold_in(own_key, 6), dim), (blocks,), jnp.float32, low / len(shards), largest / len(shards))
        level = level * jnp.repeat(jnp.exp(steps), extent[dim] // blocks).reshape((-1,) + (1,) * (len(extent) - 1 - dim))
    return level


def cumulative_ranks(count, lean):
    portions = [(1 << 20) // math.isqrt(standing ** lean) + 1 for standing in range(1, count + 1)]
    scale = 1 + sum(portions) // (1 << 30)
    return np.cumsum(np.array([max(1, weight // scale) for weight in portions]))


def ranked_ids(rng, extent, count, skew):
    listing = cumulative_ranks(count, skew)
    pick = jax.random.randint(jax.random.fold_in(rng, 1), extent, 0, int(listing[count - 1]))
    standing = jnp.searchsorted(jnp.asarray(listing, jnp.int32), pick, side="right")
    return jax.random.permutation(jax.random.fold_in(rng, 2), count)[standing].astype(jnp.int32)


def shared_out(own_key, own, number, rows, number_of, top, limit, slope):
    ranking = jax.random.permutation(own_key, number_of)
    packed, ordinary = portions_of(number_of, rows * top, limit, slope, True), portions_of(number_of, rows * top, limit, slope, False)
    places = jnp.arange(number_of)

    def named(tallies, rotation):
        used = int((tallies > 0).sum())
        fixed = max(1, used // 4)
        moved = fixed + (places - fixed + rotation * (used - fixed)) % max(1, number_of - fixed)
        return jnp.zeros((number_of,), jnp.int32).at[ranking[jnp.where(places < fixed, places, moved)]].set(jnp.asarray(tallies, jnp.int32))

    tallies = jnp.where(number % 4 == 0, named(packed, number // 4), named(ordinary, number - number // 4 - 1))
    mixed = jax.random.permutation(jax.random.fold_in(own, 3), number_of)
    source_of, receiver = mixed[0:number_of // 2 * 2:2], mixed[1:number_of // 2 * 2:2]
    slack = jnp.minimum(tallies[source_of] - 1, limit - tallies[receiver]) // 2
    slack = jnp.where((source_of == ranking[0]) | (receiver == ranking[0]) | (tallies[receiver] == 0), 0, jnp.maximum(slack, 0))
    moved = jax.random.randint(jax.random.fold_in(own, 4), (number_of // 2,), 0, 1 << 20) % (slack + 1)
    tallies = tallies.at[source_of].add(-moved).at[receiver].add(moved)
    items = jnp.searchsorted(jnp.cumsum(tallies), jnp.arange(rows * top), side="right").astype(jnp.int32)
    listing = items.reshape(top, rows).T
    listing = listing[jax.random.permutation(jax.random.fold_in(own, 1), rows)]
    rotation = jax.random.randint(jax.random.fold_in(own, 2), (rows, 1), 0, top)
    return jnp.take_along_axis(listing, (jnp.arange(top)[None, :] + rotation) % top, axis=1)


def portions_of(count, total, reach, slope, full):
    portions = [(1 << 20) // math.isqrt(grade ** slope) + 1 for grade in range(1, count + 1)]
    largest = reach if full else min(reach, max(-(-total // count), total * portions[0] // sum(portions)))
    least = 1 if total - largest >= count - 1 else 0
    given, surplus = [largest] + [least] * (count - 1), total - largest - least * (count - 1)
    while surplus > 0:
        candidates = [i for i in range(1, count) if given[i] < largest] or [i for i in range(1, count) if given[i] < reach]
        pool, budget = sum([portions[i] for i in candidates]), surplus
        for i in candidates:
            addition = min(reach - given[i], max(1, budget * portions[i] // pool), surplus)
            given[i] = given[i] + addition
            surplus = surplus - addition
    return np.array(given)


def gaussian(stream_key, extent, scale, bound, shards=(), held_as=jnp.bfloat16):
    drawn = scale * jax.random.normal(stream_key, extent, jnp.float32)
    if shards:
        drawn = drawn * block_levels(stream_key, extent, shards, -0.22, 0.18)
    return jnp.clip(drawn, -bound, bound).astype(held_as)


def setup_inputs(seed: int = 0) -> dict:
    key_of = jax.random.split(jax.random.key(seed), 12)
    item_owner_keys = jax.random.split(jax.random.fold_in(key_of[0], 1), SEQS * LEN // TOK_DEV)
    item_owner_turns = jax.random.permutation(jax.random.fold_in(key_of[0], 3), SEQS * LEN // TOK_DEV)
    item_owner = jax.vmap(lambda own, number: shared_out(jax.random.fold_in(key_of[0], 2), own, number, TOK_DEV, OWNERS, 1, CAP, 2))(item_owner_keys, item_owner_turns).reshape((SEQS, LEN, 1))
    item_row = with_ends(ranked_ids(key_of[1], (SEQS, LEN), ROWS_DEV, 2), jax.random.fold_in(key_of[1], 3), 0, ROWS_DEV - 1).astype(jnp.int32)
    hot_row = draw_hot_row(jax.random.fold_in(key_of[11], 71), 0)
    hot_flag = draw_hot_flag(jax.random.fold_in(key_of[11], 71), 0)
    seq_length = draw_seq_length(jax.random.fold_in(key_of[11], 71), 0)
    cold_table = gaussian(key_of[5], (ROWS, D), 1.0, 6.0, ((0, 64),))
    hot_table = gaussian(key_of[6], (HOT, D), 1.0, 6.0)
    proj_weight = gaussian(key_of[7], (D, 4 * D), D ** -0.5, 0.25)
    out_weight = gaussian(key_of[8], (D, D), D ** -0.5, 0.25)
    norm_gain = jnp.clip(1.0 + 0.1 * jax.random.normal(key_of[9], (1, D), jnp.float32), 0.5, 1.5)
    cotangent = gaussian(key_of[10], (SEQS, LEN, D), 1.0, 6.0, ((0, 256),))
    return dict(item_owner=item_owner, item_row=item_row, hot_row=hot_row, hot_flag=hot_flag, seq_length=seq_length, cold_table=cold_table, hot_table=hot_table, proj_weight=proj_weight, out_weight=out_weight, norm_gain=norm_gain, cotangent=cotangent)


epsilon = 1e-05

def layer_norm(values):
    center = values - lax.optimization_barrier(jnp.mean(values, axis=-1, keepdims=True))
    spread = lax.optimization_barrier(jnp.mean(center * center, axis=-1, keepdims=True))
    return center * lax.rsqrt(spread + epsilon)

def layer_grads(embedded, cotan, length, proj_weight, out_weight, norm_gain):
    seq_len, width = embedded.shape
    head_width = width // HEADS
    positions = jnp.arange(seq_len, dtype=jnp.int32)
    live = (positions < length).astype(jnp.float32)[:, None]
    masked = (cotan.astype(jnp.float32) * live).astype(jnp.bfloat16)

    def normalize(rows, scale):
        return layer_norm(rows) * scale
    normed_full, norm_back = jax.vjp(normalize, embedded.astype(jnp.float32), norm_gain)
    normed = normed_full.astype(jnp.bfloat16)
    projected = jnp.dot(normed, proj_weight, preferred_element_type=jnp.float32)
    allowed = ((positions[None, :] <= positions[:, None]) & (positions[None, :] < length)).astype(jnp.float32)
    inverse = 1.0 / length.astype(jnp.float32)

    def mixing(proj_rows):
        acted = jax.nn.silu(proj_rows).astype(jnp.bfloat16)
        gate_part = acted[:, :width].astype(jnp.float32)
        value_part = acted[:, width:2 * width].astype(jnp.float32).reshape(seq_len, HEADS, head_width)
        query_part = acted[:, 2 * width:3 * width].astype(jnp.float32).reshape(seq_len, HEADS, head_width)
        key_part = acted[:, 3 * width:].astype(jnp.float32).reshape(seq_len, HEADS, head_width)
        scores = jnp.einsum('qhd,khd->hqk', query_part, key_part) * head_width ** (-0.5)
        weights = (jax.nn.silu(scores) * allowed[None] * inverse).astype(jnp.bfloat16)
        per_head = jnp.einsum('hqk,khd->qhd', weights.astype(jnp.float32), value_part).reshape(seq_len, width)
        return (layer_norm(per_head) * gate_part).astype(jnp.bfloat16)
    mixed, mix_back = jax.vjp(mixing, projected)
    out_part = jnp.dot(mixed.T, masked, preferred_element_type=jnp.float32)
    mixed_cot = jnp.dot(masked, out_weight.T, preferred_element_type=jnp.float32).astype(jnp.bfloat16)
    proj_cot = mix_back(mixed_cot)[0].astype(jnp.bfloat16)
    proj_part = jnp.dot(normed.T, proj_cot, preferred_element_type=jnp.float32)
    normed_cot = jnp.dot(proj_cot, proj_weight.T, preferred_element_type=jnp.float32)
    emb_cot, gain_part = norm_back(normed_cot)
    emb_grad = ((masked.astype(jnp.float32) + emb_cot) * live).astype(jnp.bfloat16)
    return (emb_grad, proj_part, out_part, gain_part)

def reference(item_owner, item_row, hot_row, hot_flag, seq_length, cold_table, hot_table, proj_weight, out_weight, norm_gain, cotangent):
    width = cold_table.shape[1]
    cold_index = (item_owner[..., 0] * ROWS_DEV + item_row).astype(jnp.int32)
    from_cold = cold_table[cold_index]
    from_hot = hot_table[hot_row]
    embedded = jnp.where((hot_flag == 1)[..., None], from_hot, from_cold)

    def step(carry, inputs):
        rows, cotan, length = inputs
        emb_grad, proj_part, out_part, gain_part = layer_grads(rows, cotan, length, proj_weight, out_weight, norm_gain)
        return ((carry[0] + proj_part, carry[1] + out_part, carry[2] + gain_part), emb_grad)
    start = (jnp.zeros((width, 4 * width), jnp.float32), jnp.zeros((width, width), jnp.float32), jnp.zeros((1, width), jnp.float32))
    totals, emb_grads = lax.scan(step, start, (embedded, cotangent, seq_length))
    flat = emb_grads.reshape(-1, width).astype(jnp.float32)
    hot_mask = (hot_flag.reshape(-1) == 1)[:, None]
    hot_grad = jnp.zeros((HOT, width), jnp.float32).at[hot_row.reshape(-1)].add(jnp.where(hot_mask, flat, 0.0))
    cold_grad = jnp.zeros((ROWS, width), jnp.float32).at[cold_index.reshape(-1)].add(jnp.where(hot_mask, 0.0, flat))
    return (totals[0], totals[1], totals[2], cold_grad, hot_grad)
```

```python
import functools

import jax
import jax.numpy as jnp
from jax import lax
from jax.experimental import pallas as pl
from jax.experimental.pallas import tpu as pltpu
from jax.sharding import PartitionSpec as P

WIDE = 64
NARROW = 4
CAP = 24
TOK = 1024
LEN = 512
D = 512
HEADS = 4
ROWS = 1024
EPS = 1e-05
SCALE = 128 ** (-0.5)
MESH = pl.DeviceIdType.MESH
F32 = jnp.float32
BF16 = jnp.bfloat16


def mm(a, b):
    return jnp.dot(a, b, preferred_element_type=F32)


def mm_nt(a, b):
    return lax.dot_general(a, b, (((1,), (1,)), ((), ())), preferred_element_type=F32)


def mm_tn(a, b):
    return lax.dot_general(a, b, (((0,), (0,)), ((), ())), preferred_element_type=F32)


def iota(shape, dim):
    return lax.broadcasted_iota(jnp.int32, shape, dim).astype(F32)


def sigmoid(x):
    return 0.5 * jnp.tanh(0.5 * x) + 0.5


def onehot(mask):
    return jnp.where(mask, 1.0, 0.0).astype(BF16)


def mean(x):
    return jnp.mean(x, axis=-1, keepdims=True)


def pack(rows):
    blocks = rows.reshape(-1, CAP, D)
    return jnp.concatenate([blocks[:, :, : D // 2], blocks[:, :, D // 2 :]], axis=1).astype(BF16)


def unpack_into(dst, src):
    def step(i, carry):
        block = src[pl.ds(i * 8, 8)].astype(F32)
        rows = pl.ds(pl.multiple_of(i * 192, 192), 192)
        dst[rows, : D // 2] = block[:, :CAP].reshape(192, D // 2).astype(BF16)
        dst[rows, D // 2 :] = block[:, CAP:].reshape(192, D // 2).astype(BF16)
        return carry

    lax.fori_loop(0, 8, step, 0)


def kernel(
    tok, lens, table, hot_table, weight, out_weight, gain, cot,
    proj_out, out_out, gain_out, cold_out, hot_out,
    slots, req, want, reply, got, rows_in, place_t, hot_t, emb, normed, xhat, spread, acted, dact,
    attn, dattn, per_head, mixed, masked, mixed_cot, dhead, proj_cot, emb_grad, gain_sum,
    cold_send, cold_got, wsum, core_got, core_sum, x_got, x_sum, y_got, y_sum, z_got, gathered, cx_send, cx_got,
    loc_sem, a2a_send, a2a_recv, core_ss, core_rs, x_ss, x_rs, y_ss, y_rs, z_ss, z_rs, g_ss, g_rs, cx_ss, cx_rs,
):
    w = lax.axis_index("wide")
    n = lax.axis_index("narrow")
    core = lax.rem(w, 2)
    chip = lax.div(w, 2)
    z = lax.rem(chip, 8)
    y = lax.div(chip, 8)

    barrier = pltpu.get_barrier_semaphore()

    def greet(d, carry):
        pl.semaphore_signal(barrier, inc=1, device_id=(lax.rem(w + d, WIDE), n), device_id_type=MESH)
        return carry

    lax.fori_loop(1, WIDE, greet, 0)
    for d in range(1, NARROW):
        pl.semaphore_signal(barrier, inc=1, device_id=(w, lax.rem(n + d, NARROW)), device_id_type=MESH)

    upper = onehot(iota((128, 128), 0) < iota((128, 128), 1))
    sub = iota((128, 128), 0)
    carry = jnp.zeros((128, 1), F32)
    req_hi = jnp.zeros((128, 128), F32)
    req_lo = jnp.zeros((128, 128), F32)
    for a in range(8):
        own = tok[a : a + 1, :]
        row = tok[8 + a : 9 + a, :]
        hot = tok[16 + a : 17 + a, :]
        owns = jnp.where(sub == own, 1.0, 0.0)
        owns_b = owns.astype(BF16)
        before = mm(owns_b, upper) + carry
        rank = jnp.sum(owns * before, axis=0, keepdims=True)
        carry = carry + jnp.sum(owns, axis=1, keepdims=True)
        slots[a : a + 1, :] = jnp.where(hot >= 0.0, -1.0, own * CAP + rank)
        high = jnp.floor(row * (1.0 / 32.0))
        low = row - 32.0 * high
        ranked = sub == rank
        req_hi = req_hi + mm_nt(owns_b, jnp.where(ranked, high, 0.0).astype(BF16))
        req_lo = req_lo + mm_nt(owns_b, jnp.where(ranked, low, 0.0).astype(BF16))
    asked = 32.0 * req_hi + req_lo
    for o in range(WIDE):
        req[o] = asked[o : o + 1, :]

    pl.semaphore_wait(barrier, WIDE - 1 + NARROW - 1)

    def exchange(which, src, dst, p):
        return pltpu.make_async_remote_copy(
            src_ref=src.at[p], dst_ref=dst.at[w], send_sem=a2a_send.at[which], recv_sem=a2a_recv.at[which],
            device_id=(p, n), device_id_type=MESH,
        )

    def await_all(sem, ref):
        view = ref.at[pl.ds(0, WIDE - 1)]
        pltpu.make_async_copy(view, view, sem).wait()

    def ask(d, carry):
        exchange(0, req, want, lax.rem(w + d, WIDE)).start()
        return carry

    lax.fori_loop(1, WIDE, ask, 0)
    own_want = pltpu.make_async_copy(req.at[w], want.at[w], loc_sem.at[0])
    own_want.start()

    def build_place(a, carry):
        rows = pl.ds(pl.multiple_of(a * 192, 192), 192)
        at = iota((192, 128), 0) + (a * 192).astype(F32)
        for b in range(8):
            place_t[rows, b * 128 : (b + 1) * 128] = onehot(at == slots[b : b + 1, :])
        return carry

    lax.fori_loop(0, 8, build_place, 0)

    def build_hot(a, carry):
        rows = pl.ds(pl.multiple_of(a * 128, 128), 128)
        at = iota((128, 128), 0) + (a * 128).astype(F32)
        for b in range(8):
            hot_t[rows, b * 128 : (b + 1) * 128] = onehot(at == tok[16 + b : 17 + b, :])
        return carry

    lax.fori_loop(0, 8, build_hot, 0)

    own_want.wait()
    await_all(a2a_recv.at[0], want)

    lanes = iota((CAP, ROWS), 1)

    def answer(i, carry):
        first = lax.rem(lax.div(w, 8) + i, 8) * 8
        asked8 = want[pl.ds(first, 8)].reshape(8, 128).T
        picks = jnp.concatenate([jnp.where(lanes == asked8[:CAP, j : j + 1], 1.0, 0.0) for j in range(8)], axis=0)
        reply[pl.ds(first, 8)] = pack(mm(picks.astype(BF16), table[...]))
        for j in range(8):
            p = first + j

            @pl.when(p != w)
            def _():
                exchange(1, reply, got, p).start()

        return carry

    lax.fori_loop(0, 8, answer, 0)
    own_reply = pltpu.make_async_copy(reply.at[w], got.at[w], loc_sem.at[1])
    own_reply.start()

    tok_cols = tok[...].T
    for half in range(2):
        rows = slice(half * LEN, (half + 1) * LEN)
        hots = jnp.concatenate(
            [onehot(iota((128, TOK), 1) == tok_cols[:, 16 + a : 17 + a]) for a in range(half * 4, half * 4 + 4)], axis=0
        )
        emb[rows, :] = mm(hots, hot_table[...]).astype(BF16)
        live = iota((LEN, 1), 0) < lens[half].astype(F32)
        masked[rows, :] = jnp.where(live, cot[rows, :].astype(F32), 0.0).astype(BF16)
        mixed_cot[rows, :] = mm_nt(masked[rows, :], out_weight[...]).astype(BF16)

    own_reply.wait()
    await_all(a2a_recv.at[1], got)
    unpack_into(rows_in, got)
    slot_cols = slots[...].T
    for half in range(2):
        rows = slice(half * LEN, (half + 1) * LEN)
        picks = jnp.concatenate(
            [onehot(iota((128, WIDE * CAP), 1) == slot_cols[:, a : a + 1]) for a in range(half * 4, half * 4 + 4)], axis=0
        )
        emb[rows, :] = (mm(picks, rows_in[...]) + emb[rows, :].astype(F32)).astype(BF16)

    gain_sum[...] = jnp.zeros_like(gain_sum)

    def layer(s, carry):
        base = s * LEN
        rows = pl.ds(pl.multiple_of(base, LEN), LEN)
        length = lens[s].astype(F32)

        def norm(t, c):
            part = pl.ds(pl.multiple_of(base + t * 256, 256), 256)
            x = emb[part, :].astype(F32)
            center = x - mean(x)
            r = lax.rsqrt(mean(center * center) + EPS)
            hat = center * r
            xhat[part, :] = hat
            spread[part, :] = r
            normed[part, :] = (hat * gain[...]).astype(BF16)
            return c

        lax.fori_loop(0, 2, norm, 0)

        def project(cb, c):
            cols = pl.ds(pl.multiple_of(cb * 256, 256), 256)
            p = mm(normed[rows, :], weight[:, cols])
            sig = sigmoid(p)
            a = p * sig
            acted[:, cols] = a.astype(BF16)
            dact[:, cols] = sig + a * (1.0 - sig)
            return c

        lax.fori_loop(0, 8, project, 0)

        def cols_of(block, h):
            return pl.ds(pl.multiple_of(block * D + h * 128, 128), 128)

        def attend(h, c):
            for part in range(2):
                keys = 256 * (part + 1)
                at = slice(256 * part, 256 * part + 256)
                q = acted[at, cols_of(2, h)]
                k = acted[:keys, cols_of(3, h)]
                v = acted[:keys, cols_of(1, h)]
                scores = mm_nt(q, k) * SCALE
                sig = sigmoid(scores)
                a = scores * sig
                ii = iota((256, keys), 0) + 256.0 * part
                jj = iota((256, keys), 1)
                inverse = 1.0 / jnp.full((1, keys), length)
                allowed = jnp.where((jj <= ii) & (jj < length), inverse, 0.0)
                weights = (a * allowed).astype(BF16)
                attn[h, at, :keys] = weights
                dattn[h, at, :keys] = (sig + a * (1.0 - sig)) * (allowed * SCALE)
                per_head[at, pl.ds(pl.multiple_of(h * 128, 128), 128)] = mm(weights, v)
            return c

        lax.fori_loop(0, HEADS, attend, 0)

        def gate_step(t, c):
            part = pl.ds(pl.multiple_of(t * 256, 256), 256)
            whole = pl.ds(pl.multiple_of(base + t * 256, 256), 256)
            x = per_head[part, :]
            center = x - mean(x)
            r = lax.rsqrt(mean(center * center) + EPS)
            hat = center * r
            gate = acted[part, :D].astype(F32)
            g = mixed_cot[whole, :].astype(F32)
            mixed[whole, :] = (hat * gate).astype(BF16)
            dgate = (g * hat).astype(BF16).astype(F32)
            proj_cot[whole, :D] = (dgate * dact[part, :D]).astype(BF16)
            dhat = g * gate
            dhead[part, :] = (r * (dhat - mean(dhat) - hat * mean(dhat * hat))).astype(BF16)
            return c

        lax.fori_loop(0, 2, gate_step, 0)

        def attend_back(h, c):
            def put(block, at, to, grad):
                cols = cols_of(block, h)
                proj_cot[to, cols] = (grad.astype(BF16).astype(F32) * dact[at, cols]).astype(BF16)

            dks, dvs = [], []
            for part in range(2):
                keys = 256 * (part + 1)
                at = slice(256 * part, 256 * part + 256)
                q = acted[at, cols_of(2, h)]
                k = acted[:keys, cols_of(3, h)]
                v = acted[:keys, cols_of(1, h)]
                do = dhead[at, pl.ds(pl.multiple_of(h * 128, 128), 128)]
                da = mm_nt(do, v).astype(BF16).astype(F32)
                ds = (da * dattn[h, at, :keys]).astype(BF16)
                put(2, at, pl.ds(pl.multiple_of(base + 256 * part, 256), 256), mm(ds, k))
                dks.append(mm_tn(ds, q))
                dvs.append(mm_tn(attn[h, at, :keys], do))
            for block, grads in ((3, dks), (1, dvs)):
                put(block, slice(0, 256), pl.ds(pl.multiple_of(base, 256), 256), grads[0] + grads[1][:256])
                put(block, slice(256, 512), pl.ds(pl.multiple_of(base + 256, 256), 256), grads[1][256:])
            return c

        lax.fori_loop(0, HEADS, attend_back, 0)

        def norm_back(t, c):
            part = pl.ds(pl.multiple_of(base + t * 256, 256), 256)
            ncot = mm_nt(proj_cot[part, :], weight[...])
            hat = xhat[part, :]
            gain_sum[...] += jnp.sum(ncot * hat, axis=0, keepdims=True)
            d = ncot * gain[...]
            ecot = spread[part, :] * (d - mean(d) - hat * mean(d * hat))
            live = iota((256, 1), 0) + (t * 256).astype(F32) < length
            total = masked[part, :].astype(F32) + ecot
            emb_grad[part, :] = jnp.where(live, total, 0.0).astype(BF16)
            return c

        lax.fori_loop(0, 2, norm_back, 0)
        return carry

    lax.fori_loop(0, 2, layer, 0)

    def give(i, carry):
        first = lax.rem(lax.div(w, 8) + i, 8) * 8
        rows = pl.ds(pl.multiple_of(first * CAP, 192), 192)
        cold_send[pl.ds(first, 8)] = pack(mm(place_t[rows, :], emb_grad[...]))
        for j in range(8):
            p = first + j

            @pl.when(p != w)
            def _():
                exchange(2, cold_send, cold_got, p).start()

        return carry

    lax.fori_loop(0, 8, give, 0)
    own_cold = pltpu.make_async_copy(cold_send.at[w], cold_got.at[w], loc_sem.at[2])
    own_cold.start()

    def weight_grad(cb, carry):
        grad = mm_tn(proj_cot[:, pl.ds(pl.multiple_of(cb * D, D), D)], normed[...])
        wsum[pl.ds(cb * 8, 8), :, 0:2] = grad.reshape(8, 2, 2, 16, D).astype(BF16)
        return carry

    lax.fori_loop(0, 4, weight_grad, 0)
    out_grad = mm_tn(masked[...], mixed[...]).reshape(WIDE, 8, D)
    gains = jnp.broadcast_to(gain_sum[...].reshape(1, 1, D), (WIDE, 8, D))
    wsum[:, :, 2] = jnp.concatenate([out_grad, gains], axis=1).reshape(32, 2, 16, D).astype(BF16)
    wsum[:, :, 3] = mm(hot_t[...], emb_grad[...]).reshape(32, 2, 16, D).astype(BF16)

    peer = w + 1 - 2 * core

    def core_copy(d):
        part = lax.rem(n + d, NARROW)
        return pltpu.make_async_remote_copy(
            src_ref=wsum.at[:, 1 - core, part], dst_ref=core_got.at[part], send_sem=core_ss.at[d], recv_sem=core_rs.at[d],
            device_id=(peer, n), device_id_type=MESH,
        )

    def x_copy(d):
        part = lax.rem(n + d, NARROW)
        return pltpu.make_async_remote_copy(
            src_ref=core_sum.at[part], dst_ref=x_got.at[d - 1], send_sem=x_ss.at[d - 1], recv_sem=x_rs.at[d - 1],
            device_id=(w, part), device_id_type=MESH,
        )

    order = (2, 1, 3, 0)
    for d in order:
        core_copy(d).start()
    for d in order:
        core_copy(d).wait_recv()
        part = lax.rem(n + d, NARROW)
        core_sum[part] = (wsum[:, core, part].astype(F32) + core_got[part].astype(F32)).astype(BF16)
        if d:
            x_copy(d).start()
    total = core_sum[n].astype(F32)
    for d in (1, 3, 2):
        x_copy(d).wait_recv()
        total = total + x_got[d - 1].astype(F32)
    x_sum[...] = total.astype(BF16).reshape(4, 8, 16, D)

    def y_copy(d):
        to = lax.rem(y + d, 4)
        return pltpu.make_async_remote_copy(
            src_ref=x_sum.at[to], dst_ref=y_got.at[d - 1], send_sem=y_ss.at[d - 1], recv_sem=y_rs.at[d - 1],
            device_id=((to * 8 + z) * 2 + core, n), device_id_type=MESH,
        )

    def z_copy(d):
        to = lax.rem(z + d, 8)
        return pltpu.make_async_remote_copy(
            src_ref=y_sum.at[to], dst_ref=z_got.at[d - 1], send_sem=z_ss.at[d - 1], recv_sem=z_rs.at[d - 1],
            device_id=((y * 8 + to) * 2 + core, n), device_id_type=MESH,
        )

    def g_copy(d):
        to = lax.rem(n + d, NARROW)
        return pltpu.make_async_remote_copy(
            src_ref=gathered.at[n], dst_ref=gathered.at[n], send_sem=g_ss.at[d - 1], recv_sem=g_rs.at[d - 1],
            device_id=(w, to), device_id_type=MESH,
        )

    def cx_copy(d):
        to = lax.rem(n + d, NARROW)
        return pltpu.make_async_remote_copy(
            src_ref=cx_send.at[d - 1], dst_ref=cx_got.at[d - 1], send_sem=cx_ss.at[d - 1], recv_sem=cx_rs.at[d - 1],
            device_id=(w, to), device_id_type=MESH,
        )

    for d in (2, 1, 3):
        y_copy(d).start()
    total = x_sum[y].astype(F32)
    for d in (1, 3, 2):
        y_copy(d).wait_recv()
        total = total + y_got[d - 1].astype(F32)
    y_sum[...] = total.astype(BF16)
    for d in range(1, 8):
        z_copy(d).start()
    total = y_sum[z].astype(F32)
    for d in range(1, 8):
        z_copy(d).wait_recv()
        total = total + z_got[d - 1].astype(F32)
    gathered[n] = total
    for d in range(1, NARROW):
        g_copy(d).start()

    asked = want[...].reshape(WIDE, 128)
    high = jnp.floor(asked * (1.0 / 32.0))
    low = asked - 32.0 * high
    line = iota((128, WIDE * CAP), 1)
    within = line - CAP * jnp.floor((line + 0.5) * (1.0 / CAP))
    spot = onehot(within == iota((128, WIDE * CAP), 0))
    spread_out = 32.0 * mm(high.astype(BF16), spot) + mm(low.astype(BF16), spot)
    line64 = iota((WIDE, WIDE * CAP), 1)
    start = iota((WIDE, WIDE * CAP), 0) * CAP
    mine = (line64 >= start) & (line64 < start + CAP)
    asked_line = jnp.sum(jnp.where(mine, spread_out, 0.0), axis=0, keepdims=True)

    own_cold.wait()
    await_all(a2a_recv.at[2], cold_got)
    unpack_into(rows_in, cold_got)

    def quarter(part):
        at = iota((256, WIDE * CAP), 0) + (part * 256).astype(F32)
        return mm(onehot(at == asked_line), rows_in[...])

    for d in (2, 1, 3):
        cx_send[d - 1] = quarter(lax.rem(n + d, NARROW)).astype(BF16)
        cx_copy(d).start()
    cold_out[...] = quarter(n)

    for d in range(1, NARROW):
        g_copy(d).wait_recv()
    proj_out[...] = gathered[0:2].reshape(32, D).T
    out_out[...] = gathered[2, 0:8].T
    gain_out[...] = gathered[2, 8:9]
    for k in range(NARROW):

        @pl.when(n == k)
        def _():
            hot_out[...] = gathered[3, 4 * k : 4 * k + 4]

    for d in (1, 3, 2):
        cx_copy(d).wait_recv()
        cold_out[...] += cx_got[d - 1].astype(F32)

    await_all(a2a_send.at[0], req)
    await_all(a2a_send.at[1], reply)
    await_all(a2a_send.at[2], cold_send)
    for d in range(NARROW):
        core_copy(d).wait_send()
    for d in range(1, NARROW):
        x_copy(d).wait_send()
        y_copy(d).wait_send()
        g_copy(d).wait_send()
        cx_copy(d).wait_send()
    for d in range(1, 8):
        z_copy(d).wait_send()


def local(
    item_owner, item_row, hot_row, hot_flag, seq_length, cold_table, hot_table, proj_weight, out_weight, norm_gain, cotangent
):
    hot_id = jnp.where(hot_flag == 1, hot_row, -1)
    tok = jnp.concatenate([a.reshape(8, 128) for a in (item_owner, item_row, hot_id)], axis=0).astype(F32)
    tok = jnp.concatenate([tok, jnp.zeros((8, 128), F32)], axis=0)
    vm = pl.BlockSpec(memory_space=pltpu.VMEM)
    sm = pl.BlockSpec(memory_space=pltpu.SMEM)
    v = pltpu.VMEM
    dma = pltpu.SemaphoreType.DMA
    slots = WIDE * CAP
    block = (WIDE, 48, 256)
    scratch = [
        v((8, 128), F32), v((WIDE, 1, 128), F32), v((WIDE, 1, 128), F32),
        v(block, BF16), v(block, BF16), v((slots, D), BF16), v((slots, TOK), BF16), v((TOK, TOK), BF16),
        v((TOK, D), BF16), v((TOK, D), BF16), v((TOK, D), F32), v((TOK, 1), F32),
        v((LEN, 4 * D), BF16), v((LEN, 4 * D), F32), v((HEADS, LEN, LEN), BF16), v((HEADS, LEN, LEN), F32),
        v((LEN, D), F32), v((TOK, D), BF16), v((TOK, D), BF16), v((TOK, D), BF16), v((LEN, D), BF16),
        v((TOK, 4 * D), BF16), v((TOK, D), BF16), v((1, D), F32),
        v(block, BF16), v(block, BF16),
        v((32, 2, 4, 16, D), BF16), v((4, 32, 16, D), BF16), v((4, 32, 16, D), BF16), v((3, 32, 16, D), BF16),
        v((4, 8, 16, D), BF16), v((3, 8, 16, D), BF16), v((8, 16, D), BF16), v((7, 16, D), BF16), v((4, 16, D), F32),
        v((3, 256, D), BF16), v((3, 256, D), BF16),
        dma((3,)), dma((3,)), dma((3,)), dma((4,)), dma((4,)), dma((3,)), dma((3,)), dma((3,)), dma((3,)),
        dma((7,)), dma((7,)), dma((3,)), dma((3,)), dma((3,)), dma((3,)),
    ]
    out_shape = [
        jax.ShapeDtypeStruct((D, 32), F32), jax.ShapeDtypeStruct((D, 8), F32), jax.ShapeDtypeStruct((1, D), F32),
        jax.ShapeDtypeStruct((256, D), F32), jax.ShapeDtypeStruct((4, D), F32),
    ]
    proj, out, gain, cold, hot = pl.pallas_call(
        kernel,
        out_shape=out_shape,
        in_specs=[vm, sm] + [vm] * 6,
        out_specs=[vm] * 5,
        scratch_shapes=scratch,
        compiler_params=pltpu.CompilerParams(collective_id=0, has_side_effects=True, vmem_limit_bytes=62 * 1024 * 1024),
    )(tok, seq_length, cold_table, hot_table, proj_weight, out_weight, norm_gain, cotangent.reshape(TOK, D))
    gain = lax.dynamic_slice(gain, (0, lax.axis_index("wide") * 8), (1, 8))
    return proj, out, gain, cold, hot


def solution(mesh):
    both = P(("wide", "narrow"))
    in_specs = (both, both, both, both, both, P("wide"), P(), P(), P(), P(), both)
    out_specs = (P(None, "wide"), P(None, "wide"), P(None, "wide"), both, both)
    return jax.shard_map(local, mesh=mesh, in_specs=in_specs, out_specs=out_specs, check_vma=False)
```

```python
import functools

import jax
import jax.numpy as jnp
from jax import lax
from jax.experimental import pallas as pl
from jax.experimental.pallas import tpu as pltpu
from jax.sharding import PartitionSpec as P

WIDE = 64
NARROW = 4
CAP = 24
TOK = 1024
LEN = 512
D = 512
HALF = 256
HEADS = 4
ROWS = 1024
EPS = 1e-05
SCALE = 128 ** (-0.5)
MESH = pl.DeviceIdType.MESH
F32 = jnp.float32
BF16 = jnp.bfloat16


def mm(a, b):
    return jnp.dot(a, b, preferred_element_type=F32)


def mm_nt(a, b):
    return lax.dot_general(a, b, (((1,), (1,)), ((), ())), preferred_element_type=F32)


def mm_tn(a, b):
    return lax.dot_general(a, b, (((0,), (0,)), ((), ())), preferred_element_type=F32)


def iota(shape, dim):
    return lax.broadcasted_iota(jnp.int32, shape, dim).astype(F32)


def sigmoid(x):
    return 0.5 * jnp.tanh(0.5 * x) + 0.5


def onehot(mask):
    return jnp.where(mask, 1.0, 0.0).astype(BF16)


def mean(x):
    return jnp.mean(x, axis=-1, keepdims=True)


def pack(rows):
    half = rows.shape[1] // 2
    blocks = rows.reshape(-1, CAP, rows.shape[1])
    return jnp.concatenate([blocks[:, :, :half], blocks[:, :, half:]], axis=1).astype(BF16)


def unpack_into(dst, src, start=0):
    half = src.shape[-1]

    def step(i, carry):
        block = src[pl.ds(i * 8, 8)].astype(F32)
        rows = pl.ds(pl.multiple_of(i * 192, 192), 192)
        dst[rows, start : start + half] = block[:, :CAP].reshape(192, half).astype(BF16)
        dst[rows, start + half : start + 2 * half] = block[:, CAP:].reshape(192, half).astype(BF16)
        return carry

    lax.fori_loop(0, 8, step, 0)


def kernel(
    owner, row_in, hot_row, hot_flag, lens, gain, table_in, hot_table_in, weight_in, out_weight_in, cot_in,
    gathered_out, cold_own, cx_got,
    table, hot_table, weight, out_weight, cot, tok, slots, req, want, reply, got, rows_in, place_t, hot_t, emb, normed, xhat, spread, acted, dact,
    attn, dattn, per_head, mixed, masked, mixed_cot, dhead, proj_cot, emb_grad, gain_sum,
    cold_send, cold_got, wsum, core_got, core_sum, x_got, x_sum, y_got, y_sum, z_got, gathered, cx_send,
    load_sem, loc_sem, a2a_send, a2a_recv, core_ss, core_rs, x_ss, x_rs, y_ss, y_rs, z_ss, z_rs, g_ss, g_rs, cx_ss, cx_rs,
):
    w = lax.axis_index("wide")
    n = lax.axis_index("narrow")
    core = lax.rem(w, 2)
    chip = lax.div(w, 2)
    z = lax.rem(chip, 8)
    y = lax.div(chip, 8)

    loads = [
        pltpu.make_async_copy(src, dst, load_sem.at[i])
        for i, (src, dst) in enumerate(
            [(table_in, table), (hot_table_in, hot_table), (cot_in, cot), (out_weight_in, out_weight), (weight_in, weight)]
        )
    ]
    for load in loads:
        load.start()

    barrier = pltpu.get_barrier_semaphore()

    def greet(d, carry):
        pl.semaphore_signal(barrier, inc=1, device_id=(lax.rem(w + d, WIDE), n), device_id_type=MESH)
        return carry

    lax.fori_loop(1, WIDE, greet, 0)
    for d in range(1, NARROW):
        pl.semaphore_signal(barrier, inc=1, device_id=(w, lax.rem(n + d, NARROW)), device_id_type=MESH)

    for a in range(8):
        at = (slice(a // 4, a // 4 + 1), slice(a % 4 * 128, a % 4 * 128 + 128))
        tok[a : a + 1, :] = owner[a // 4, :, at[1]].astype(F32)
        tok[8 + a : 9 + a, :] = row_in[at].astype(F32)
        tok[16 + a : 17 + a, :] = jnp.where(hot_flag[at] == 1, hot_row[at], -1).astype(F32)

    upper = onehot(iota((128, 128), 0) < iota((128, 128), 1))
    sub = iota((128, 128), 0)
    carry = jnp.zeros((128, 1), F32)
    req_hi = jnp.zeros((128, 128), F32)
    req_lo = jnp.zeros((128, 128), F32)
    for a in range(8):
        own = tok[a : a + 1, :]
        row = tok[8 + a : 9 + a, :]
        hot = tok[16 + a : 17 + a, :]
        owns = jnp.where(sub == own, 1.0, 0.0)
        owns_b = owns.astype(BF16)
        before = mm(owns_b, upper) + carry
        rank = jnp.sum(owns * before, axis=0, keepdims=True)
        carry = carry + jnp.sum(owns, axis=1, keepdims=True)
        slots[a : a + 1, :] = jnp.where(hot >= 0.0, -1.0, own * CAP + rank)
        high = jnp.floor(row * (1.0 / 32.0))
        low = row - 32.0 * high
        ranked = sub == rank
        req_hi = req_hi + mm_nt(owns_b, jnp.where(ranked, high, 0.0).astype(BF16))
        req_lo = req_lo + mm_nt(owns_b, jnp.where(ranked, low, 0.0).astype(BF16))
    asked = 32.0 * req_hi + req_lo
    for o in range(WIDE):
        req[o] = asked[o : o + 1, :]

    pl.semaphore_wait(barrier, WIDE - 1 + NARROW - 1)

    def exchange(which, src, dst, p):
        return pltpu.make_async_remote_copy(
            src_ref=src.at[p], dst_ref=dst.at[w], send_sem=a2a_send.at[which], recv_sem=a2a_recv.at[which],
            device_id=(p, n), device_id_type=MESH,
        )

    def await_all(sem, ref):
        view = ref.at[pl.ds(0, WIDE - 1)]
        pltpu.make_async_copy(view, view, sem).wait()

    def ask(d, carry):
        exchange(0, req, want, lax.rem(w + d, WIDE)).start()
        return carry

    lax.fori_loop(1, WIDE, ask, 0)
    own_want = pltpu.make_async_copy(req.at[w], want.at[w], loc_sem.at[0])
    own_want.start()

    def build_place(a, carry):
        rows = pl.ds(pl.multiple_of(a * 192, 192), 192)
        at = iota((192, 128), 0) + (a * 192).astype(F32)
        for b in range(8):
            place_t[rows, b * 128 : (b + 1) * 128] = onehot(at == slots[b : b + 1, :])
        return carry

    lax.fori_loop(0, 8, build_place, 0)

    def build_hot(a, carry):
        rows = pl.ds(pl.multiple_of(a * 128, 128), 128)
        at = iota((128, 128), 0) + (a * 128).astype(F32)
        for b in range(8):
            hot_t[rows, b * 128 : (b + 1) * 128] = onehot(at == tok[16 + b : 17 + b, :])
        return carry

    lax.fori_loop(0, 8, build_hot, 0)

    own_want.wait()
    loads[0].wait()
    await_all(a2a_recv.at[0], want)

    lanes = iota((CAP, ROWS), 1)

    def answer(i, carry):
        first = lax.rem(lax.div(w, 8) + i, 8) * 8
        asked8 = want[pl.ds(first, 8)].reshape(8, 128).T
        picks = jnp.concatenate([jnp.where(lanes == asked8[:CAP, j : j + 1], 1.0, 0.0) for j in range(8)], axis=0)
        reply[pl.ds(first, 8)] = pack(mm(picks.astype(BF16), table[...]))
        for j in range(8):
            p = first + j

            @pl.when(p != w)
            def _():
                exchange(1, reply, got, p).start()

        return carry

    lax.fori_loop(0, 8, answer, 0)
    own_reply = pltpu.make_async_copy(reply.at[w], got.at[w], loc_sem.at[1])
    own_reply.start()

    for load in loads[1:]:
        load.wait()
    tok_cols = tok[...].T
    for half in range(2):
        rows = slice(half * LEN, (half + 1) * LEN)
        hots = jnp.concatenate(
            [onehot(iota((128, TOK), 1) == tok_cols[:, 16 + a : 17 + a]) for a in range(half * 4, half * 4 + 4)], axis=0
        )
        emb[rows, :] = mm(hots, hot_table[...]).astype(BF16)
        live = iota((LEN, 1), 0) < lens[half].astype(F32)
        masked[rows, :] = jnp.where(live, cot[rows, :].astype(F32), 0.0).astype(BF16)
        mixed_cot[rows, :] = mm_nt(masked[rows, :], out_weight[...]).astype(BF16)

    own_reply.wait()
    await_all(a2a_recv.at[1], got)
    unpack_into(rows_in, got)
    slot_cols = slots[...].T
    for half in range(2):
        rows = slice(half * LEN, (half + 1) * LEN)
        picks = jnp.concatenate(
            [onehot(iota((128, WIDE * CAP), 1) == slot_cols[:, a : a + 1]) for a in range(half * 4, half * 4 + 4)], axis=0
        )
        emb[rows, :] = (mm(picks, rows_in[...]) + emb[rows, :].astype(F32)).astype(BF16)

    gain_sum[...] = jnp.zeros_like(gain_sum)

    def layer(s, carry):
        base = s * LEN
        rows = pl.ds(pl.multiple_of(base, LEN), LEN)
        length = lens[s].astype(F32)

        def norm(t, c):
            part = pl.ds(pl.multiple_of(base + t * 256, 256), 256)
            here = pl.ds(pl.multiple_of(t * 256, 256), 256)
            x = emb[part, :].astype(F32)
            center = x - mean(x)
            r = lax.rsqrt(mean(center * center) + EPS)
            hat = center * r
            xhat[here, :] = hat
            spread[here, :] = r
            normed[part, :] = (hat * gain[...]).astype(BF16)
            return c

        lax.fori_loop(0, 2, norm, 0)

        def project(cb, c):
            cols = pl.ds(pl.multiple_of(cb * 256, 256), 256)
            p = mm(normed[rows, :], weight[:, cols])
            sig = sigmoid(p)
            a = p * sig
            acted[:, cols] = a.astype(BF16)
            dact[:, cols] = sig + a * (1.0 - sig)
            return c

        lax.fori_loop(0, 8, project, 0)

        def cols_of(block, h):
            return pl.ds(pl.multiple_of(block * D + h * 128, 128), 128)

        def attend(h, c):
            for part in range(2):
                keys = 256 * (part + 1)
                at = slice(256 * part, 256 * part + 256)
                q = acted[at, cols_of(2, h)]
                k = acted[:keys, cols_of(3, h)]
                v = acted[:keys, cols_of(1, h)]
                scores = mm_nt(q, k) * SCALE
                sig = sigmoid(scores)
                a = scores * sig
                ii = iota((256, keys), 0) + 256.0 * part
                jj = iota((256, keys), 1)
                inverse = 1.0 / jnp.full((1, keys), length)
                allowed = jnp.where((jj <= ii) & (jj < length), inverse, 0.0)
                weights = (a * allowed).astype(BF16)
                attn[h, at, :keys] = weights
                dattn[h, at, :keys] = (sig + a * (1.0 - sig)) * (allowed * SCALE)
                per_head[at, pl.ds(pl.multiple_of(h * 128, 128), 128)] = mm(weights, v)
            return c

        lax.fori_loop(0, HEADS, attend, 0)

        def gate_step(t, c):
            part = pl.ds(pl.multiple_of(t * 256, 256), 256)
            whole = pl.ds(pl.multiple_of(base + t * 256, 256), 256)
            x = per_head[part, :]
            center = x - mean(x)
            r = lax.rsqrt(mean(center * center) + EPS)
            hat = center * r
            gate = acted[part, :D].astype(F32)
            g = mixed_cot[whole, :].astype(F32)
            mixed[whole, :] = (hat * gate).astype(BF16)
            dgate = (g * hat).astype(BF16).astype(F32)
            proj_cot[whole, :D] = (dgate * dact[part, :D]).astype(BF16)
            dhat = g * gate
            dhead[part, :] = (r * (dhat - mean(dhat) - hat * mean(dhat * hat))).astype(BF16)
            return c

        lax.fori_loop(0, 2, gate_step, 0)

        def attend_back(h, c):
            def put(block, at, to, grad):
                cols = cols_of(block, h)
                proj_cot[to, cols] = (grad.astype(BF16).astype(F32) * dact[at, cols]).astype(BF16)

            dks, dvs = [], []
            for part in range(2):
                keys = 256 * (part + 1)
                at = slice(256 * part, 256 * part + 256)
                q = acted[at, cols_of(2, h)]
                k = acted[:keys, cols_of(3, h)]
                v = acted[:keys, cols_of(1, h)]
                do = dhead[at, pl.ds(pl.multiple_of(h * 128, 128), 128)]
                da = mm_nt(do, v).astype(BF16).astype(F32)
                ds = (da * dattn[h, at, :keys]).astype(BF16)
                put(2, at, pl.ds(pl.multiple_of(base + 256 * part, 256), 256), mm(ds, k))
                dks.append(mm_tn(ds, q))
                dvs.append(mm_tn(attn[h, at, :keys], do))
            for block, grads in ((3, dks), (1, dvs)):
                put(block, slice(0, 256), pl.ds(pl.multiple_of(base, 256), 256), grads[0] + grads[1][:256])
                put(block, slice(256, 512), pl.ds(pl.multiple_of(base + 256, 256), 256), grads[1][256:])
            return c

        lax.fori_loop(0, HEADS, attend_back, 0)

        def norm_back(t, c):
            part = pl.ds(pl.multiple_of(base + t * 256, 256), 256)
            here = pl.ds(pl.multiple_of(t * 256, 256), 256)
            ncot = mm_nt(proj_cot[part, :], weight[...])
            hat = xhat[here, :]
            gain_sum[...] += jnp.sum(ncot * hat, axis=0, keepdims=True)
            d = ncot * gain[...]
            ecot = spread[here, :] * (d - mean(d) - hat * mean(d * hat))
            live = iota((256, 1), 0) + (t * 256).astype(F32) < length
            total = masked[part, :].astype(F32) + ecot
            emb_grad[part, :] = jnp.where(live, total, 0.0).astype(BF16)
            return c

        lax.fori_loop(0, 2, norm_back, 0)
        return carry

    lax.fori_loop(0, 2, layer, 0)

    def give(half):
        def step(i, carry):
            first = lax.rem(lax.div(w, 8) + i, 8) * 8
            rows = pl.ds(pl.multiple_of(first * CAP, 192), 192)
            cold_send[half, pl.ds(first, 8)] = pack(mm(place_t[rows, :], emb_grad[:, half * HALF : (half + 1) * HALF]))
            for j in range(8):
                p = first + j

                @pl.when(p != w)
                def _():
                    exchange(2 + half, cold_send.at[half], cold_got.at[half], p).start()

            return carry

        lax.fori_loop(0, 8, step, 0)
        own = pltpu.make_async_copy(cold_send.at[half, w], cold_got.at[half, w], loc_sem.at[2 + half])
        own.start()
        return own

    def sums(half):
        cols = slice(half * HALF, (half + 1) * HALF)

        def weight_grad(cb, carry):
            grad = mm_tn(proj_cot[:, pl.ds(pl.multiple_of(cb * D, D), D)], normed[:, cols]).reshape(8, 2, 2, 16, HALF).astype(BF16)
            for c in range(2):
                for part in range(2):
                    wsum[half, c, part, pl.ds(cb * 8, 8)] = grad[:, c, part]
            return carry

        lax.fori_loop(0, 4, weight_grad, 0)
        out_grad = mm_tn(masked[...], mixed[:, cols]).reshape(WIDE, 8, HALF)
        gains = jnp.broadcast_to(gain_sum[:, cols].reshape(1, 1, HALF), (WIDE, 8, HALF))
        both = jnp.concatenate([out_grad, gains], axis=1).reshape(32, 2, 16, HALF).astype(BF16)
        hots = mm(hot_t[...], emb_grad[:, cols]).reshape(32, 2, 16, HALF).astype(BF16)
        for c in range(2):
            wsum[half, c, 2] = both[:, c]
            wsum[half, c, 3] = hots[:, c]

    peer = w + 1 - 2 * core
    order = (2, 1, 3, 0)

    def remote(src, dst, sems, index, to):
        return pltpu.make_async_remote_copy(
            src_ref=src, dst_ref=dst, send_sem=sems[0].at[index], recv_sem=sems[1].at[index],
            device_id=to, device_id_type=MESH,
        )

    def core_copy(half, d):
        part = lax.rem(n + d, NARROW)
        return remote(wsum.at[half, 1 - core, part], core_got.at[half, part], (core_ss, core_rs), half * 4 + d, (peer, n))

    def x_copy(half, d):
        part = lax.rem(n + d, NARROW)
        return remote(core_sum.at[half, part], x_got.at[half, d - 1], (x_ss, x_rs), half * 3 + d - 1, (w, part))

    def y_copy(half, d):
        to = lax.rem(y + d, 4)
        return remote(
            x_sum.at[half, to], y_got.at[half, d - 1], (y_ss, y_rs), half * 3 + d - 1, ((to * 8 + z) * 2 + core, n)
        )

    def z_copy(half, d):
        to = lax.rem(z + d, 8)
        return remote(
            y_sum.at[half, to], z_got.at[half, d - 1], (z_ss, z_rs), half * 7 + d - 1, ((y * 8 + to) * 2 + core, n)
        )

    def g_copy(half, d):
        to = lax.rem(n + d, NARROW)
        return remote(gathered.at[half, n], gathered.at[half, n], (g_ss, g_rs), half * 3 + d - 1, (w, to))

    def cx_copy(half, d):
        to = lax.rem(n + d, NARROW)
        return remote(cx_send.at[half, d - 1], cx_got.at[half, d - 1], (cx_ss, cx_rs), half * 3 + d - 1, (w, to))

    def core_start(half):
        for d in order:
            core_copy(half, d).start()

    def core_step(half):
        for d in order:
            core_copy(half, d).wait_recv()
            part = lax.rem(n + d, NARROW)
            core_sum[half, part] = (wsum[half, core, part].astype(F32) + core_got[half, part].astype(F32)).astype(BF16)
            if d:
                x_copy(half, d).start()

    def x_step(half):
        total = core_sum[half, n].astype(F32)
        for d in (1, 3, 2):
            x_copy(half, d).wait_recv()
            total = total + x_got[half, d - 1].astype(F32)
        x_sum[half] = total.astype(BF16).reshape(4, 8, 16, HALF)
        for d in (2, 1, 3):
            y_copy(half, d).start()

    def y_step(half):
        total = x_sum[half, y].astype(F32)
        for d in (1, 3, 2):
            y_copy(half, d).wait_recv()
            total = total + y_got[half, d - 1].astype(F32)
        y_sum[half] = total.astype(BF16)
        for d in range(1, 8):
            z_copy(half, d).start()

    def z_step(half):
        total = y_sum[half, z].astype(F32)
        for d in range(1, 8):
            z_copy(half, d).wait_recv()
            total = total + z_got[half, d - 1].astype(F32)
        gathered[half, n] = total
        for d in range(1, NARROW):
            g_copy(half, d).start()

    def cold_step(half, own, line):
        cols = slice(half * HALF, (half + 1) * HALF)
        own.wait()
        await_all(a2a_recv.at[2 + half], cold_got.at[half])
        unpack_into(rows_in, cold_got.at[half], half * HALF)

        def quarter(part):
            at = iota((256, WIDE * CAP), 0) + (part * 256).astype(F32)
            return mm(onehot(at == line), rows_in[:, cols])

        for d in (2, 1, 3):
            cx_send[half, d - 1] = quarter(lax.rem(n + d, NARROW)).astype(BF16)
            cx_copy(half, d).start()
        cold_own[:, cols] = quarter(n)

    own0 = give(0)
    sums(0)
    core_start(0)
    own1 = give(1)
    core_step(0)
    sums(1)
    core_start(1)
    core_step(1)

    asked = want[...].reshape(WIDE, 128)
    high = jnp.floor(asked * (1.0 / 32.0))
    low = asked - 32.0 * high
    line = iota((128, WIDE * CAP), 1)
    within = line - CAP * jnp.floor((line + 0.5) * (1.0 / CAP))
    spot = onehot(within == iota((128, WIDE * CAP), 0))
    spread_out = 32.0 * mm(high.astype(BF16), spot) + mm(low.astype(BF16), spot)
    line64 = iota((WIDE, WIDE * CAP), 1)
    start = iota((WIDE, WIDE * CAP), 0) * CAP
    mine = (line64 >= start) & (line64 < start + CAP)
    asked_line = jnp.sum(jnp.where(mine, spread_out, 0.0), axis=0, keepdims=True)

    x_step(0)
    cold_step(0, own0, asked_line)
    y_step(0)
    x_step(1)
    cold_step(1, own1, asked_line)
    z_step(0)
    y_step(1)
    z_step(1)
    for half in range(2):
        for d in range(1, NARROW):
            g_copy(half, d).wait_recv()
    gathered_out[...] = gathered[...]
    for half in range(2):
        for d in range(1, NARROW):
            cx_copy(half, d).wait_recv()

    await_all(a2a_send.at[0], req)
    await_all(a2a_send.at[1], reply)
    for half in range(2):
        await_all(a2a_send.at[2 + half], cold_send.at[half])
        for d in range(NARROW):
            core_copy(half, d).wait_send()
        for d in range(1, NARROW):
            x_copy(half, d).wait_send()
            y_copy(half, d).wait_send()
            g_copy(half, d).wait_send()
            cx_copy(half, d).wait_send()
        for d in range(1, 8):
            z_copy(half, d).wait_send()


def finish(gathered, cold_own, cx_got, proj_out, out_out, gain_out, cold_out, hot_out, turned):
    w = lax.axis_index("wide")
    n = lax.axis_index("narrow")
    for half in range(2):
        cols = slice(half * HALF, (half + 1) * HALF)
        proj_out[:, cols] = gathered[half, 0:2].reshape(32, HALF)
        out_out[:, cols] = gathered[half, 2, 0:8]
        turned[cols, :] = gathered[half, 2, 8:16].T
        for k in range(NARROW):

            @pl.when(n == k)
            def _():
                hot_out[:, cols] = gathered[half, 3, 4 * k : 4 * k + 4]

        total = cold_own[:, cols]
        for d in range(NARROW - 1):
            total = total + cx_got[half, d].astype(F32)
        cold_out[:, cols] = total
    gain_out[...] = turned[pl.ds(pl.multiple_of(w * 8, 8), 8), :].T[0:1, :]


def local(
    item_owner, item_row, hot_row, hot_flag, seq_length, cold_table, hot_table, proj_weight, out_weight, norm_gain, cotangent
):
    vm = pl.BlockSpec(memory_space=pltpu.VMEM)
    sm = pl.BlockSpec(memory_space=pltpu.SMEM)
    v = pltpu.VMEM
    dma = pltpu.SemaphoreType.DMA
    slots = WIDE * CAP
    block = (WIDE, 48, 256)
    scratch = [
        v((ROWS, D), BF16), v((TOK, D), BF16), v((D, 4 * D), BF16), v((D, D), BF16), v((TOK, D), BF16),
        v((32, 128), F32), v((8, 128), F32), v((WIDE, 1, 128), F32), v((WIDE, 1, 128), F32),
        v(block, BF16), v(block, BF16), v((slots, D), BF16), v((slots, TOK), BF16), v((TOK, TOK), BF16),
        v((TOK, D), BF16), v((TOK, D), BF16), v((LEN, D), F32), v((LEN, 1), F32),
        v((LEN, 4 * D), BF16), v((LEN, 4 * D), F32), v((HEADS, LEN, LEN), BF16), v((HEADS, LEN, LEN), F32),
        v((LEN, D), F32), v((TOK, D), BF16), v((TOK, D), BF16), v((TOK, D), BF16), v((LEN, D), BF16),
        v((TOK, 4 * D), BF16), v((TOK, D), BF16), v((1, D), F32),
        v((2, WIDE, 48, 128), BF16), v((2, WIDE, 48, 128), BF16),
        v((2, 2, 4, 32, 16, HALF), BF16), v((2, 4, 32, 16, HALF), BF16), v((2, 4, 32, 16, HALF), BF16),
        v((2, 3, 32, 16, HALF), BF16), v((2, 4, 8, 16, HALF), BF16), v((2, 3, 8, 16, HALF), BF16),
        v((2, 8, 16, HALF), BF16), v((2, 7, 16, HALF), BF16), v((2, 4, 16, HALF), F32), v((2, 3, 256, HALF), BF16),
        dma((5,)), dma((4,)), dma((4,)), dma((4,)), dma((8,)), dma((8,)), dma((6,)), dma((6,)), dma((6,)), dma((6,)),
        dma((14,)), dma((14,)), dma((6,)), dma((6,)), dma((6,)), dma((6,)),
    ]
    shape = jax.ShapeDtypeStruct
    parts = pl.pallas_call(
        kernel,
        out_shape=[shape((2, 4, 16, HALF), F32), shape((256, D), F32), shape((2, 3, 256, HALF), BF16)],
        in_specs=[vm] * 4 + [sm, vm] + [pl.BlockSpec(memory_space=pl.ANY)] * 5,
        out_specs=[vm] * 3,
        scratch_shapes=scratch,
        compiler_params=pltpu.CompilerParams(collective_id=0, has_side_effects=True, vmem_limit_bytes=62 * 1024 * 1024),
    )(
        item_owner.transpose(0, 2, 1), item_row, hot_row, hot_flag, seq_length, norm_gain,
        cold_table, hot_table, proj_weight, out_weight, cotangent.reshape(TOK, D),
    )
    proj, out, gain, cold, hot = pl.pallas_call(
        finish,
        out_shape=[shape((32, D), F32), shape((8, D), F32), shape((1, 8), F32), shape((256, D), F32), shape((4, D), F32)],
        in_specs=[vm] * 3,
        out_specs=[vm] * 5,
        scratch_shapes=[v((D, 8), F32)],
    )(*parts)
    return proj.T, out.T, gain, cold, hot


def solution(mesh):
    both = P(("wide", "narrow"))
    in_specs = (both, both, both, both, both, P("wide"), P(), P(), P(), P(), both)
    out_specs = (P(None, "wide"), P(None, "wide"), P(None, "wide"), both, both)
    return jax.shard_map(local, mesh=mesh, in_specs=in_specs, out_specs=out_specs, check_vma=False)
```

```python
import functools

import jax
import jax.numpy as jnp
from jax import lax
from jax.experimental import pallas as pl
from jax.experimental.pallas import tpu as pltpu
from jax.sharding import PartitionSpec as P

WIDE = 64
NARROW = 4
CAP = 24
TOK = 1024
LEN = 512
D = 512
HALF = 256
HEADS = 4
ROWS = 1024
EPS = 1e-05
SCALE = 128 ** (-0.5)
MESH = pl.DeviceIdType.MESH
F32 = jnp.float32
BF16 = jnp.bfloat16


def mm(a, b):
    return jnp.dot(a, b, preferred_element_type=F32)


def mm_nt(a, b):
    return lax.dot_general(a, b, (((1,), (1,)), ((), ())), preferred_element_type=F32)


def mm_tn(a, b):
    return lax.dot_general(a, b, (((0,), (0,)), ((), ())), preferred_element_type=F32)


def iota(shape, dim):
    return lax.broadcasted_iota(jnp.int32, shape, dim).astype(F32)


def sigmoid(x):
    return 0.5 * jnp.tanh(0.5 * x) + 0.5


def onehot(mask):
    return jnp.where(mask, 1.0, 0.0).astype(BF16)


def mean(x):
    return jnp.mean(x, axis=-1, keepdims=True)


def pack(rows):
    half = rows.shape[1] // 2
    blocks = rows.reshape(-1, CAP, rows.shape[1])
    return jnp.concatenate([blocks[:, :, :half], blocks[:, :, half:]], axis=1).astype(BF16)


def kernel(
    owner, row_in, hot_row, hot_flag, lens, gain, table_in, hot_table_in, weight_in, out_weight_in, cot_in,
    proj_out, out_out, gain_out, cold_out, hot_out,
    table, hot_table, weight, out_weight, cot, tok, slots, req, want, reply, got, rows_in, place_t, hot_t, emb, normed, xhat, spread, acted, dact,
    attn, dattn, per_head, mixed, masked, mixed_cot, dhead, proj_cot, emb_grad, gain_sum,
    cold_send, cold_got, wsum, core_got, core_sum, x_got, x_on, x_on_got, x_sum, y_got, y_sum, z_got, gathered, cx_send, cx_got, quarter_t, turned,
    load_sem, loc_sem, a2a_send, req_recv, rep_recv, cold_recv, core_ss, core_rs, x_ss, x_rs, y_ss, y_rs, z_ss, z_rs, g_ss, g_rs, cx_ss, cx_rs,
):
    w = lax.axis_index("wide")
    n = lax.axis_index("narrow")
    core = lax.rem(w, 2)
    chip = lax.div(w, 2)
    z = lax.rem(chip, 8)
    y = lax.div(chip, 8)

    loads = [
        pltpu.make_async_copy(src, dst, load_sem.at[i])
        for i, (src, dst) in enumerate(
            [(table_in, table), (hot_table_in, hot_table), (cot_in, cot), (out_weight_in, out_weight), (weight_in, weight)]
        )
    ]
    for load in loads:
        load.start()

    barrier = pltpu.get_barrier_semaphore()

    def greet(d, carry):
        pl.semaphore_signal(barrier, inc=1, device_id=(lax.rem(w + d, WIDE), n), device_id_type=MESH)
        return carry

    lax.fori_loop(1, WIDE, greet, 0)
    for d in range(1, NARROW):
        pl.semaphore_signal(barrier, inc=1, device_id=(w, lax.rem(n + d, NARROW)), device_id_type=MESH)

    for a in range(8):
        at = (slice(a // 4, a // 4 + 1), slice(a % 4 * 128, a % 4 * 128 + 128))
        tok[a : a + 1, :] = owner[a // 4, :, at[1]].astype(F32)
        tok[8 + a : 9 + a, :] = row_in[at].astype(F32)
        tok[16 + a : 17 + a, :] = jnp.where(hot_flag[at] == 1, hot_row[at], -1).astype(F32)

    upper = onehot(iota((128, 128), 0) < iota((128, 128), 1))
    sub = iota((128, 128), 0)
    carry = jnp.zeros((128, 1), F32)
    req_hi = jnp.zeros((128, 128), F32)
    req_lo = jnp.zeros((128, 128), F32)
    for a in range(8):
        own = tok[a : a + 1, :]
        row = tok[8 + a : 9 + a, :]
        hot = tok[16 + a : 17 + a, :]
        owns = jnp.where(sub == own, 1.0, 0.0)
        owns_b = owns.astype(BF16)
        before = mm(owns_b, upper) + carry
        rank = jnp.sum(owns * before, axis=0, keepdims=True)
        carry = carry + jnp.sum(owns, axis=1, keepdims=True)
        slots[a : a + 1, :] = jnp.where(hot >= 0.0, -1.0, own * CAP + rank)
        high = jnp.floor(row * (1.0 / 32.0))
        low = row - 32.0 * high
        ranked = sub == rank
        req_hi = req_hi + mm_nt(owns_b, jnp.where(ranked, high, 0.0).astype(BF16))
        req_lo = req_lo + mm_nt(owns_b, jnp.where(ranked, low, 0.0).astype(BF16))
    asked = 32.0 * req_hi + req_lo
    for o in range(WIDE):
        req[o] = asked[o : o + 1, :]

    pl.semaphore_wait(barrier, WIDE - 1 + NARROW - 1)

    group = lax.div(w, 8)

    def exchange(src, dst, sends, recv, p):
        return pltpu.make_async_remote_copy(
            src_ref=src, dst_ref=dst, send_sem=a2a_send.at[sends], recv_sem=recv, device_id=(p, n), device_id_type=MESH
        )

    def await_bytes(sem, view):
        pltpu.make_async_copy(view, view, sem).wait()

    others = pl.ds(0, WIDE - 1)

    def ask(d, carry):
        p = lax.rem(w + d, WIDE)
        exchange(req.at[p], want.at[w], 0, req_recv.at[group], p).start()
        return carry

    lax.fori_loop(1, WIDE, ask, 0)
    pltpu.make_async_copy(req.at[w], want.at[w], req_recv.at[group]).start()
    loads[0].wait()

    lanes = iota((CAP, ROWS), 1)

    def answer(i, carry):
        which = lax.rem(group + i, 8)
        first = which * 8
        eight = pl.ds(first, 8)
        await_bytes(req_recv.at[which], want.at[eight])
        asked8 = want[eight].reshape(8, 128).T
        picks = jnp.concatenate([jnp.where(lanes == asked8[:CAP, j : j + 1], 1.0, 0.0) for j in range(8)], axis=0)
        reply[eight] = pack(mm(picks.astype(BF16), table[...]))
        for j in range(8):
            p = first + j

            @pl.when(p != w)
            def _():
                exchange(reply.at[p], got.at[w], 1, rep_recv.at[group], p).start()

        return carry

    lax.fori_loop(0, 8, answer, 0)
    pltpu.make_async_copy(reply.at[w], got.at[w], rep_recv.at[group]).start()

    def build_place(a, carry):
        rows = pl.ds(pl.multiple_of(a * 192, 192), 192)
        at = iota((192, 128), 0) + (a * 192).astype(F32)
        for b in range(8):
            place_t[rows, b * 128 : (b + 1) * 128] = onehot(at == slots[b : b + 1, :])
        return carry

    lax.fori_loop(0, 8, build_place, 0)

    def build_hot(a, carry):
        rows = pl.ds(pl.multiple_of(a * 128, 128), 128)
        at = iota((128, 128), 0) + (a * 128).astype(F32)
        for b in range(8):
            hot_t[rows, b * 128 : (b + 1) * 128] = onehot(at == tok[16 + b : 17 + b, :])
        return carry

    lax.fori_loop(0, 8, build_hot, 0)
    for load in loads[1:]:
        load.wait()
    tok_cols = tok[...].T
    for half in range(2):
        rows = slice(half * LEN, (half + 1) * LEN)
        hots = jnp.concatenate(
            [onehot(iota((128, TOK), 1) == tok_cols[:, 16 + a : 17 + a]) for a in range(half * 4, half * 4 + 4)], axis=0
        )
        emb[rows, :] = mm(hots, hot_table[...]).astype(BF16)
        live = iota((LEN, 1), 0) < lens[half].astype(F32)
        masked[rows, :] = jnp.where(live, cot[rows, :].astype(F32), 0.0).astype(BF16)
        mixed_cot[rows, :] = mm_nt(masked[rows, :], out_weight[...]).astype(BF16)

    slot_cols = slots[...].T

    def place(i, carry):
        which = lax.rem(group - i + 8, 8)
        eight = pl.ds(which * 8, 8)
        await_bytes(rep_recv.at[which], got.at[eight])
        block = got[eight].astype(F32)
        rows_8 = jnp.concatenate([block[:, :CAP].reshape(192, HALF), block[:, CAP:].reshape(192, HALF)], axis=1)
        at = iota((128, 192), 1) + (which * 192).astype(F32)
        picks = jnp.concatenate([onehot(at == slot_cols[:, a : a + 1]) for a in range(8)], axis=0)
        emb[...] = (emb[...].astype(F32) + mm(picks, rows_8.astype(BF16))).astype(BF16)
        return carry

    lax.fori_loop(0, 8, place, 0)

    gain_sum[...] = jnp.zeros_like(gain_sum)

    def layer(s, carry):
        base = s * LEN
        rows = pl.ds(pl.multiple_of(base, LEN), LEN)
        length = lens[s].astype(F32)

        def norm(t, c):
            part = pl.ds(pl.multiple_of(base + t * 256, 256), 256)
            here = pl.ds(pl.multiple_of(t * 256, 256), 256)
            x = emb[part, :].astype(F32)
            center = x - mean(x)
            r = lax.rsqrt(mean(center * center) + EPS)
            hat = center * r
            xhat[here, :] = hat
            spread[here, :] = r
            normed[part, :] = (hat * gain[...]).astype(BF16)
            return c

        lax.fori_loop(0, 2, norm, 0)

        def project(cb, c):
            def raw(i):
                return mm(normed[rows, :], weight[:, i * 256 : i * 256 + 256])

            ahead = raw(0)
            for i in range(8):
                x = 0.5 * ahead
                if i < 7:
                    ahead = raw(i + 1)
                cols = slice(i * 256, i * 256 + 256)
                t = jnp.tanh(x)
                xt = x * t
                acted[:, cols] = (xt + x).astype(BF16)
                dact[:, cols] = ((0.5 * t + 0.5) * (1.0 + x - xt)).astype(BF16)
            return c

        lax.fori_loop(0, 1, project, 0)

        def cols_of(block, h):
            return pl.ds(pl.multiple_of(block * D + h * 128, 128), 128)

        inverse = jnp.where(iota((1, LEN), 1) < length, 1.0 / jnp.full((1, LEN), length), 0.0)

        def attend(pair, c):
            for h in [pair * 4 + i for i in range(4)]:
                for part in range(2):
                    keys = 256 * (part + 1)
                    at = slice(256 * part, 256 * part + 256)
                    k = acted[:keys, cols_of(3, h)]
                    x = mm_nt(acted[at, cols_of(2, h)], k) * (0.5 * SCALE)
                    t = jnp.tanh(x)
                    xt = x * t
                    a = xt + x
                    slope = (t + 1.0) * (1.0 + x - xt)
                    weights = []
                    for block in range(part + 1):
                        these = slice(256 * block, 256 * block + 256)
                        scale = inverse[:, these]
                        if block == part:
                            scale = jnp.where(iota((256, 256), 1) <= iota((256, 256), 0), scale, 0.0)
                        weights.append((a[:, these] * scale).astype(BF16))
                        attn[h, at, these] = weights[-1]
                        dattn[h, at, these] = (slope[:, these] * scale).astype(BF16)
                    w_all = weights[0] if part == 0 else jnp.concatenate(weights, axis=1)
                    per_head[at, pl.ds(pl.multiple_of(h * 128, 128), 128)] = mm(w_all, acted[:keys, cols_of(1, h)])
            return c

        lax.fori_loop(0, 1, attend, 0)

        def gate_step(t, c):
            part = pl.ds(pl.multiple_of(t * 256, 256), 256)
            whole = pl.ds(pl.multiple_of(base + t * 256, 256), 256)
            x = per_head[part, :]
            center = x - mean(x)
            r = lax.rsqrt(mean(center * center) + EPS)
            hat = center * r
            gate = acted[part, :D].astype(F32)
            g = mixed_cot[whole, :].astype(F32)
            mixed[whole, :] = (hat * gate).astype(BF16)
            dgate = (g * hat).astype(BF16)
            proj_cot[whole, :D] = dgate * dact[part, :D]
            dhat = g * gate
            dhead[part, :] = (r * (dhat - mean(dhat) - hat * mean(dhat * hat))).astype(BF16)
            return c

        lax.fori_loop(0, 2, gate_step, 0)

        def attend_back(pair, c):
            for h in [pair * 4 + i for i in range(4)]:
                head_back(h)
            return c

        def head_back(h):
            def put(block, at, to, grad):
                cols = cols_of(block, h)
                proj_cot[to, cols] = grad.astype(BF16) * dact[at, cols]

            dks, dvs = [], []
            for part in range(2):
                keys = 256 * (part + 1)
                at = slice(256 * part, 256 * part + 256)
                q = acted[at, cols_of(2, h)]
                k = acted[:keys, cols_of(3, h)]
                v = acted[:keys, cols_of(1, h)]
                do = dhead[at, pl.ds(pl.multiple_of(h * 128, 128), 128)]
                ds = mm_nt(do, v).astype(BF16) * dattn[h, at, :keys]
                put(2, at, pl.ds(pl.multiple_of(base + 256 * part, 256), 256), mm(ds, k) * (0.5 * SCALE))
                dks.append(mm_tn(ds, q) * (0.5 * SCALE))
                dvs.append(mm_tn(attn[h, at, :keys], do))
            for block, grads in ((3, dks), (1, dvs)):
                put(block, slice(0, 256), pl.ds(pl.multiple_of(base, 256), 256), grads[0] + grads[1][:256])
                put(block, slice(256, 512), pl.ds(pl.multiple_of(base + 256, 256), 256), grads[1][256:])

        lax.fori_loop(0, 1, attend_back, 0)

        ncot = mm_nt(proj_cot[rows, :], weight[...])
        hat = xhat[...]
        gain_sum[...] += jnp.sum(ncot * hat, axis=0, keepdims=True)
        d = ncot * gain[...]
        ecot = spread[...] * (d - mean(d) - hat * mean(d * hat))
        total = masked[rows, :].astype(F32) + ecot
        emb_grad[rows, :] = jnp.where(iota((LEN, 1), 0) < length, total, 0.0).astype(BF16)
        return carry

    lax.fori_loop(0, 2, layer, 0)

    def give(half):
        def step(i, carry):
            first = lax.rem(group + i, 8) * 8
            rows = pl.ds(pl.multiple_of(first * CAP, 192), 192)
            cold_send[half, pl.ds(first, 8)] = pack(mm(place_t[rows, :], emb_grad[:, half * HALF : (half + 1) * HALF]))
            for j in range(8):
                p = first + j

                @pl.when(p != w)
                def _():
                    give_copy(half, p).start()

            return carry

        lax.fori_loop(0, 8, step, 0)
        own = pltpu.make_async_copy(cold_send.at[half, w], cold_got.at[half, w], loc_sem.at[half])
        own.start()
        return own

    def message(ref, which, block):
        if which == 0:
            return ref.at[0, block]
        return ref.at[1, block, pl.ds(0, 32)] if which == 1 else ref.at[1, block, pl.ds(32, 16)]

    def give_copy(which, p):
        return exchange(message(cold_send, which, p), message(cold_got, which, w), 2 + which, cold_recv.at[which], p)

    def give_rest(d, carry):
        give_copy(2, lax.rem(w + d, WIDE)).start()
        return carry

    def sums(half):
        cols = slice(half * HALF, (half + 1) * HALF)

        def weight_grad(cb, carry):
            grad = mm_tn(proj_cot[:, pl.ds(pl.multiple_of(cb * D, D), D)], normed[:, cols]).reshape(8, 2, 2, 16, HALF).astype(BF16)
            for c in range(2):
                for part in range(2):
                    wsum[half, c, part, pl.ds(cb * 8, 8)] = grad[:, c, part]
            return carry

        lax.fori_loop(0, 4, weight_grad, 0)
        out_grad = mm_tn(masked[...], mixed[:, cols]).reshape(WIDE, 8, HALF)
        gains = jnp.broadcast_to(gain_sum[:, cols].reshape(1, 1, HALF), (WIDE, 8, HALF))
        both = jnp.concatenate([out_grad, gains], axis=1).reshape(32, 2, 16, HALF).astype(BF16)
        hots = mm(hot_t[...], emb_grad[:, cols]).reshape(32, 2, 16, HALF).astype(BF16)
        for c in range(2):
            wsum[half, c, 2] = both[:, c]
            wsum[half, c, 3] = hots[:, c]

    peer = w + 1 - 2 * core
    sides = (n + 1 - 2 * lax.rem(n, 2), NARROW - 1 - n)
    parts = (lax.rem(n + 2, NARROW), sides[0], sides[1], n)

    def remote(src, dst, sems, index, to):
        return pltpu.make_async_remote_copy(
            src_ref=src, dst_ref=dst, send_sem=sems[0].at[index], recv_sem=sems[1].at[index],
            device_id=to, device_id_type=MESH,
        )

    def core_copy(half, j):
        src = wsum.at[half, 1 - core, parts[j]]
        return remote(src, core_got.at[half, parts[j]], (core_ss, core_rs), half * 4 + j, (peer, n))

    def chips(side):
        return pl.ds(16 * side, 16)

    def x_copy(half, side, on):
        src = core_sum.at[half, parts[0] if on else sides[side], chips(side)]
        return remote(src, x_got.at[half, side, on], (x_ss, x_rs), half * 6 + side * 3 + on, (w, sides[side]))

    def x_on_copy(half, side):
        dst = x_on_got.at[half, side]
        return remote(x_on.at[half, side], dst, (x_ss, x_rs), half * 6 + side * 3 + 2, (w, sides[1 - side]))

    def y_copy(half, d):
        to = lax.rem(y + d, 4)
        return remote(
            x_sum.at[half, to], y_got.at[half, d - 1], (y_ss, y_rs), half * 3 + d - 1, ((to * 8 + z) * 2 + core, n)
        )

    def z_copy(half, d):
        to = lax.rem(z + d, 8)
        return remote(
            y_sum.at[half, to], z_got.at[half, d - 1], (z_ss, z_rs), half * 7 + d - 1, ((y * 8 + to) * 2 + core, n)
        )

    def g_copy(half, d):
        to = lax.rem(n + d, NARROW)
        return remote(gathered.at[half, n], gathered.at[half, n], (g_ss, g_rs), half * 3 + d - 1, (w, to))

    def cx_copy(piece, d):
        to = lax.rem(n + d, NARROW)
        units = pl.ds(0, 2) if piece == 0 else pl.ds(piece + 1, 1)
        return remote(cx_send.at[units, d - 1], cx_got.at[units, d - 1], (cx_ss, cx_rs), piece * 3 + d - 1, (w, to))

    def core_start(half):
        for j in range(4):
            core_copy(half, j).start()

    def core_step(half):
        for j in range(4):
            core_copy(half, j).wait_recv()
            part = parts[j]
            core_sum[half, part] = (wsum[half, core, part].astype(F32) + core_got[half, part].astype(F32)).astype(BF16)
            if j == 0:
                x_copy(half, 0, 1).start()
                x_copy(half, 1, 1).start()
            elif j < 3:
                x_copy(half, j - 1, 0).start()

    def x_pass(half):
        for side in range(2):
            x_copy(half, side, 1).wait_recv()
            mine = core_sum[half, sides[1 - side], chips(side)].astype(F32)
            x_on[half, side] = (mine + x_got[half, side, 1].astype(F32)).astype(BF16)
            x_on_copy(half, side).start()

    def x_step(half):
        for side in range(2):
            x_copy(half, side, 0).wait_recv()
            x_on_copy(half, side).wait_recv()
            total = core_sum[half, n, chips(side)].astype(F32) + x_got[half, side, 0].astype(F32)
            total = total + x_on_got[half, side].astype(F32)
            x_sum[half, 2 * side : 2 * side + 2] = total.astype(BF16).reshape(2, 8, 16, HALF)
        for d in (2, 1, 3):
            y_copy(half, d).start()

    def y_step(half):
        total = x_sum[half, y].astype(F32)
        for d in (1, 3, 2):
            y_copy(half, d).wait_recv()
            total = total + y_got[half, d - 1].astype(F32)
        y_sum[half] = total.astype(BF16)
        for d in range(1, 8):
            z_copy(half, d).start()

    def z_step(half):
        total = y_sum[half, z].astype(F32)
        for d in range(1, 8):
            z_copy(half, d).wait_recv()
            total = total + z_got[half, d - 1].astype(F32)
        gathered[half, n] = total
        for d in range(1, NARROW):
            g_copy(half, d).start()

    def cold_step(piece):
        await_bytes(cold_recv.at[piece], message(cold_got, piece, others))
        units = (0, 1) if piece == 0 else (piece + 1,)

        def unpack(i, carry):
            rows = pl.ds(pl.multiple_of(i * 192, 192), 192)
            for u in units:
                low = 16 * (u % 2)
                block = cold_got[u // 2, pl.ds(i * 8, 8), low : low + 32].astype(F32)
                part = block[:, low // 2 : low // 2 + CAP].reshape(192, 128)
                rows_in[rows, u * 128 : (u + 1) * 128] = part.astype(BF16)
            return carry

        lax.fori_loop(0, 8, unpack, 0)
        cols = slice(units[0] * 128, units[-1] * 128 + 128)

        def quarter(part):
            return mm(quarter_t[part], rows_in[:, cols])

        for d in (2, 1, 3):
            sums_out = quarter(lax.rem(n + d, NARROW)).astype(BF16)
            for i, u in enumerate(units):
                cx_send[u, d - 1] = sums_out[:, i * 128 : (i + 1) * 128]
            cx_copy(piece, d).start()
        cold_out[:, cols] = quarter(n)

    own0 = give(0)
    sums(0)
    core_start(0)
    own1 = give(1)
    lax.fori_loop(1, WIDE, give_rest, 0)
    core_step(0)
    sums(1)
    core_start(1)
    core_step(1)
    x_pass(0)

    asked = want[...].reshape(WIDE, 128)
    high = jnp.floor(asked * (1.0 / 32.0))
    low = asked - 32.0 * high
    line = iota((128, WIDE * CAP), 1)
    within = line - CAP * jnp.floor((line + 0.5) * (1.0 / CAP))
    spot = onehot(within == iota((128, WIDE * CAP), 0))
    spread_out = 32.0 * mm(high.astype(BF16), spot) + mm(low.astype(BF16), spot)
    line64 = iota((WIDE, WIDE * CAP), 1)
    start = iota((WIDE, WIDE * CAP), 0) * CAP
    mine = (line64 >= start) & (line64 < start + CAP)
    asked_line = jnp.sum(jnp.where(mine, spread_out, 0.0), axis=0, keepdims=True)
    for part in range(4):
        quarter_t[part] = onehot(iota((256, WIDE * CAP), 0) + 256.0 * part == asked_line)
    own0.wait()
    own1.wait()

    x_step(0)
    x_pass(1)
    cold_step(0)
    y_step(0)
    x_step(1)
    z_step(0)
    cold_step(1)
    y_step(1)
    cold_step(2)
    z_step(1)
    for half in range(2):
        cols = slice(half * HALF, (half + 1) * HALF)
        for d in range(1, NARROW):
            g_copy(half, d).wait_recv()
        proj_out[:, cols] = gathered[half, 0:2].reshape(32, HALF)
        out_out[:, cols] = gathered[half, 2, 0:8]
        turned[cols, :] = gathered[half, 2, 8:16].T
        for k in range(NARROW):

            @pl.when(n == k)
            def _():
                hot_out[:, cols] = gathered[half, 3, 4 * k : 4 * k + 4]

    gain_out[...] = turned[pl.ds(pl.multiple_of(w * 8, 8), 8), :].T[0:1, :]
    for piece in range(3):
        for d in range(1, NARROW):
            cx_copy(piece, d).wait_recv()
    for u in range(4):
        total = cold_out[:, u * 128 : (u + 1) * 128]
        for d in range(NARROW - 1):
            total = total + cx_got[u, d].astype(F32)
        cold_out[:, u * 128 : (u + 1) * 128] = total

    await_bytes(a2a_send.at[0], req.at[others])
    await_bytes(a2a_send.at[1], reply.at[others])
    for piece in range(3):
        await_bytes(a2a_send.at[2 + piece], message(cold_send, piece, others))
        for d in range(1, NARROW):
            cx_copy(piece, d).wait_send()
    for half in range(2):
        for j in range(4):
            core_copy(half, j).wait_send()
        for side in range(2):
            x_copy(half, side, 0).wait_send()
            x_copy(half, side, 1).wait_send()
            x_on_copy(half, side).wait_send()
        for d in range(1, NARROW):
            y_copy(half, d).wait_send()
            g_copy(half, d).wait_send()
        for d in range(1, 8):
            z_copy(half, d).wait_send()


def finish(*refs):
    sems = refs[-1]
    copies = [pltpu.make_async_copy(refs[i], refs[5 + i], sems.at[i]) for i in range(5)]
    for copy in copies:
        copy.start()
    for copy in copies:
        copy.wait()


def local(
    item_owner, item_row, hot_row, hot_flag, seq_length, cold_table, hot_table, proj_weight, out_weight, norm_gain, cotangent
):
    vm = pl.BlockSpec(memory_space=pltpu.VMEM)
    sm = pl.BlockSpec(memory_space=pltpu.SMEM)
    v = pltpu.VMEM
    dma = pltpu.SemaphoreType.DMA
    slots = WIDE * CAP
    block = (WIDE, 48, 256)
    scratch = [
        v((ROWS, D), BF16), v((TOK, D), BF16), v((D, 4 * D), BF16), v((D, D), BF16), v((TOK, D), BF16),
        v((32, 128), F32), v((8, 128), F32), v((WIDE, 1, 128), F32), v((WIDE, 1, 128), F32),
        v(block, BF16), v(block, BF16), v((slots, D), BF16), v((slots, TOK), BF16), v((TOK, TOK), BF16),
        v((TOK, D), BF16), v((TOK, D), BF16), v((LEN, D), F32), v((LEN, 1), F32),
        v((LEN, 4 * D), BF16), v((LEN, 4 * D), BF16), v((HEADS, LEN, LEN), BF16), v((HEADS, LEN, LEN), BF16),
        v((LEN, D), F32), v((TOK, D), BF16), v((TOK, D), BF16), v((TOK, D), BF16), v((LEN, D), BF16),
        v((TOK, 4 * D), BF16), v((TOK, D), BF16), v((1, D), F32),
        v((2, WIDE, 48, 128), BF16), v((2, WIDE, 48, 128), BF16),
        v((2, 2, 4, 32, 16, HALF), BF16), v((2, 4, 32, 16, HALF), BF16), v((2, 4, 32, 16, HALF), BF16),
        v((2, 2, 2, 16, 16, HALF), BF16), v((2, 2, 16, 16, HALF), BF16), v((2, 2, 16, 16, HALF), BF16),
        v((2, 4, 8, 16, HALF), BF16), v((2, 3, 8, 16, HALF), BF16),
        v((2, 8, 16, HALF), BF16), v((2, 7, 16, HALF), BF16), v((2, 4, 16, HALF), F32),
        v((4, 3, 256, 128), BF16), v((4, 3, 256, 128), BF16), v((4, 256, slots), BF16), v((D, 8), F32),
        dma((5,)), dma((2,)), dma((5,)), dma((8,)), dma((8,)), dma((3,)), dma((8,)), dma((8,)), dma((12,)), dma((12,)), dma((6,)), dma((6,)),
        dma((14,)), dma((14,)), dma((6,)), dma((6,)), dma((9,)), dma((9,)),
    ]
    shape = jax.ShapeDtypeStruct
    results = [shape((32, D), F32), shape((8, D), F32), shape((1, 8), F32), shape((256, D), F32), shape((4, D), F32)]
    hbm = pl.BlockSpec(memory_space=pl.ANY)
    parts = pl.pallas_call(
        kernel,
        out_shape=results,
        in_specs=[vm] * 4 + [sm, vm] + [hbm] * 5,
        out_specs=[vm] * 5,
        scratch_shapes=scratch,
        compiler_params=pltpu.CompilerParams(collective_id=0, has_side_effects=True, vmem_limit_bytes=62 * 1024 * 1024),
    )(
        item_owner.transpose(0, 2, 1), item_row, hot_row, hot_flag, seq_length, norm_gain,
        cold_table, hot_table, proj_weight, out_weight, cotangent.reshape(TOK, D),
    )
    proj, out, gain, cold, hot = pl.pallas_call(
        finish,
        out_shape=results,
        in_specs=[vm] * 5,
        out_specs=[hbm] * 5,
        scratch_shapes=[dma((5,))],
    )(*parts)
    return proj.T, out.T, gain, cold, hot


def solution(mesh):
    both = P(("wide", "narrow"))
    in_specs = (both, both, both, both, both, P("wide"), P(), P(), P(), P(), both)
    out_specs = (P(None, "wide"), P(None, "wide"), P(None, "wide"), both, both)
    return jax.shard_map(local, mesh=mesh, in_specs=in_specs, out_specs=out_specs, check_vma=False)
```

```python
import functools

import jax
import jax.numpy as jnp
from jax import lax
from jax.experimental import pallas as pl
from jax.experimental.pallas import tpu as pltpu
from jax.sharding import PartitionSpec as P

WIDE = 64
NARROW = 4
CAP = 24
TOK = 1024
LEN = 512
D = 512
HALF = 256
HEADS = 4
ROWS = 1024
EPS = 1e-05
SCALE = 128 ** (-0.5)
MESH = pl.DeviceIdType.MESH
F32 = jnp.float32
BF16 = jnp.bfloat16


def mm(a, b):
    return jnp.dot(a, b, preferred_element_type=F32)


def mm_nt(a, b):
    return lax.dot_general(a, b, (((1,), (1,)), ((), ())), preferred_element_type=F32)


def mm_tn(a, b):
    return lax.dot_general(a, b, (((0,), (0,)), ((), ())), preferred_element_type=F32)


def iota(shape, dim):
    return lax.broadcasted_iota(jnp.int32, shape, dim).astype(F32)


def sigmoid(x):
    return 0.5 * jnp.tanh(0.5 * x) + 0.5


def onehot(mask):
    return jnp.where(mask, 1.0, 0.0).astype(BF16)


def mean(x):
    return jnp.mean(x, axis=-1, keepdims=True)


def pack(rows):
    half = rows.shape[1] // 2
    blocks = rows.reshape(-1, CAP, rows.shape[1])
    return jnp.concatenate([blocks[:, :, :half], blocks[:, :, half:]], axis=1).astype(BF16)


def kernel(
    owner_in, row_in_in, hot_row_in, hot_flag_in, lens_in, gain_in, table_in, hot_table_in, weight_in, out_weight_in, cot_in,
    proj_out, out_out, gain_out, cold_out, hot_out,
    owner, row_in, hot_row, hot_flag, lens, gain, table, hot_table, weight, out_weight, cot, tok, slots, req, want, reply, got, rows_in, place_t, hot_t, emb, normed, xhat, spread, acted, dact,
    attn, dattn, per_head, mixed, masked, mixed_cot, dhead, proj_cot, emb_grad, gain_sum,
    cold_send, cold_got, wsum, core_got, core_sum, x_got, x_on, x_on_got, x_sum, y_got, y_sum, z_got, gathered, cx_send, cx_got, quarter_t, turned,
    load_sem, loc_sem, a2a_send, req_recv, rep_recv, cold_recv, core_ss, core_rs, x_ss, x_rs, y_ss, y_rs, z_ss, z_rs, g_ss, g_rs, cx_ss, cx_rs,
):
    w = lax.axis_index("wide")
    n = lax.axis_index("narrow")
    core = lax.rem(w, 2)
    chip = lax.div(w, 2)
    z = lax.rem(chip, 8)
    y = lax.div(chip, 8)

    loads = [
        pltpu.make_async_copy(src, dst, load_sem.at[i])
        for i, (src, dst) in enumerate(
            [
                (owner_in, owner), (row_in_in, row_in), (hot_row_in, hot_row), (hot_flag_in, hot_flag), (table_in, table),
                (lens_in, lens), (gain_in, gain), (hot_table_in, hot_table), (cot_in, cot), (out_weight_in, out_weight),
                (weight_in, weight),
            ]
        )
    ]
    for load in loads:
        load.start()

    barrier = pltpu.get_barrier_semaphore()

    def greet(d, carry):
        pl.semaphore_signal(barrier, inc=1, device_id=(lax.rem(w + d, WIDE), n), device_id_type=MESH)
        return carry

    lax.fori_loop(1, WIDE, greet, 0)
    for d in range(1, NARROW):
        pl.semaphore_signal(barrier, inc=1, device_id=(w, lax.rem(n + d, NARROW)), device_id_type=MESH)

    for load in loads[:4]:
        load.wait()
    for a in range(8):
        at = (slice(a // 4, a // 4 + 1), slice(a % 4 * 128, a % 4 * 128 + 128))
        tok[a : a + 1, :] = owner[a // 4, :, at[1]].astype(F32)
        tok[8 + a : 9 + a, :] = row_in[at].astype(F32)
        tok[16 + a : 17 + a, :] = jnp.where(hot_flag[at] == 1, hot_row[at], -1).astype(F32)

    upper = onehot(iota((128, 128), 0) < iota((128, 128), 1))
    sub = iota((128, 128), 0)
    carry = jnp.zeros((128, 1), F32)
    req_hi = jnp.zeros((128, 128), F32)
    req_lo = jnp.zeros((128, 128), F32)
    for a in range(8):
        own = tok[a : a + 1, :]
        row = tok[8 + a : 9 + a, :]
        hot = tok[16 + a : 17 + a, :]
        owns = jnp.where(sub == own, 1.0, 0.0)
        owns_b = owns.astype(BF16)
        before = mm(owns_b, upper) + carry
        rank = jnp.sum(owns * before, axis=0, keepdims=True)
        carry = carry + jnp.sum(owns, axis=1, keepdims=True)
        slots[a : a + 1, :] = jnp.where(hot >= 0.0, -1.0, own * CAP + rank)
        high = jnp.floor(row * (1.0 / 32.0))
        low = row - 32.0 * high
        ranked = sub == rank
        req_hi = req_hi + mm_nt(owns_b, jnp.where(ranked, high, 0.0).astype(BF16))
        req_lo = req_lo + mm_nt(owns_b, jnp.where(ranked, low, 0.0).astype(BF16))
    asked = 32.0 * req_hi + req_lo
    for o in range(WIDE):
        req[o] = asked[o : o + 1, :]

    pl.semaphore_wait(barrier, WIDE - 1 + NARROW - 1)

    group = lax.div(w, 8)

    def exchange(src, dst, sends, recv, p):
        return pltpu.make_async_remote_copy(
            src_ref=src, dst_ref=dst, send_sem=a2a_send.at[sends], recv_sem=recv, device_id=(p, n), device_id_type=MESH
        )

    def await_bytes(sem, view):
        pltpu.make_async_copy(view, view, sem).wait()

    others = pl.ds(0, WIDE - 1)

    def ask(d, carry):
        p = lax.rem(w + d, WIDE)
        exchange(req.at[p], want.at[w], 0, req_recv.at[group], p).start()
        return carry

    lax.fori_loop(1, WIDE, ask, 0)
    pltpu.make_async_copy(req.at[w], want.at[w], req_recv.at[group]).start()
    loads[4].wait()

    lanes = iota((CAP, ROWS), 1)

    def answer(i, carry):
        which = lax.rem(group + i, 8)
        first = which * 8
        eight = pl.ds(first, 8)
        await_bytes(req_recv.at[which], want.at[eight])
        asked8 = want[eight].reshape(8, 128).T
        picks = jnp.concatenate([jnp.where(lanes == asked8[:CAP, j : j + 1], 1.0, 0.0) for j in range(8)], axis=0)
        reply[eight] = pack(mm(picks.astype(BF16), table[...]))
        for j in range(8):
            p = first + j

            @pl.when(p != w)
            def _():
                exchange(reply.at[p], got.at[w], 1, rep_recv.at[group], p).start()

        return carry

    lax.fori_loop(0, 8, answer, 0)
    pltpu.make_async_copy(reply.at[w], got.at[w], rep_recv.at[group]).start()

    def build_place(a, carry):
        rows = pl.ds(pl.multiple_of(a * 192, 192), 192)
        at = iota((192, 128), 0) + (a * 192).astype(F32)
        for b in range(8):
            place_t[rows, b * 128 : (b + 1) * 128] = onehot(at == slots[b : b + 1, :])
        return carry

    lax.fori_loop(0, 8, build_place, 0)

    def build_hot(a, carry):
        rows = pl.ds(pl.multiple_of(a * 128, 128), 128)
        at = iota((128, 128), 0) + (a * 128).astype(F32)
        for b in range(8):
            hot_t[rows, b * 128 : (b + 1) * 128] = onehot(at == tok[16 + b : 17 + b, :])
        return carry

    lax.fori_loop(0, 8, build_hot, 0)
    for load in loads[5:]:
        load.wait()
    tok_cols = tok[...].T
    for half in range(2):
        rows = slice(half * LEN, (half + 1) * LEN)
        hots = jnp.concatenate(
            [onehot(iota((128, TOK), 1) == tok_cols[:, 16 + a : 17 + a]) for a in range(half * 4, half * 4 + 4)], axis=0
        )
        emb[rows, :] = mm(hots, hot_table[...]).astype(BF16)
        live = iota((LEN, 1), 0) < lens[half].astype(F32)
        masked[rows, :] = jnp.where(live, cot[rows, :].astype(F32), 0.0).astype(BF16)
        mixed_cot[rows, :] = mm_nt(masked[rows, :], out_weight[...]).astype(BF16)

    slot_cols = slots[...].T

    def place(i, carry):
        which = lax.rem(group - i + 8, 8)
        eight = pl.ds(which * 8, 8)
        await_bytes(rep_recv.at[which], got.at[eight])
        block = got[eight].astype(F32)
        rows_8 = jnp.concatenate([block[:, :CAP].reshape(192, HALF), block[:, CAP:].reshape(192, HALF)], axis=1)
        at = iota((128, 192), 1) + (which * 192).astype(F32)
        picks = jnp.concatenate([onehot(at == slot_cols[:, a : a + 1]) for a in range(8)], axis=0)
        emb[...] = (emb[...].astype(F32) + mm(picks, rows_8.astype(BF16))).astype(BF16)
        return carry

    lax.fori_loop(0, 8, place, 0)

    gain_sum[...] = jnp.zeros_like(gain_sum)

    def layer(s, carry):
        base = s * LEN
        rows = pl.ds(pl.multiple_of(base, LEN), LEN)
        length = lens[s].astype(F32)

        def norm(t, c):
            part = pl.ds(pl.multiple_of(base + t * 256, 256), 256)
            here = pl.ds(pl.multiple_of(t * 256, 256), 256)
            x = emb[part, :].astype(F32)
            center = x - mean(x)
            r = lax.rsqrt(mean(center * center) + EPS)
            hat = center * r
            xhat[here, :] = hat
            spread[here, :] = r
            normed[part, :] = (hat * gain[...]).astype(BF16)
            return c

        lax.fori_loop(0, 2, norm, 0)

        def project(cb, c):
            def raw(i):
                return mm(normed[rows, :], weight[:, i * 256 : i * 256 + 256])

            ahead = raw(0)
            for i in range(8):
                x = 0.5 * ahead
                if i < 7:
                    ahead = raw(i + 1)
                cols = slice(i * 256, i * 256 + 256)
                t = jnp.tanh(x)
                xt = x * t
                acted[:, cols] = (xt + x).astype(BF16)
                dact[:, cols] = ((0.5 * t + 0.5) * (1.0 + x - xt)).astype(BF16)
            return c

        lax.fori_loop(0, 1, project, 0)

        def cols_of(block, h):
            return pl.ds(pl.multiple_of(block * D + h * 128, 128), 128)

        inverse = jnp.where(iota((1, LEN), 1) < length, 1.0 / jnp.full((1, LEN), length), 0.0)

        def attend(pair, c):
            for h in [pair * 4 + i for i in range(4)]:
                for part in range(2):
                    keys = 256 * (part + 1)
                    at = slice(256 * part, 256 * part + 256)
                    k = acted[:keys, cols_of(3, h)]
                    x = mm_nt(acted[at, cols_of(2, h)], k) * (0.5 * SCALE)
                    t = jnp.tanh(x)
                    xt = x * t
                    a = xt + x
                    slope = (t + 1.0) * (1.0 + x - xt)
                    weights = []
                    for block in range(part + 1):
                        these = slice(256 * block, 256 * block + 256)
                        scale = inverse[:, these]
                        if block == part:
                            scale = jnp.where(iota((256, 256), 1) <= iota((256, 256), 0), scale, 0.0)
                        weights.append((a[:, these] * scale).astype(BF16))
                        attn[h, at, these] = weights[-1]
                        dattn[h, at, these] = (slope[:, these] * scale).astype(BF16)
                    w_all = weights[0] if part == 0 else jnp.concatenate(weights, axis=1)
                    per_head[at, pl.ds(pl.multiple_of(h * 128, 128), 128)] = mm(w_all, acted[:keys, cols_of(1, h)])
            return c

        lax.fori_loop(0, 1, attend, 0)

        def gate_step(t, c):
            part = pl.ds(pl.multiple_of(t * 256, 256), 256)
            whole = pl.ds(pl.multiple_of(base + t * 256, 256), 256)
            x = per_head[part, :]
            center = x - mean(x)
            r = lax.rsqrt(mean(center * center) + EPS)
            hat = center * r
            gate = acted[part, :D].astype(F32)
            g = mixed_cot[whole, :].astype(F32)
            mixed[whole, :] = (hat * gate).astype(BF16)
            dgate = (g * hat).astype(BF16)
            proj_cot[whole, :D] = dgate * dact[part, :D]
            dhat = g * gate
            dhead[part, :] = (r * (dhat - mean(dhat) - hat * mean(dhat * hat))).astype(BF16)
            return c

        lax.fori_loop(0, 2, gate_step, 0)

        def attend_back(pair, c):
            for h in [pair * 4 + i for i in range(4)]:
                head_back(h)
            return c

        def head_back(h):
            def put(block, at, to, grad):
                cols = cols_of(block, h)
                proj_cot[to, cols] = grad.astype(BF16) * dact[at, cols]

            dks, dvs = [], []
            for part in range(2):
                keys = 256 * (part + 1)
                at = slice(256 * part, 256 * part + 256)
                q = acted[at, cols_of(2, h)]
                k = acted[:keys, cols_of(3, h)]
                v = acted[:keys, cols_of(1, h)]
                do = dhead[at, pl.ds(pl.multiple_of(h * 128, 128), 128)]
                ds = mm_nt(do, v).astype(BF16) * dattn[h, at, :keys]
                put(2, at, pl.ds(pl.multiple_of(base + 256 * part, 256), 256), mm(ds, k) * (0.5 * SCALE))
                dks.append(mm_tn(ds, q) * (0.5 * SCALE))
                dvs.append(mm_tn(attn[h, at, :keys], do))
            for block, grads in ((3, dks), (1, dvs)):
                put(block, slice(0, 256), pl.ds(pl.multiple_of(base, 256), 256), grads[0] + grads[1][:256])
                put(block, slice(256, 512), pl.ds(pl.multiple_of(base + 256, 256), 256), grads[1][256:])

        lax.fori_loop(0, 1, attend_back, 0)

        for t in range(2):
            here = slice(256 * t, 256 * t + 256)
            part = pl.ds(pl.multiple_of(base + 256 * t, 256), 256)
            ncot = mm_nt(proj_cot[part, :], weight[...])
            hat = xhat[here, :]
            gain_sum[...] += jnp.sum(ncot * hat, axis=0, keepdims=True)
            d = ncot * gain[...]
            ecot = spread[here, :] * (d - mean(d) - hat * mean(d * hat))
            total = masked[part, :].astype(F32) + ecot
            emb_grad[part, :] = jnp.where(iota((256, 1), 0) + 256.0 * t < length, total, 0.0).astype(BF16)
        return carry

    lax.fori_loop(0, 2, layer, 0)

    def give(half):
        def step(i, carry):
            first = lax.rem(group + i, 8) * 8
            rows = pl.ds(pl.multiple_of(first * CAP, 192), 192)
            cold_send[half, pl.ds(first, 8)] = pack(mm(place_t[rows, :], emb_grad[:, half * HALF : (half + 1) * HALF]))
            for j in range(8):
                p = first + j

                @pl.when(p != w)
                def _():
                    give_copy(half, p).start()

            return carry

        lax.fori_loop(0, 8, step, 0)
        own = pltpu.make_async_copy(cold_send.at[half, w], cold_got.at[half, w], loc_sem.at[half])
        own.start()
        return own

    def message(ref, which, block):
        if which == 0:
            return ref.at[0, block]
        return ref.at[1, block, pl.ds(0, 32)] if which == 1 else ref.at[1, block, pl.ds(32, 16)]

    def give_copy(which, p):
        return exchange(message(cold_send, which, p), message(cold_got, which, w), 2 + which, cold_recv.at[which], p)

    def give_rest(d, carry):
        give_copy(2, lax.rem(w + d, WIDE)).start()
        return carry

    def sums_a(half):
        cols = slice(half * HALF, (half + 1) * HALF)
        out_grad = mm_tn(masked[...], mixed[:, cols]).reshape(WIDE, 8, HALF)
        gains = jnp.broadcast_to(gain_sum[:, cols].reshape(1, 1, HALF), (WIDE, 8, HALF))
        both = jnp.concatenate([out_grad, gains], axis=1).reshape(32, 2, 16, HALF).astype(BF16)
        hots = mm(hot_t[...], emb_grad[:, cols]).reshape(32, 2, 16, HALF).astype(BF16)
        for c in range(2):
            wsum[half, c, 2] = both[:, c]
            wsum[half, c, 3] = hots[:, c]

    def sums_b(half):
        cols = slice(half * HALF, (half + 1) * HALF)

        def weight_grad(cb, carry):
            grad = mm_tn(proj_cot[:, pl.ds(pl.multiple_of(cb * D, D), D)], normed[:, cols]).reshape(8, 2, 2, 16, HALF).astype(BF16)
            for c in range(2):
                for part in range(2):
                    wsum[half, c, part, pl.ds(cb * 8, 8)] = grad[:, c, part]
            return carry

        lax.fori_loop(0, 4, weight_grad, 0)

    peer = w + 1 - 2 * core
    sides = (n + 1 - 2 * lax.rem(n, 2), NARROW - 1 - n)
    parts = (lax.rem(n + 2, NARROW), sides[0], sides[1], n)

    def remote(src, dst, sems, index, to):
        return pltpu.make_async_remote_copy(
            src_ref=src, dst_ref=dst, send_sem=sems[0].at[index], recv_sem=sems[1].at[index],
            device_id=to, device_id_type=MESH,
        )

    def core_copy(half, part):
        src = wsum.at[half, 1 - core, part]
        return remote(src, core_got.at[half, part], (core_ss, core_rs), half * 4 + part, (peer, n))

    def chips(side):
        return pl.ds(16 * side, 16)

    def x_copy(half, side, on):
        src = core_sum.at[half, parts[0] if on else sides[side], chips(side)]
        return remote(src, x_got.at[half, side, on], (x_ss, x_rs), half * 6 + side * 3 + on, (w, sides[side]))

    def x_on_copy(half, side):
        dst = x_on_got.at[half, side]
        return remote(x_on.at[half, side], dst, (x_ss, x_rs), half * 6 + side * 3 + 2, (w, sides[1 - side]))

    def y_copy(half, d):
        to = lax.rem(y + d, 4)
        return remote(
            x_sum.at[half, to], y_got.at[half, d - 1], (y_ss, y_rs), half * 3 + d - 1, ((to * 8 + z) * 2 + core, n)
        )

    def z_copy(half, d):
        to = lax.rem(z + d, 8)
        return remote(
            y_sum.at[half, to], z_got.at[half, d - 1], (z_ss, z_rs), half * 7 + d - 1, ((y * 8 + to) * 2 + core, n)
        )

    def g_copy(half, d):
        to = lax.rem(n + d, NARROW)
        return remote(gathered.at[half, n], gathered.at[half, n], (g_ss, g_rs), half * 3 + d - 1, (w, to))

    def cx_copy(piece, d):
        to = lax.rem(n + d, NARROW)
        units = pl.ds(0, 2) if piece == 0 else pl.ds(piece + 1, 1)
        return remote(cx_send.at[units, d - 1], cx_got.at[units, d - 1], (cx_ss, cx_rs), piece * 3 + d - 1, (w, to))

    def core_start(half, first):
        for part in (first, first + 1):
            core_copy(half, part).start()

    def core_step(half):
        for part in range(4):
            core_copy(half, part).wait_recv()
        for j in range(4):
            part = parts[j]
            core_sum[half, part] = (wsum[half, core, part].astype(F32) + core_got[half, part].astype(F32)).astype(BF16)
            if j == 0:
                x_copy(half, 0, 1).start()
                x_copy(half, 1, 1).start()
            elif j < 3:
                x_copy(half, j - 1, 0).start()

    def x_pass(half):
        for side in range(2):
            x_copy(half, side, 1).wait_recv()
            mine = core_sum[half, sides[1 - side], chips(side)].astype(F32)
            x_on[half, side] = (mine + x_got[half, side, 1].astype(F32)).astype(BF16)
            x_on_copy(half, side).start()

    def x_step(half):
        for side in range(2):
            x_copy(half, side, 0).wait_recv()
            x_on_copy(half, side).wait_recv()
            total = core_sum[half, n, chips(side)].astype(F32) + x_got[half, side, 0].astype(F32)
            total = total + x_on_got[half, side].astype(F32)
            x_sum[half, 2 * side : 2 * side + 2] = total.astype(BF16).reshape(2, 8, 16, HALF)
        for d in (2, 1, 3):
            y_copy(half, d).start()

    def y_step(half):
        total = x_sum[half, y].astype(F32)
        for d in (1, 3, 2):
            y_copy(half, d).wait_recv()
            total = total + y_got[half, d - 1].astype(F32)
        y_sum[half] = total.astype(BF16)
        for d in range(1, 8):
            z_copy(half, d).start()

    def z_step(half):
        total = y_sum[half, z].astype(F32)
        for d in range(1, 8):
            z_copy(half, d).wait_recv()
            total = total + z_got[half, d - 1].astype(F32)
        gathered[half, n] = total
        for d in range(1, NARROW):
            g_copy(half, d).start()

    def cold_step(piece):
        await_bytes(cold_recv.at[piece], message(cold_got, piece, others))
        units = (0, 1) if piece == 0 else (piece + 1,)

        def unpack(i, carry):
            rows = pl.ds(pl.multiple_of(i * 192, 192), 192)
            for u in units:
                low = 16 * (u % 2)
                block = cold_got[u // 2, pl.ds(i * 8, 8), low : low + 32].astype(F32)
                part = block[:, low // 2 : low // 2 + CAP].reshape(192, 128)
                rows_in[rows, u * 128 : (u + 1) * 128] = part.astype(BF16)
            return carry

        lax.fori_loop(0, 8, unpack, 0)
        cols = slice(units[0] * 128, units[-1] * 128 + 128)

        def quarter(part):
            return mm(quarter_t[part], rows_in[:, cols])

        for d in (2, 1, 3):
            sums_out = quarter(lax.rem(n + d, NARROW)).astype(BF16)
            for i, u in enumerate(units):
                cx_send[u, d - 1] = sums_out[:, i * 128 : (i + 1) * 128]
            cx_copy(piece, d).start()
        cold_out[:, cols] = quarter(n)

    own0 = give(0)
    sums_a(0)
    core_start(0, 2)
    sums_b(0)
    core_start(0, 0)
    sums_a(1)
    core_start(1, 2)
    core_step(0)
    sums_b(1)
    core_start(1, 0)
    own1 = give(1)
    lax.fori_loop(1, WIDE, give_rest, 0)
    core_step(1)
    x_pass(0)

    asked = want[...].reshape(WIDE, 128)
    high = jnp.floor(asked * (1.0 / 32.0))
    low = asked - 32.0 * high
    line = iota((128, WIDE * CAP), 1)
    within = line - CAP * jnp.floor((line + 0.5) * (1.0 / CAP))
    spot = onehot(within == iota((128, WIDE * CAP), 0))
    spread_out = 32.0 * mm(high.astype(BF16), spot) + mm(low.astype(BF16), spot)
    line64 = iota((WIDE, WIDE * CAP), 1)
    start = iota((WIDE, WIDE * CAP), 0) * CAP
    mine = (line64 >= start) & (line64 < start + CAP)
    asked_line = jnp.sum(jnp.where(mine, spread_out, 0.0), axis=0, keepdims=True)
    for part in range(4):
        quarter_t[part] = onehot(iota((256, WIDE * CAP), 0) + 256.0 * part == asked_line)
    own0.wait()
    own1.wait()

    x_pass(1)
    x_step(0)
    x_step(1)
    cold_step(0)
    y_step(0)
    cold_step(1)
    y_step(1)
    z_step(0)
    cold_step(2)
    z_step(1)
    for half in range(2):
        cols = slice(half * HALF, (half + 1) * HALF)
        for d in range(1, NARROW):
            g_copy(half, d).wait_recv()
        proj_out[:, cols] = gathered[half, 0:2].reshape(32, HALF)
        out_out[:, cols] = gathered[half, 2, 0:8]
        turned[cols, :] = gathered[half, 2, 8:16].T
        for k in range(NARROW):

            @pl.when(n == k)
            def _():
                hot_out[:, cols] = gathered[half, 3, 4 * k : 4 * k + 4]

    gain_out[...] = turned[pl.ds(pl.multiple_of(w * 8, 8), 8), :].T[0:1, :]
    for piece in range(3):
        for d in range(1, NARROW):
            cx_copy(piece, d).wait_recv()
    for u in range(4):
        total = cold_out[:, u * 128 : (u + 1) * 128]
        for d in range(NARROW - 1):
            total = total + cx_got[u, d].astype(F32)
        cold_out[:, u * 128 : (u + 1) * 128] = total

    await_bytes(a2a_send.at[0], req.at[others])
    await_bytes(a2a_send.at[1], reply.at[others])
    for piece in range(3):
        await_bytes(a2a_send.at[2 + piece], message(cold_send, piece, others))
        for d in range(1, NARROW):
            cx_copy(piece, d).wait_send()
    for half in range(2):
        for part in range(4):
            core_copy(half, part).wait_send()
        for side in range(2):
            x_copy(half, side, 0).wait_send()
            x_copy(half, side, 1).wait_send()
            x_on_copy(half, side).wait_send()
        for d in range(1, NARROW):
            y_copy(half, d).wait_send()
            g_copy(half, d).wait_send()
        for d in range(1, 8):
            z_copy(half, d).wait_send()


def finish(*refs):
    sems = refs[-1]
    copies = [pltpu.make_async_copy(refs[i], refs[5 + i], sems.at[i]) for i in range(5)]
    for copy in copies:
        copy.start()
    for copy in copies:
        copy.wait()


def local(
    item_owner, item_row, hot_row, hot_flag, seq_length, cold_table, hot_table, proj_weight, out_weight, norm_gain, cotangent
):
    vm = pl.BlockSpec(memory_space=pltpu.VMEM)
    v = pltpu.VMEM
    dma = pltpu.SemaphoreType.DMA
    slots = WIDE * CAP
    block = (WIDE, 48, 256)
    i32 = jnp.int32
    scratch = [
        v((2, 1, LEN), i32), v((2, LEN), i32), v((2, LEN), i32), v((2, LEN), i32), pltpu.SMEM((2,), i32), v((1, D), F32),
        v((ROWS, D), BF16), v((TOK, D), BF16), v((D, 4 * D), BF16), v((D, D), BF16), v((TOK, D), BF16),
        v((32, 128), F32), v((8, 128), F32), v((WIDE, 1, 128), F32), v((WIDE, 1, 128), F32),
        v(block, BF16), v(block, BF16), v((slots, D), BF16), v((slots, TOK), BF16), v((TOK, TOK), BF16),
        v((TOK, D), BF16), v((TOK, D), BF16), v((LEN, D), F32), v((LEN, 1), F32),
        v((LEN, 4 * D), BF16), v((LEN, 4 * D), BF16), v((HEADS, LEN, LEN), BF16), v((HEADS, LEN, LEN), BF16),
        v((LEN, D), F32), v((TOK, D), BF16), v((TOK, D), BF16), v((TOK, D), BF16), v((LEN, D), BF16),
        v((TOK, 4 * D), BF16), v((TOK, D), BF16), v((1, D), F32),
        v((2, WIDE, 48, 128), BF16), v((2, WIDE, 48, 128), BF16),
        v((2, 2, 4, 32, 16, HALF), BF16), v((2, 4, 32, 16, HALF), BF16), v((2, 4, 32, 16, HALF), BF16),
        v((2, 2, 2, 16, 16, HALF), BF16), v((2, 2, 16, 16, HALF), BF16), v((2, 2, 16, 16, HALF), BF16),
        v((2, 4, 8, 16, HALF), BF16), v((2, 3, 8, 16, HALF), BF16),
        v((2, 8, 16, HALF), BF16), v((2, 7, 16, HALF), BF16), v((2, 4, 16, HALF), F32),
        v((4, 3, 256, 128), BF16), v((4, 3, 256, 128), BF16), v((4, 256, slots), BF16), v((D, 8), F32),
        dma((11,)), dma((2,)), dma((5,)), dma((8,)), dma((8,)), dma((3,)), dma((8,)), dma((8,)), dma((12,)), dma((12,)), dma((6,)), dma((6,)),
        dma((14,)), dma((14,)), dma((6,)), dma((6,)), dma((9,)), dma((9,)),
    ]
    shape = jax.ShapeDtypeStruct
    results = [shape((32, D), F32), shape((8, D), F32), shape((1, 8), F32), shape((256, D), F32), shape((4, D), F32)]
    hbm = pl.BlockSpec(memory_space=pl.ANY)
    parts = pl.pallas_call(
        kernel,
        out_shape=results,
        in_specs=[hbm] * 11,
        out_specs=[vm] * 5,
        scratch_shapes=scratch,
        compiler_params=pltpu.CompilerParams(collective_id=0, has_side_effects=True, vmem_limit_bytes=62 * 1024 * 1024),
    )(
        item_owner.transpose(0, 2, 1), item_row, hot_row, hot_flag, seq_length, norm_gain,
        cold_table, hot_table, proj_weight, out_weight, cotangent.reshape(TOK, D),
    )
    proj, out, gain, cold, hot = pl.pallas_call(
        finish,
        out_shape=results,
        in_specs=[vm] * 5,
        out_specs=[hbm] * 5,
        scratch_shapes=[dma((5,))],
    )(*parts)
    return proj.T, out.T, gain, cold, hot


def solution(mesh):
    both = P(("wide", "narrow"))
    in_specs = (both, both, both, both, both, P("wide"), P(), P(), P(), P(), both)
    out_specs = (P(None, "wide"), P(None, "wide"), P(None, "wide"), both, both)
    return jax.shard_map(local, mesh=mesh, in_specs=in_specs, out_specs=out_specs, check_vma=False)
```

```python
import functools

import jax
import jax.numpy as jnp
from jax import lax
from jax.experimental import pallas as pl
from jax.experimental.pallas import tpu as pltpu
from jax.sharding import PartitionSpec as P

WIDE = 64
NARROW = 4
CAP = 24
TOK = 1024
LEN = 512
D = 512
HALF = 256
HEADS = 4
ROWS = 1024
EPS = 1e-05
SCALE = 128 ** (-0.5)
MESH = pl.DeviceIdType.MESH
F32 = jnp.float32
BF16 = jnp.bfloat16


def mm(a, b):
    return jnp.dot(a, b, preferred_element_type=F32)


def mm_nt(a, b):
    return lax.dot_general(a, b, (((1,), (1,)), ((), ())), preferred_element_type=F32)


def mm_tn(a, b):
    return lax.dot_general(a, b, (((0,), (0,)), ((), ())), preferred_element_type=F32)


def iota(shape, dim):
    return lax.broadcasted_iota(jnp.int32, shape, dim).astype(F32)


def sigmoid(x):
    return 0.5 * jnp.tanh(0.5 * x) + 0.5


def onehot(mask):
    return jnp.where(mask, 1.0, 0.0).astype(BF16)


def mean(x):
    return jnp.mean(x, axis=-1, keepdims=True)


def pack(rows):
    half = rows.shape[1] // 2
    blocks = rows.reshape(-1, CAP, rows.shape[1])
    return jnp.concatenate([blocks[:, :, :half], blocks[:, :, half:]], axis=1).astype(BF16)


def kernel(
    owner_in, row_in_in, hot_row_in, hot_flag_in, lens_in, gain_in, table_in, hot_table_in, weight_in, out_weight_in, cot_in,
    proj_out, out_out, gain_out, cold_out, hot_out,
    owner, row_in, hot_row, hot_flag, lens, gain, table, hot_table, weight, out_weight, cot, tok, slots, req, want, reply, got, rows_in, place_t, hot_t, emb, normed, xhat, spread, acted, dact,
    attn, dattn, per_head, mixed, masked, mixed_cot, dhead, proj_cot, emb_grad, gain_sum,
    cold_send, cold_got, wsum, core_got, core_sum, x_got, x_on, x_on_got, x_sum, y_got, y_sum, z_got, gathered, cx_send, cx_got, quarter_t, turned,
    load_sem, loc_sem, a2a_send, req_recv, rep_recv, cold_recv, core_ss, core_rs, x_ss, x_rs, y_ss, y_rs, z_ss, z_rs, g_ss, g_rs, cx_ss, cx_rs,
):
    w = lax.axis_index("wide")
    n = lax.axis_index("narrow")
    core = lax.rem(w, 2)
    chip = lax.div(w, 2)
    z = lax.rem(chip, 8)
    y = lax.div(chip, 8)

    loads = [
        pltpu.make_async_copy(src, dst, load_sem.at[i])
        for i, (src, dst) in enumerate(
            [
                (owner_in, owner), (row_in_in, row_in), (hot_row_in, hot_row), (hot_flag_in, hot_flag), (table_in, table),
                (lens_in, lens), (gain_in, gain), (hot_table_in, hot_table), (cot_in, cot), (out_weight_in, out_weight),
                (weight_in, weight),
            ]
        )
    ]
    for load in loads:
        load.start()

    barrier = pltpu.get_barrier_semaphore()

    def greet(d, carry):
        pl.semaphore_signal(barrier, inc=1, device_id=(lax.rem(w + d, WIDE), n), device_id_type=MESH)
        return carry

    lax.fori_loop(1, WIDE, greet, 0)
    for d in range(1, NARROW):
        pl.semaphore_signal(barrier, inc=1, device_id=(w, lax.rem(n + d, NARROW)), device_id_type=MESH)

    for load in loads[:4]:
        load.wait()
    for a in range(8):
        at = (slice(a // 4, a // 4 + 1), slice(a % 4 * 128, a % 4 * 128 + 128))
        tok[a : a + 1, :] = owner[a // 4, :, at[1]].astype(F32)
        tok[8 + a : 9 + a, :] = row_in[at].astype(F32)
        tok[16 + a : 17 + a, :] = jnp.where(hot_flag[at] == 1, hot_row[at], -1).astype(F32)

    upper = onehot(iota((128, 128), 0) < iota((128, 128), 1))
    sub = iota((128, 128), 0)
    carry = jnp.zeros((128, 1), F32)
    req_hi = jnp.zeros((128, 128), F32)
    req_lo = jnp.zeros((128, 128), F32)
    for a in range(8):
        own = tok[a : a + 1, :]
        row = tok[8 + a : 9 + a, :]
        hot = tok[16 + a : 17 + a, :]
        owns = jnp.where(sub == own, 1.0, 0.0)
        owns_b = owns.astype(BF16)
        before = mm(owns_b, upper) + carry
        rank = jnp.sum(owns * before, axis=0, keepdims=True)
        carry = carry + jnp.sum(owns, axis=1, keepdims=True)
        slots[a : a + 1, :] = jnp.where(hot >= 0.0, -1.0, own * CAP + rank)
        high = jnp.floor(row * (1.0 / 32.0))
        low = row - 32.0 * high
        ranked = sub == rank
        req_hi = req_hi + mm_nt(owns_b, jnp.where(ranked, high, 0.0).astype(BF16))
        req_lo = req_lo + mm_nt(owns_b, jnp.where(ranked, low, 0.0).astype(BF16))
    asked = 32.0 * req_hi + req_lo
    for o in range(WIDE):
        req[o] = asked[o : o + 1, :]

    pl.semaphore_wait(barrier, WIDE - 1 + NARROW - 1)

    group = lax.div(w, 8)

    def exchange(src, dst, sends, recv, p):
        return pltpu.make_async_remote_copy(
            src_ref=src, dst_ref=dst, send_sem=a2a_send.at[sends], recv_sem=recv, device_id=(p, n), device_id_type=MESH
        )

    def await_bytes(sem, view):
        pltpu.make_async_copy(view, view, sem).wait()

    others = pl.ds(0, WIDE - 1)

    def ask(d, carry):
        p = lax.rem(w + d, WIDE)
        exchange(req.at[p], want.at[w], 0, req_recv.at[group], p).start()
        return carry

    lax.fori_loop(1, WIDE, ask, 0)
    pltpu.make_async_copy(req.at[w], want.at[w], req_recv.at[group]).start()
    loads[4].wait()

    lanes = iota((CAP, ROWS), 1)

    def answer(i, carry):
        which = lax.rem(group + i, 8)
        first = which * 8
        eight = pl.ds(first, 8)
        await_bytes(req_recv.at[which], want.at[eight])
        asked8 = want[eight].reshape(8, 128).T
        picks = jnp.concatenate([jnp.where(lanes == asked8[:CAP, j : j + 1], 1.0, 0.0) for j in range(8)], axis=0)
        reply[eight] = pack(mm(picks.astype(BF16), table[...]))
        for j in range(8):
            p = first + j

            @pl.when(p != w)
            def _():
                exchange(reply.at[p], got.at[w], 1, rep_recv.at[group], p).start()

        return carry

    lax.fori_loop(0, 8, answer, 0)
    pltpu.make_async_copy(reply.at[w], got.at[w], rep_recv.at[group]).start()

    def build_place(a, carry):
        rows = pl.ds(pl.multiple_of(a * 192, 192), 192)
        at = iota((192, 128), 0) + (a * 192).astype(F32)
        for b in range(8):
            place_t[rows, b * 128 : (b + 1) * 128] = onehot(at == slots[b : b + 1, :])
        return carry

    lax.fori_loop(0, 8, build_place, 0)

    def build_hot(a, carry):
        rows = pl.ds(pl.multiple_of(a * 128, 128), 128)
        at = iota((128, 128), 0) + (a * 128).astype(F32)
        for b in range(8):
            hot_t[rows, b * 128 : (b + 1) * 128] = onehot(at == tok[16 + b : 17 + b, :])
        return carry

    lax.fori_loop(0, 8, build_hot, 0)
    for load in loads[5:]:
        load.wait()
    tok_cols = tok[...].T
    for half in range(2):
        rows = slice(half * LEN, (half + 1) * LEN)
        hots = jnp.concatenate(
            [onehot(iota((128, TOK), 1) == tok_cols[:, 16 + a : 17 + a]) for a in range(half * 4, half * 4 + 4)], axis=0
        )
        emb[rows, :] = mm(hots, hot_table[...]).astype(BF16)
        live = iota((LEN, 1), 0) < lens[half].astype(F32)
        masked[rows, :] = jnp.where(live, cot[rows, :].astype(F32), 0.0).astype(BF16)
        mixed_cot[rows, :] = mm_nt(masked[rows, :], out_weight[...]).astype(BF16)

    slot_cols = slots[...].T

    def place(i, carry):
        which = lax.rem(group - i + 8, 8)
        eight = pl.ds(which * 8, 8)
        await_bytes(rep_recv.at[which], got.at[eight])
        block = got[eight].astype(F32)
        rows_8 = jnp.concatenate([block[:, :CAP].reshape(192, HALF), block[:, CAP:].reshape(192, HALF)], axis=1)
        at = iota((128, 192), 1) + (which * 192).astype(F32)
        picks = jnp.concatenate([onehot(at == slot_cols[:, a : a + 1]) for a in range(8)], axis=0)
        emb[...] = (emb[...].astype(F32) + mm(picks, rows_8.astype(BF16))).astype(BF16)
        return carry

    lax.fori_loop(0, 8, place, 0)

    gain_sum[...] = jnp.zeros_like(gain_sum)

    def layer(s, carry):
        base = s * LEN
        rows = pl.ds(pl.multiple_of(base, LEN), LEN)
        length = lens[s].astype(F32)

        def norm(t, c):
            part = pl.ds(pl.multiple_of(base + t * 256, 256), 256)
            here = pl.ds(pl.multiple_of(t * 256, 256), 256)
            x = emb[part, :].astype(F32)
            center = x - mean(x)
            r = lax.rsqrt(mean(center * center) + EPS)
            hat = center * r
            xhat[here, :] = hat
            spread[here, :] = r
            normed[part, :] = (hat * gain[...]).astype(BF16)
            return c

        lax.fori_loop(0, 2, norm, 0)

        def project(cb, c):
            def raw(i):
                return mm(normed[rows, :], weight[:, i * 256 : i * 256 + 256])

            ahead = raw(0)
            for i in range(8):
                x = 0.5 * ahead
                if i < 7:
                    ahead = raw(i + 1)
                cols = slice(i * 256, i * 256 + 256)
                t = jnp.tanh(x)
                xt = x * t
                acted[:, cols] = (xt + x).astype(BF16)
                dact[:, cols] = ((0.5 * t + 0.5) * (1.0 + x - xt)).astype(BF16)
            return c

        lax.fori_loop(0, 1, project, 0)

        def cols_of(block, h):
            return pl.ds(pl.multiple_of(block * D + h * 128, 128), 128)

        inverse = jnp.where(iota((1, LEN), 1) < length, 1.0 / jnp.full((1, LEN), length), 0.0)

        def attend(pair, c):
            for h in [pair * 4 + i for i in range(4)]:
                for part in range(2):
                    keys = 256 * (part + 1)
                    at = slice(256 * part, 256 * part + 256)
                    k = acted[:keys, cols_of(3, h)]
                    x = mm_nt(acted[at, cols_of(2, h)], k) * (0.5 * SCALE)
                    t = jnp.tanh(x)
                    xt = x * t
                    a = xt + x
                    slope = (t + 1.0) * (1.0 + x - xt)
                    weights = []
                    for block in range(part + 1):
                        these = slice(256 * block, 256 * block + 256)
                        scale = inverse[:, these]
                        if block == part:
                            scale = jnp.where(iota((256, 256), 1) <= iota((256, 256), 0), scale, 0.0)
                        weights.append((a[:, these] * scale).astype(BF16))
                        attn[h, at, these] = weights[-1]
                        dattn[h, at, these] = (slope[:, these] * scale).astype(BF16)
                    w_all = weights[0] if part == 0 else jnp.concatenate(weights, axis=1)
                    per_head[at, pl.ds(pl.multiple_of(h * 128, 128), 128)] = mm(w_all, acted[:keys, cols_of(1, h)])
            return c

        lax.fori_loop(0, 1, attend, 0)

        def gate_step(t, c):
            part = pl.ds(pl.multiple_of(t * 256, 256), 256)
            whole = pl.ds(pl.multiple_of(base + t * 256, 256), 256)
            x = per_head[part, :]
            center = x - mean(x)
            r = lax.rsqrt(mean(center * center) + EPS)
            hat = center * r
            gate = acted[part, :D].astype(F32)
            g = mixed_cot[whole, :].astype(F32)
            mixed[whole, :] = (hat * gate).astype(BF16)
            dgate = (g * hat).astype(BF16)
            proj_cot[whole, :D] = dgate * dact[part, :D]
            dhat = g * gate
            dhead[part, :] = (r * (dhat - mean(dhat) - hat * mean(dhat * hat))).astype(BF16)
            return c

        lax.fori_loop(0, 2, gate_step, 0)

        def attend_back(pair, c):
            for h in [pair * 4 + i for i in range(4)]:
                head_back(h)
            return c

        def head_back(h):
            def put(block, at, to, grad):
                cols = cols_of(block, h)
                proj_cot[to, cols] = grad.astype(BF16) * dact[at, cols]

            dks, dvs = [], []
            for part in range(2):
                keys = 256 * (part + 1)
                at = slice(256 * part, 256 * part + 256)
                q = acted[at, cols_of(2, h)]
                k = acted[:keys, cols_of(3, h)]
                v = acted[:keys, cols_of(1, h)]
                do = dhead[at, pl.ds(pl.multiple_of(h * 128, 128), 128)]
                ds = mm_nt(do, v).astype(BF16) * dattn[h, at, :keys]
                put(2, at, pl.ds(pl.multiple_of(base + 256 * part, 256), 256), mm(ds, k) * (0.5 * SCALE))
                dks.append(mm_tn(ds, q) * (0.5 * SCALE))
                dvs.append(mm_tn(attn[h, at, :keys], do))
            for block, grads in ((3, dks), (1, dvs)):
                put(block, slice(0, 256), pl.ds(pl.multiple_of(base, 256), 256), grads[0] + grads[1][:256])
                put(block, slice(256, 512), pl.ds(pl.multiple_of(base + 256, 256), 256), grads[1][256:])

        lax.fori_loop(0, 1, attend_back, 0)

        for t in range(2):
            here = slice(256 * t, 256 * t + 256)
            part = pl.ds(pl.multiple_of(base + 256 * t, 256), 256)
            ncot = mm_nt(proj_cot[part, :], weight[...])
            hat = xhat[here, :]
            gain_sum[...] += jnp.sum(ncot * hat, axis=0, keepdims=True)
            d = ncot * gain[...]
            ecot = spread[here, :] * (d - mean(d) - hat * mean(d * hat))
            total = masked[part, :].astype(F32) + ecot
            emb_grad[part, :] = jnp.where(iota((256, 1), 0) + 256.0 * t < length, total, 0.0).astype(BF16)
        return carry

    lax.fori_loop(0, 2, layer, 0)

    def give(half):
        def step(i, carry):
            first = lax.rem(group + i, 8) * 8
            rows = pl.ds(pl.multiple_of(first * CAP, 192), 192)
            cold_send[half, pl.ds(first, 8)] = pack(mm(place_t[rows, :], emb_grad[:, half * HALF : (half + 1) * HALF]))
            for j in range(8):
                p = first + j

                @pl.when(p != w)
                def _():
                    give_copy(half, p).start()

            return carry

        lax.fori_loop(0, 8, step, 0)
        own = pltpu.make_async_copy(cold_send.at[half, w], cold_got.at[half, w], loc_sem.at[half])
        own.start()
        return own

    def message(ref, which, block):
        if which == 0:
            return ref.at[0, block]
        return ref.at[1, block, pl.ds(0, 32)] if which == 1 else ref.at[1, block, pl.ds(32, 16)]

    def give_copy(which, p):
        return exchange(message(cold_send, which, p), message(cold_got, which, w), 2 + which, cold_recv.at[which], p)

    def give_rest(d, carry):
        give_copy(2, lax.rem(w + d, WIDE)).start()
        return carry

    def sums_a(half):
        cols = slice(half * HALF, (half + 1) * HALF)
        out_grad = mm_tn(masked[...], mixed[:, cols]).reshape(WIDE, 8, HALF)
        gains = jnp.broadcast_to(gain_sum[:, cols].reshape(1, 1, HALF), (WIDE, 8, HALF))
        both = jnp.concatenate([out_grad, gains], axis=1).reshape(32, 2, 16, HALF).astype(BF16)
        hots = mm(hot_t[...], emb_grad[:, cols]).reshape(32, 2, 16, HALF).astype(BF16)
        for c in range(2):
            wsum[half, c, 2] = both[:, c]
            wsum[half, c, 3] = hots[:, c]

    def sums_b(half):
        cols = slice(half * HALF, (half + 1) * HALF)

        def weight_grad(cb, carry):
            grad = mm_tn(proj_cot[:, pl.ds(pl.multiple_of(cb * D, D), D)], normed[:, cols]).reshape(8, 2, 2, 16, HALF).astype(BF16)
            for c in range(2):
                for part in range(2):
                    wsum[half, c, part, pl.ds(cb * 8, 8)] = grad[:, c, part]
            return carry

        lax.fori_loop(0, 4, weight_grad, 0)

    peer = w + 1 - 2 * core
    sides = (n + 1 - 2 * lax.rem(n, 2), NARROW - 1 - n)
    parts = (lax.rem(n + 2, NARROW), sides[0], sides[1], n)

    def remote(src, dst, sems, index, to):
        return pltpu.make_async_remote_copy(
            src_ref=src, dst_ref=dst, send_sem=sems[0].at[index], recv_sem=sems[1].at[index],
            device_id=to, device_id_type=MESH,
        )

    def core_copy(half, part):
        src = wsum.at[half, 1 - core, part]
        return remote(src, core_got.at[half, part], (core_ss, core_rs), half * 4 + part, (peer, n))

    def chips(side):
        return pl.ds(16 * side, 16)

    def x_copy(half, side, on):
        src = core_sum.at[half, parts[0] if on else sides[side], chips(side)]
        return remote(src, x_got.at[half, side, on], (x_ss, x_rs), half * 6 + side * 3 + on, (w, sides[side]))

    def x_on_copy(half, side):
        dst = x_on_got.at[half, side]
        return remote(x_on.at[half, side], dst, (x_ss, x_rs), half * 6 + side * 3 + 2, (w, sides[1 - side]))

    def y_copy(half, d):
        to = lax.rem(y + d, 4)
        return remote(
            x_sum.at[half, to], y_got.at[half, d - 1], (y_ss, y_rs), half * 3 + d - 1, ((to * 8 + z) * 2 + core, n)
        )

    def z_copy(half, d):
        to = lax.rem(z + d, 8)
        return remote(
            y_sum.at[half, to], z_got.at[half, d - 1], (z_ss, z_rs), half * 7 + d - 1, ((y * 8 + to) * 2 + core, n)
        )

    def g_copy(half, d):
        to = lax.rem(n + d, NARROW)
        return remote(gathered.at[half, n], gathered.at[half, n], (g_ss, g_rs), half * 3 + d - 1, (w, to))

    def cx_copy(piece, d):
        to = lax.rem(n + d, NARROW)
        units = pl.ds(0, 2) if piece == 0 else pl.ds(piece + 1, 1)
        return remote(cx_send.at[units, d - 1], cx_got.at[units, d - 1], (cx_ss, cx_rs), piece * 3 + d - 1, (w, to))

    def core_start(half, first):
        for part in (first, first + 1):
            core_copy(half, part).start()

    def core_step(half):
        for part in range(4):
            core_copy(half, part).wait_recv()
        for j in range(4):
            part = parts[j]
            core_sum[half, part] = (wsum[half, core, part].astype(F32) + core_got[half, part].astype(F32)).astype(BF16)
            if j == 0:
                x_copy(half, 0, 1).start()
                x_copy(half, 1, 1).start()
            elif j < 3:
                x_copy(half, j - 1, 0).start()

    def x_pass(half):
        for side in range(2):
            x_copy(half, side, 1).wait_recv()
            mine = core_sum[half, sides[1 - side], chips(side)].astype(F32)
            x_on[half, side] = (mine + x_got[half, side, 1].astype(F32)).astype(BF16)
            x_on_copy(half, side).start()

    def x_step(half):
        for side in range(2):
            x_copy(half, side, 0).wait_recv()
            x_on_copy(half, side).wait_recv()
            total = core_sum[half, n, chips(side)].astype(F32) + x_got[half, side, 0].astype(F32)
            total = total + x_on_got[half, side].astype(F32)
            x_sum[half, 2 * side : 2 * side + 2] = total.astype(BF16).reshape(2, 8, 16, HALF)
        for d in (2, 1, 3):
            y_copy(half, d).start()

    def y_step(half):
        total = x_sum[half, y].astype(F32)
        for d in (1, 3, 2):
            y_copy(half, d).wait_recv()
            total = total + y_got[half, d - 1].astype(F32)
        y_sum[half] = total.astype(BF16)
        for d in range(1, 8):
            z_copy(half, d).start()

    def z_step(half):
        total = y_sum[half, z].astype(F32)
        for d in range(1, 8):
            z_copy(half, d).wait_recv()
            total = total + z_got[half, d - 1].astype(F32)
        gathered[half, n] = total
        for d in range(1, NARROW):
            g_copy(half, d).start()

    def cold_step(piece):
        await_bytes(cold_recv.at[piece], message(cold_got, piece, others))
        units = (0, 1) if piece == 0 else (piece + 1,)

        def unpack(i, carry):
            rows = pl.ds(pl.multiple_of(i * 192, 192), 192)
            for u in units:
                low = 16 * (u % 2)
                block = cold_got[u // 2, pl.ds(i * 8, 8), low : low + 32].astype(F32)
                part = block[:, low // 2 : low // 2 + CAP].reshape(192, 128)
                rows_in[rows, u * 128 : (u + 1) * 128] = part.astype(BF16)
            return carry

        lax.fori_loop(0, 8, unpack, 0)
        cols = slice(units[0] * 128, units[-1] * 128 + 128)

        def quarter(part):
            return mm(quarter_t[part], rows_in[:, cols])

        for d in (2, 1, 3):
            sums_out = quarter(lax.rem(n + d, NARROW)).astype(BF16)
            for i, u in enumerate(units):
                cx_send[u, d - 1] = sums_out[:, i * 128 : (i + 1) * 128]
            cx_copy(piece, d).start()
        cold_out[:, cols] = quarter(n)

    own0 = give(0)
    sums_a(0)
    core_start(0, 2)
    sums_b(0)
    core_start(0, 0)
    sums_a(1)
    core_start(1, 2)
    core_step(0)
    sums_b(1)
    core_start(1, 0)
    own1 = give(1)
    lax.fori_loop(1, WIDE, give_rest, 0)
    x_pass(0)
    core_step(1)

    asked = want[...].reshape(WIDE, 128)
    high = jnp.floor(asked * (1.0 / 32.0))
    low = asked - 32.0 * high
    line = iota((128, WIDE * CAP), 1)
    within = line - CAP * jnp.floor((line + 0.5) * (1.0 / CAP))
    spot = onehot(within == iota((128, WIDE * CAP), 0))
    spread_out = 32.0 * mm(high.astype(BF16), spot) + mm(low.astype(BF16), spot)
    line64 = iota((WIDE, WIDE * CAP), 1)
    start = iota((WIDE, WIDE * CAP), 0) * CAP
    mine = (line64 >= start) & (line64 < start + CAP)
    asked_line = jnp.sum(jnp.where(mine, spread_out, 0.0), axis=0, keepdims=True)
    for part in range(4):
        quarter_t[part] = onehot(iota((256, WIDE * CAP), 0) + 256.0 * part == asked_line)
    own0.wait()
    own1.wait()

    x_step(0)
    x_pass(1)
    cold_step(0)
    x_step(1)
    y_step(0)
    cold_step(1)
    y_step(1)
    cold_step(2)
    z_step(0)
    z_step(1)
    for half in range(2):
        cols = slice(half * HALF, (half + 1) * HALF)
        for d in range(1, NARROW):
            g_copy(half, d).wait_recv()
        proj_out[:, cols] = gathered[half, 0:2].reshape(32, HALF)
        out_out[:, cols] = gathered[half, 2, 0:8]
        turned[cols, :] = gathered[half, 2, 8:16].T
        for k in range(NARROW):

            @pl.when(n == k)
            def _():
                hot_out[:, cols] = gathered[half, 3, 4 * k : 4 * k + 4]

    gain_out[...] = turned[pl.ds(pl.multiple_of(w * 8, 8), 8), :].T[0:1, :]
    for piece in range(3):
        for d in range(1, NARROW):
            cx_copy(piece, d).wait_recv()
    for u in range(4):
        total = cold_out[:, u * 128 : (u + 1) * 128]
        for d in range(NARROW - 1):
            total = total + cx_got[u, d].astype(F32)
        cold_out[:, u * 128 : (u + 1) * 128] = total

    await_bytes(a2a_send.at[0], req.at[others])
    await_bytes(a2a_send.at[1], reply.at[others])
    for piece in range(3):
        await_bytes(a2a_send.at[2 + piece], message(cold_send, piece, others))
        for d in range(1, NARROW):
            cx_copy(piece, d).wait_send()
    for half in range(2):
        for part in range(4):
            core_copy(half, part).wait_send()
        for side in range(2):
            x_copy(half, side, 0).wait_send()
            x_copy(half, side, 1).wait_send()
            x_on_copy(half, side).wait_send()
        for d in range(1, NARROW):
            y_copy(half, d).wait_send()
            g_copy(half, d).wait_send()
        for d in range(1, 8):
            z_copy(half, d).wait_send()


def finish(*refs):
    sems = refs[-1]
    copies = [pltpu.make_async_copy(refs[i], refs[5 + i], sems.at[i]) for i in range(5)]
    for copy in copies:
        copy.start()
    for copy in copies:
        copy.wait()


def local(
    item_owner, item_row, hot_row, hot_flag, seq_length, cold_table, hot_table, proj_weight, out_weight, norm_gain, cotangent
):
    vm = pl.BlockSpec(memory_space=pltpu.VMEM)
    v = pltpu.VMEM
    dma = pltpu.SemaphoreType.DMA
    slots = WIDE * CAP
    block = (WIDE, 48, 256)
    i32 = jnp.int32
    scratch = [
        v((2, 1, LEN), i32), v((2, LEN), i32), v((2, LEN), i32), v((2, LEN), i32), pltpu.SMEM((2,), i32), v((1, D), F32),
        v((ROWS, D), BF16), v((TOK, D), BF16), v((D, 4 * D), BF16), v((D, D), BF16), v((TOK, D), BF16),
        v((32, 128), F32), v((8, 128), F32), v((WIDE, 1, 128), F32), v((WIDE, 1, 128), F32),
        v(block, BF16), v(block, BF16), v((slots, D), BF16), v((slots, TOK), BF16), v((TOK, TOK), BF16),
        v((TOK, D), BF16), v((TOK, D), BF16), v((LEN, D), F32), v((LEN, 1), F32),
        v((LEN, 4 * D), BF16), v((LEN, 4 * D), BF16), v((HEADS, LEN, LEN), BF16), v((HEADS, LEN, LEN), BF16),
        v((LEN, D), F32), v((TOK, D), BF16), v((TOK, D), BF16), v((TOK, D), BF16), v((LEN, D), BF16),
        v((TOK, 4 * D), BF16), v((TOK, D), BF16), v((1, D), F32),
        v((2, WIDE, 48, 128), BF16), v((2, WIDE, 48, 128), BF16),
        v((2, 2, 4, 32, 16, HALF), BF16), v((2, 4, 32, 16, HALF), BF16), v((2, 4, 32, 16, HALF), BF16),
        v((2, 2, 2, 16, 16, HALF), BF16), v((2, 2, 16, 16, HALF), BF16), v((2, 2, 16, 16, HALF), BF16),
        v((2, 4, 8, 16, HALF), BF16), v((2, 3, 8, 16, HALF), BF16),
        v((2, 8, 16, HALF), BF16), v((2, 7, 16, HALF), BF16), v((2, 4, 16, HALF), F32),
        v((4, 3, 256, 128), BF16), v((4, 3, 256, 128), BF16), v((4, 256, slots), BF16), v((D, 8), F32),
        dma((11,)), dma((2,)), dma((5,)), dma((8,)), dma((8,)), dma((3,)), dma((8,)), dma((8,)), dma((12,)), dma((12,)), dma((6,)), dma((6,)),
        dma((14,)), dma((14,)), dma((6,)), dma((6,)), dma((9,)), dma((9,)),
    ]
    shape = jax.ShapeDtypeStruct
    results = [shape((32, D), F32), shape((8, D), F32), shape((1, 8), F32), shape((256, D), F32), shape((4, D), F32)]
    hbm = pl.BlockSpec(memory_space=pl.ANY)
    parts = pl.pallas_call(
        kernel,
        out_shape=results,
        in_specs=[hbm] * 11,
        out_specs=[vm] * 5,
        scratch_shapes=scratch,
        compiler_params=pltpu.CompilerParams(collective_id=0, has_side_effects=True, vmem_limit_bytes=62 * 1024 * 1024),
    )(
        item_owner.transpose(0, 2, 1), item_row, hot_row, hot_flag, seq_length, norm_gain,
        cold_table, hot_table, proj_weight, out_weight, cotangent.reshape(TOK, D),
    )
    proj, out, gain, cold, hot = pl.pallas_call(
        finish,
        out_shape=results,
        in_specs=[vm] * 5,
        out_specs=[hbm] * 5,
        scratch_shapes=[dma((5,))],
    )(*parts)
    return proj.T, out.T, gain, cold, hot


def solution(mesh):
    both = P(("wide", "narrow"))
    in_specs = (both, both, both, both, both, P("wide"), P(), P(), P(), P(), both)
    out_specs = (P(None, "wide"), P(None, "wide"), P(None, "wide"), both, both)
    return jax.shard_map(local, mesh=mesh, in_specs=in_specs, out_specs=out_specs, check_vma=False)
```

```python
import functools

import jax
import jax.numpy as jnp
from jax import lax
from jax.experimental import pallas as pl
from jax.experimental.pallas import tpu as pltpu
from jax.sharding import PartitionSpec as P

WIDE = 64
NARROW = 4
CAP = 24
TOK = 1024
LEN = 512
D = 512
HALF = 256
HEADS = 4
ROWS = 1024
EPS = 1e-05
SCALE = 128 ** (-0.5)
MESH = pl.DeviceIdType.MESH
F32 = jnp.float32
BF16 = jnp.bfloat16


def mm(a, b):
    return jnp.dot(a, b, preferred_element_type=F32)


def mm_nt(a, b):
    return lax.dot_general(a, b, (((1,), (1,)), ((), ())), preferred_element_type=F32)


def mm_tn(a, b):
    return lax.dot_general(a, b, (((0,), (0,)), ((), ())), preferred_element_type=F32)


def iota(shape, dim):
    return lax.broadcasted_iota(jnp.int32, shape, dim).astype(F32)


def sigmoid(x):
    return 0.5 * jnp.tanh(0.5 * x) + 0.5


def onehot(mask):
    return jnp.where(mask, 1.0, 0.0).astype(BF16)


def mean(x):
    return jnp.mean(x, axis=-1, keepdims=True)


def pack(rows):
    half = rows.shape[1] // 2
    blocks = rows.reshape(-1, CAP, rows.shape[1])
    return jnp.concatenate([blocks[:, :, :half], blocks[:, :, half:]], axis=1).astype(BF16)


def kernel(
    owner_in, row_in_in, hot_row_in, hot_flag_in, lens_in, gain_in, table_in, hot_table_in, weight_in, out_weight_in, cot_in,
    proj_hbm, out_hbm, gain_hbm, cold_hbm, hot_hbm,
    proj_out, out_out, gain_out, cold_out, hot_out, store_sem,
    owner, row_in, hot_row, hot_flag, lens, gain, table, hot_table, weight, out_weight, cot, tok, slots, req, want, reply, got, rows_in, place_t, hot_t, emb, normed, xhat, spread, acted, dact,
    attn, dattn, per_head, mixed, masked, mixed_cot, dhead, proj_cot, emb_grad, gain_sum,
    cold_send, cold_got, wsum, core_got, core_sum, x_got, x_on, x_on_got, x_sum, y_got, y_sum, z_got, gathered, cx_send, cx_got, quarter_t, turned,
    load_sem, loc_sem, a2a_send, req_recv, rep_recv, cold_recv, core_ss, core_rs, x_ss, x_rs, y_ss, y_rs, z_ss, z_rs, g_ss, g_rs, cx_ss, cx_rs,
):
    w = lax.axis_index("wide")
    n = lax.axis_index("narrow")
    core = lax.rem(w, 2)
    chip = lax.div(w, 2)
    z = lax.rem(chip, 8)
    y = lax.div(chip, 8)

    loads = [
        pltpu.make_async_copy(src, dst, load_sem.at[i])
        for i, (src, dst) in enumerate(
            [
                (owner_in, owner), (row_in_in, row_in), (hot_row_in, hot_row), (hot_flag_in, hot_flag), (table_in, table),
                (lens_in, lens), (gain_in, gain), (hot_table_in, hot_table), (cot_in, cot), (out_weight_in, out_weight),
                (weight_in, weight),
            ]
        )
    ]
    for load in loads:
        load.start()

    barrier = pltpu.get_barrier_semaphore()

    def greet(d, carry):
        pl.semaphore_signal(barrier, inc=1, device_id=(lax.rem(w + d, WIDE), n), device_id_type=MESH)
        return carry

    lax.fori_loop(1, WIDE, greet, 0)
    for d in range(1, NARROW):
        pl.semaphore_signal(barrier, inc=1, device_id=(w, lax.rem(n + d, NARROW)), device_id_type=MESH)

    for load in loads[:4]:
        load.wait()
    for a in range(8):
        at = (slice(a // 4, a // 4 + 1), slice(a % 4 * 128, a % 4 * 128 + 128))
        tok[a : a + 1, :] = owner[a // 4, :, at[1]].astype(F32)
        tok[8 + a : 9 + a, :] = row_in[at].astype(F32)
        tok[16 + a : 17 + a, :] = jnp.where(hot_flag[at] == 1, hot_row[at], -1).astype(F32)

    upper = onehot(iota((128, 128), 0) < iota((128, 128), 1))
    sub = iota((128, 128), 0)
    carry = jnp.zeros((128, 1), F32)
    req_hi = jnp.zeros((128, 128), F32)
    req_lo = jnp.zeros((128, 128), F32)
    for a in range(8):
        own = tok[a : a + 1, :]
        row = tok[8 + a : 9 + a, :]
        hot = tok[16 + a : 17 + a, :]
        owns = jnp.where(sub == own, 1.0, 0.0)
        owns_b = owns.astype(BF16)
        before = mm(owns_b, upper) + carry
        rank = jnp.sum(owns * before, axis=0, keepdims=True)
        carry = carry + jnp.sum(owns, axis=1, keepdims=True)
        slots[a : a + 1, :] = jnp.where(hot >= 0.0, -1.0, own * CAP + rank)
        high = jnp.floor(row * (1.0 / 32.0))
        low = row - 32.0 * high
        ranked = sub == rank
        req_hi = req_hi + mm_nt(owns_b, jnp.where(ranked, high, 0.0).astype(BF16))
        req_lo = req_lo + mm_nt(owns_b, jnp.where(ranked, low, 0.0).astype(BF16))
    asked = 32.0 * req_hi + req_lo
    for o in range(WIDE):
        req[o] = asked[o : o + 1, :]

    pl.semaphore_wait(barrier, WIDE - 1 + NARROW - 1)

    group = lax.div(w, 8)

    def exchange(src, dst, sends, recv, p):
        return pltpu.make_async_remote_copy(
            src_ref=src, dst_ref=dst, send_sem=a2a_send.at[sends], recv_sem=recv, device_id=(p, n), device_id_type=MESH
        )

    def await_bytes(sem, view):
        pltpu.make_async_copy(view, view, sem).wait()

    others = pl.ds(0, WIDE - 1)

    def ask(d, carry):
        p = lax.rem(w + d, WIDE)
        exchange(req.at[p], want.at[w], 0, req_recv.at[group], p).start()
        return carry

    lax.fori_loop(1, WIDE, ask, 0)
    pltpu.make_async_copy(req.at[w], want.at[w], req_recv.at[group]).start()
    loads[4].wait()

    lanes = iota((CAP, ROWS), 1)

    def answer(i, carry):
        which = lax.rem(group + i, 8)
        first = which * 8
        eight = pl.ds(first, 8)
        await_bytes(req_recv.at[which], want.at[eight])
        asked8 = want[eight].reshape(8, 128).T
        picks = jnp.concatenate([jnp.where(lanes == asked8[:CAP, j : j + 1], 1.0, 0.0) for j in range(8)], axis=0)
        reply[eight] = pack(mm(picks.astype(BF16), table[...]))
        for j in range(8):
            p = first + j

            @pl.when(p != w)
            def _():
                exchange(reply.at[p], got.at[w], 1, rep_recv.at[group], p).start()

        return carry

    lax.fori_loop(0, 8, answer, 0)
    pltpu.make_async_copy(reply.at[w], got.at[w], rep_recv.at[group]).start()

    def build_place(a, carry):
        rows = pl.ds(pl.multiple_of(a * 192, 192), 192)
        at = iota((192, 128), 0) + (a * 192).astype(F32)
        for b in range(8):
            place_t[rows, b * 128 : (b + 1) * 128] = onehot(at == slots[b : b + 1, :])
        return carry

    lax.fori_loop(0, 8, build_place, 0)

    def build_hot(a, carry):
        rows = pl.ds(pl.multiple_of(a * 128, 128), 128)
        at = iota((128, 128), 0) + (a * 128).astype(F32)
        for b in range(8):
            hot_t[rows, b * 128 : (b + 1) * 128] = onehot(at == tok[16 + b : 17 + b, :])
        return carry

    lax.fori_loop(0, 8, build_hot, 0)
    for load in loads[5:]:
        load.wait()
    tok_cols = tok[...].T
    for half in range(2):
        rows = slice(half * LEN, (half + 1) * LEN)
        hots = jnp.concatenate(
            [onehot(iota((128, TOK), 1) == tok_cols[:, 16 + a : 17 + a]) for a in range(half * 4, half * 4 + 4)], axis=0
        )
        emb[rows, :] = mm(hots, hot_table[...]).astype(BF16)
        live = iota((LEN, 1), 0) < lens[half].astype(F32)
        masked[rows, :] = jnp.where(live, cot[rows, :].astype(F32), 0.0).astype(BF16)
        mixed_cot[rows, :] = mm_nt(masked[rows, :], out_weight[...]).astype(BF16)

    slot_cols = slots[...].T

    def place(i, carry):
        which = lax.rem(group - i + 8, 8)
        eight = pl.ds(which * 8, 8)
        await_bytes(rep_recv.at[which], got.at[eight])
        block = got[eight].astype(F32)
        rows_8 = jnp.concatenate([block[:, :CAP].reshape(192, HALF), block[:, CAP:].reshape(192, HALF)], axis=1)
        at = iota((128, 192), 1) + (which * 192).astype(F32)
        picks = jnp.concatenate([onehot(at == slot_cols[:, a : a + 1]) for a in range(8)], axis=0)
        emb[...] = (emb[...].astype(F32) + mm(picks, rows_8.astype(BF16))).astype(BF16)
        return carry

    lax.fori_loop(0, 8, place, 0)

    gain_sum[...] = jnp.zeros_like(gain_sum)

    def layer(s, carry):
        base = s * LEN
        rows = pl.ds(pl.multiple_of(base, LEN), LEN)
        length = lens[s].astype(F32)

        def norm(t, c):
            part = pl.ds(pl.multiple_of(base + t * 256, 256), 256)
            here = pl.ds(pl.multiple_of(t * 256, 256), 256)
            x = emb[part, :].astype(F32)
            center = x - mean(x)
            r = lax.rsqrt(mean(center * center) + EPS)
            hat = center * r
            xhat[here, :] = hat
            spread[here, :] = r
            normed[part, :] = (hat * gain[...]).astype(BF16)
            return c

        lax.fori_loop(0, 2, norm, 0)

        def project(cb, c):
            def raw(i):
                return mm(normed[rows, :], weight[:, i * 256 : i * 256 + 256])

            ahead = raw(0)
            for i in range(8):
                x = 0.5 * ahead
                if i < 7:
                    ahead = raw(i + 1)
                cols = slice(i * 256, i * 256 + 256)
                t = jnp.tanh(x)
                xt = x * t
                acted[:, cols] = (xt + x).astype(BF16)
                dact[:, cols] = ((0.5 * t + 0.5) * (1.0 + x - xt)).astype(BF16)
            return c

        lax.fori_loop(0, 1, project, 0)

        def cols_of(block, h):
            return pl.ds(pl.multiple_of(block * D + h * 128, 128), 128)

        inverse = jnp.where(iota((1, LEN), 1) < length, 1.0 / jnp.full((1, LEN), length), 0.0)

        def attend(pair, c):
            for h in [pair * 4 + i for i in range(4)]:
                for part in range(2):
                    keys = 256 * (part + 1)
                    at = slice(256 * part, 256 * part + 256)
                    k = acted[:keys, cols_of(3, h)]
                    x = mm_nt(acted[at, cols_of(2, h)], k) * (0.5 * SCALE)
                    t = jnp.tanh(x)
                    xt = x * t
                    a = xt + x
                    slope = (t + 1.0) * (1.0 + x - xt)
                    weights = []
                    for block in range(part + 1):
                        these = slice(256 * block, 256 * block + 256)
                        scale = inverse[:, these]
                        if block == part:
                            scale = jnp.where(iota((256, 256), 1) <= iota((256, 256), 0), scale, 0.0)
                        weights.append((a[:, these] * scale).astype(BF16))
                        attn[h, at, these] = weights[-1]
                        dattn[h, at, these] = (slope[:, these] * scale).astype(BF16)
                    w_all = weights[0] if part == 0 else jnp.concatenate(weights, axis=1)
                    per_head[at, pl.ds(pl.multiple_of(h * 128, 128), 128)] = mm(w_all, acted[:keys, cols_of(1, h)])
            return c

        lax.fori_loop(0, 1, attend, 0)

        def gate_step(t, c):
            part = pl.ds(pl.multiple_of(t * 256, 256), 256)
            whole = pl.ds(pl.multiple_of(base + t * 256, 256), 256)
            x = per_head[part, :]
            center = x - mean(x)
            r = lax.rsqrt(mean(center * center) + EPS)
            hat = center * r
            gate = acted[part, :D].astype(F32)
            g = mixed_cot[whole, :].astype(F32)
            mixed[whole, :] = (hat * gate).astype(BF16)
            dgate = (g * hat).astype(BF16)
            proj_cot[whole, :D] = dgate * dact[part, :D]
            dhat = g * gate
            dhead[part, :] = (r * (dhat - mean(dhat) - hat * mean(dhat * hat))).astype(BF16)
            return c

        lax.fori_loop(0, 2, gate_step, 0)

        def attend_back(pair, c):
            for h in [pair * 4 + i for i in range(4)]:
                head_back(h)
            return c

        def head_back(h):
            def put(block, at, to, grad):
                cols = cols_of(block, h)
                proj_cot[to, cols] = grad.astype(BF16) * dact[at, cols]

            dks, dvs = [], []
            for part in range(2):
                keys = 256 * (part + 1)
                at = slice(256 * part, 256 * part + 256)
                q = acted[at, cols_of(2, h)]
                k = acted[:keys, cols_of(3, h)]
                v = acted[:keys, cols_of(1, h)]
                do = dhead[at, pl.ds(pl.multiple_of(h * 128, 128), 128)]
                ds = mm_nt(do, v).astype(BF16) * dattn[h, at, :keys]
                put(2, at, pl.ds(pl.multiple_of(base + 256 * part, 256), 256), mm(ds, k) * (0.5 * SCALE))
                dks.append(mm_tn(ds, q) * (0.5 * SCALE))
                dvs.append(mm_tn(attn[h, at, :keys], do))
            for block, grads in ((3, dks), (1, dvs)):
                put(block, slice(0, 256), pl.ds(pl.multiple_of(base, 256), 256), grads[0] + grads[1][:256])
                put(block, slice(256, 512), pl.ds(pl.multiple_of(base + 256, 256), 256), grads[1][256:])

        lax.fori_loop(0, 1, attend_back, 0)

        for t in range(2):
            here = slice(256 * t, 256 * t + 256)
            part = pl.ds(pl.multiple_of(base + 256 * t, 256), 256)
            ncot = mm_nt(proj_cot[part, :], weight[...])
            hat = xhat[here, :]
            gain_sum[...] += jnp.sum(ncot * hat, axis=0, keepdims=True)
            d = ncot * gain[...]
            ecot = spread[here, :] * (d - mean(d) - hat * mean(d * hat))
            total = masked[part, :].astype(F32) + ecot
            emb_grad[part, :] = jnp.where(iota((256, 1), 0) + 256.0 * t < length, total, 0.0).astype(BF16)
        return carry

    lax.fori_loop(0, 2, layer, 0)

    def give(half):
        def step(i, carry):
            first = lax.rem(group + i, 8) * 8
            rows = pl.ds(pl.multiple_of(first * CAP, 192), 192)
            cold_send[half, pl.ds(first, 8)] = pack(mm(place_t[rows, :], emb_grad[:, half * HALF : (half + 1) * HALF]))
            for j in range(8):
                p = first + j

                @pl.when(p != w)
                def _():
                    give_copy(half, p).start()

            return carry

        lax.fori_loop(0, 8, step, 0)
        own = pltpu.make_async_copy(cold_send.at[half, w], cold_got.at[half, w], loc_sem.at[half])
        own.start()
        return own

    def message(ref, which, block):
        if which == 0:
            return ref.at[0, block]
        return ref.at[1, block, pl.ds(0, 32)] if which == 1 else ref.at[1, block, pl.ds(32, 16)]

    def give_copy(which, p):
        return exchange(message(cold_send, which, p), message(cold_got, which, w), 2 + which, cold_recv.at[which], p)

    def give_rest(d, carry):
        give_copy(2, lax.rem(w + d, WIDE)).start()
        return carry

    def sums_a(half):
        cols = slice(half * HALF, (half + 1) * HALF)
        out_grad = mm_tn(masked[...], mixed[:, cols]).reshape(WIDE, 8, HALF)
        gains = jnp.broadcast_to(gain_sum[:, cols].reshape(1, 1, HALF), (WIDE, 8, HALF))
        both = jnp.concatenate([out_grad, gains], axis=1).reshape(32, 2, 16, HALF).astype(BF16)
        hots = mm(hot_t[...], emb_grad[:, cols]).reshape(32, 2, 16, HALF).astype(BF16)
        for c in range(2):
            wsum[half, c, 2] = both[:, c]
            wsum[half, c, 3] = hots[:, c]

    def sums_b(half):
        cols = slice(half * HALF, (half + 1) * HALF)

        def weight_grad(cb, carry):
            grad = mm_tn(proj_cot[:, pl.ds(pl.multiple_of(cb * D, D), D)], normed[:, cols]).reshape(8, 2, 2, 16, HALF).astype(BF16)
            for c in range(2):
                for part in range(2):
                    wsum[half, c, part, pl.ds(cb * 8, 8)] = grad[:, c, part]
            return carry

        lax.fori_loop(0, 4, weight_grad, 0)

    peer = w + 1 - 2 * core
    sides = (n + 1 - 2 * lax.rem(n, 2), NARROW - 1 - n)
    parts = (lax.rem(n + 2, NARROW), sides[0], sides[1], n)

    def remote(src, dst, sems, index, to):
        return pltpu.make_async_remote_copy(
            src_ref=src, dst_ref=dst, send_sem=sems[0].at[index], recv_sem=sems[1].at[index],
            device_id=to, device_id_type=MESH,
        )

    def core_copy(half, part):
        src = wsum.at[half, 1 - core, part]
        return remote(src, core_got.at[half, part], (core_ss, core_rs), half * 4 + part, (peer, n))

    def chips(side):
        return pl.ds(16 * side, 16)

    def x_copy(half, side, on):
        src = core_sum.at[half, parts[0] if on else sides[side], chips(side)]
        return remote(src, x_got.at[half, side, on], (x_ss, x_rs), half * 6 + side * 3 + on, (w, sides[side]))

    def x_on_copy(half, side):
        dst = x_on_got.at[half, side]
        return remote(x_on.at[half, side], dst, (x_ss, x_rs), half * 6 + side * 3 + 2, (w, sides[1 - side]))

    def y_copy(half, d):
        to = lax.rem(y + d, 4)
        return remote(
            x_sum.at[half, to], y_got.at[half, d - 1], (y_ss, y_rs), half * 3 + d - 1, ((to * 8 + z) * 2 + core, n)
        )

    def z_copy(half, d):
        to = lax.rem(z + d, 8)
        return remote(
            y_sum.at[half, to], z_got.at[half, d - 1], (z_ss, z_rs), half * 7 + d - 1, ((y * 8 + to) * 2 + core, n)
        )

    def g_copy(half, d):
        to = lax.rem(n + d, NARROW)
        return remote(gathered.at[half, n], gathered.at[half, n], (g_ss, g_rs), half * 3 + d - 1, (w, to))

    def cx_copy(piece, d):
        to = lax.rem(n + d, NARROW)
        units = pl.ds(0, 2) if piece == 0 else pl.ds(piece + 1, 1)
        return remote(cx_send.at[units, d - 1], cx_got.at[units, d - 1], (cx_ss, cx_rs), piece * 3 + d - 1, (w, to))

    def core_start(half, first):
        for part in (first, first + 1):
            core_copy(half, part).start()

    def core_step(half):
        for part in range(4):
            core_copy(half, part).wait_recv()
        for j in range(4):
            part = parts[j]
            core_sum[half, part] = (wsum[half, core, part].astype(F32) + core_got[half, part].astype(F32)).astype(BF16)
            if j == 0:
                x_copy(half, 0, 1).start()
                x_copy(half, 1, 1).start()
            elif j < 3:
                x_copy(half, j - 1, 0).start()

    def x_pass(half):
        for side in range(2):
            x_copy(half, side, 1).wait_recv()
            mine = core_sum[half, sides[1 - side], chips(side)].astype(F32)
            x_on[half, side] = (mine + x_got[half, side, 1].astype(F32)).astype(BF16)
            x_on_copy(half, side).start()

    def x_step(half):
        for side in range(2):
            x_copy(half, side, 0).wait_recv()
            x_on_copy(half, side).wait_recv()
            total = core_sum[half, n, chips(side)].astype(F32) + x_got[half, side, 0].astype(F32)
            total = total + x_on_got[half, side].astype(F32)
            x_sum[half, 2 * side : 2 * side + 2] = total.astype(BF16).reshape(2, 8, 16, HALF)
        for d in (2, 1, 3):
            y_copy(half, d).start()

    def y_step(half):
        total = x_sum[half, y].astype(F32)
        for d in (1, 3, 2):
            y_copy(half, d).wait_recv()
            total = total + y_got[half, d - 1].astype(F32)
        y_sum[half] = total.astype(BF16)
        for d in range(1, 8):
            z_copy(half, d).start()

    def z_step(half):
        total = y_sum[half, z].astype(F32)
        for d in range(1, 8):
            z_copy(half, d).wait_recv()
            total = total + z_got[half, d - 1].astype(F32)
        gathered[half, n] = total
        for d in range(1, NARROW):
            g_copy(half, d).start()

    def cold_step(piece):
        await_bytes(cold_recv.at[piece], message(cold_got, piece, others))
        units = (0, 1) if piece == 0 else (piece + 1,)

        def unpack(i, carry):
            rows = pl.ds(pl.multiple_of(i * 192, 192), 192)
            for u in units:
                low = 16 * (u % 2)
                block = cold_got[u // 2, pl.ds(i * 8, 8), low : low + 32].astype(F32)
                part = block[:, low // 2 : low // 2 + CAP].reshape(192, 128)
                rows_in[rows, u * 128 : (u + 1) * 128] = part.astype(BF16)
            return carry

        lax.fori_loop(0, 8, unpack, 0)
        cols = slice(units[0] * 128, units[-1] * 128 + 128)

        def quarter(part):
            return mm(quarter_t[part], rows_in[:, cols])

        for d in (2, 1, 3):
            sums_out = quarter(lax.rem(n + d, NARROW)).astype(BF16)
            for i, u in enumerate(units):
                cx_send[u, d - 1] = sums_out[:, i * 128 : (i + 1) * 128]
            cx_copy(piece, d).start()
        cold_out[:, cols] = quarter(n)

    own0 = give(0)
    sums_a(0)
    core_start(0, 2)
    sums_b(0)
    core_start(0, 0)
    sums_a(1)
    core_start(1, 2)
    core_step(0)
    sums_b(1)
    core_start(1, 0)
    own1 = give(1)
    lax.fori_loop(1, WIDE, give_rest, 0)
    x_pass(0)
    core_step(1)

    asked = want[...].reshape(WIDE, 128)
    high = jnp.floor(asked * (1.0 / 32.0))
    low = asked - 32.0 * high
    line = iota((128, WIDE * CAP), 1)
    within = line - CAP * jnp.floor((line + 0.5) * (1.0 / CAP))
    spot = onehot(within == iota((128, WIDE * CAP), 0))
    spread_out = 32.0 * mm(high.astype(BF16), spot) + mm(low.astype(BF16), spot)
    line64 = iota((WIDE, WIDE * CAP), 1)
    start = iota((WIDE, WIDE * CAP), 0) * CAP
    mine = (line64 >= start) & (line64 < start + CAP)
    asked_line = jnp.sum(jnp.where(mine, spread_out, 0.0), axis=0, keepdims=True)
    for part in range(4):
        quarter_t[part] = onehot(iota((256, WIDE * CAP), 0) + 256.0 * part == asked_line)
    own0.wait()
    own1.wait()

    x_step(0)
    x_pass(1)
    cold_step(0)
    x_step(1)
    y_step(0)
    y_step(1)
    cold_step(1)
    z_step(0)
    z_step(1)
    cold_step(2)
    for half in range(2):
        cols = slice(half * HALF, (half + 1) * HALF)
        for d in range(1, NARROW):
            g_copy(half, d).wait_recv()
        proj_out[:, cols] = gathered[half, 0:2].reshape(32, HALF)
        out_out[:, cols] = gathered[half, 2, 0:8]
        turned[cols, :] = gathered[half, 2, 8:16].T
        for k in range(NARROW):

            @pl.when(n == k)
            def _():
                hot_out[:, cols] = gathered[half, 3, 4 * k : 4 * k + 4]

    gain_out[...] = turned[pl.ds(pl.multiple_of(w * 8, 8), 8), :].T[0:1, :]
    stores = [
        pltpu.make_async_copy(src, dst, store_sem.at[i])
        for i, (src, dst) in enumerate([(proj_out, proj_hbm), (out_out, out_hbm), (gain_out, gain_hbm), (hot_out, hot_hbm)])
    ]
    for store in stores:
        store.start()
    for piece in range(3):
        for d in range(1, NARROW):
            cx_copy(piece, d).wait_recv()
        units = (0, 1) if piece == 0 else (piece + 1,)
        cols = slice(units[0] * 128, units[-1] * 128 + 128)
        for u in units:
            total = cold_out[:, u * 128 : (u + 1) * 128]
            for d in range(NARROW - 1):
                total = total + cx_got[u, d].astype(F32)
            cold_out[:, u * 128 : (u + 1) * 128] = total
        stores.append(pltpu.make_async_copy(cold_out.at[:, cols], cold_hbm.at[:, cols], store_sem.at[4 + piece]))
        stores[-1].start()

    await_bytes(a2a_send.at[0], req.at[others])
    await_bytes(a2a_send.at[1], reply.at[others])
    for piece in range(3):
        await_bytes(a2a_send.at[2 + piece], message(cold_send, piece, others))
        for d in range(1, NARROW):
            cx_copy(piece, d).wait_send()
    for half in range(2):
        for part in range(4):
            core_copy(half, part).wait_send()
        for side in range(2):
            x_copy(half, side, 0).wait_send()
            x_copy(half, side, 1).wait_send()
            x_on_copy(half, side).wait_send()
        for d in range(1, NARROW):
            y_copy(half, d).wait_send()
            g_copy(half, d).wait_send()
        for d in range(1, 8):
            z_copy(half, d).wait_send()
    for store in stores:
        store.wait()


def finish(*refs):
    sems = refs[-1]
    copies = [pltpu.make_async_copy(refs[i], refs[5 + i], sems.at[i]) for i in range(5)]
    for copy in copies:
        copy.start()
    for copy in copies:
        copy.wait()


def local(
    item_owner, item_row, hot_row, hot_flag, seq_length, cold_table, hot_table, proj_weight, out_weight, norm_gain, cotangent
):
    vm = pl.BlockSpec(memory_space=pltpu.VMEM)
    v = pltpu.VMEM
    dma = pltpu.SemaphoreType.DMA
    slots = WIDE * CAP
    block = (WIDE, 48, 256)
    i32 = jnp.int32
    scratch = [
        v((32, D), F32), v((8, D), F32), v((1, 8), F32), v((256, D), F32), v((4, D), F32), dma((7,)),
        v((2, 1, LEN), i32), v((2, LEN), i32), v((2, LEN), i32), v((2, LEN), i32), pltpu.SMEM((2,), i32), v((1, D), F32),
        v((ROWS, D), BF16), v((TOK, D), BF16), v((D, 4 * D), BF16), v((D, D), BF16), v((TOK, D), BF16),
        v((32, 128), F32), v((8, 128), F32), v((WIDE, 1, 128), F32), v((WIDE, 1, 128), F32),
        v(block, BF16), v(block, BF16), v((slots, D), BF16), v((slots, TOK), BF16), v((TOK, TOK), BF16),
        v((TOK, D), BF16), v((TOK, D), BF16), v((LEN, D), F32), v((LEN, 1), F32),
        v((LEN, 4 * D), BF16), v((LEN, 4 * D), BF16), v((HEADS, LEN, LEN), BF16), v((HEADS, LEN, LEN), BF16),
        v((LEN, D), F32), v((TOK, D), BF16), v((TOK, D), BF16), v((TOK, D), BF16), v((LEN, D), BF16),
        v((TOK, 4 * D), BF16), v((TOK, D), BF16), v((1, D), F32),
        v((2, WIDE, 48, 128), BF16), v((2, WIDE, 48, 128), BF16),
        v((2, 2, 4, 32, 16, HALF), BF16), v((2, 4, 32, 16, HALF), BF16), v((2, 4, 32, 16, HALF), BF16),
        v((2, 2, 2, 16, 16, HALF), BF16), v((2, 2, 16, 16, HALF), BF16), v((2, 2, 16, 16, HALF), BF16),
        v((2, 4, 8, 16, HALF), BF16), v((2, 3, 8, 16, HALF), BF16),
        v((2, 8, 16, HALF), BF16), v((2, 7, 16, HALF), BF16), v((2, 4, 16, HALF), F32),
        v((4, 3, 256, 128), BF16), v((4, 3, 256, 128), BF16), v((4, 256, slots), BF16), v((D, 8), F32),
        dma((11,)), dma((2,)), dma((5,)), dma((8,)), dma((8,)), dma((3,)), dma((8,)), dma((8,)), dma((12,)), dma((12,)), dma((6,)), dma((6,)),
        dma((14,)), dma((14,)), dma((6,)), dma((6,)), dma((9,)), dma((9,)),
    ]
    shape = jax.ShapeDtypeStruct
    results = [shape((32, D), F32), shape((8, D), F32), shape((1, 8), F32), shape((256, D), F32), shape((4, D), F32)]
    hbm = pl.BlockSpec(memory_space=pl.ANY)
    parts = pl.pallas_call(
        kernel,
        out_shape=results,
        in_specs=[hbm] * 11,
        out_specs=[hbm] * 5,
        scratch_shapes=scratch,
        compiler_params=pltpu.CompilerParams(collective_id=0, has_side_effects=True, vmem_limit_bytes=62 * 1024 * 1024),
    )(
        item_owner.transpose(0, 2, 1), item_row, hot_row, hot_flag, seq_length, norm_gain,
        cold_table, hot_table, proj_weight, out_weight, cotangent.reshape(TOK, D),
    )
    proj, out, gain, cold, hot = pl.pallas_call(
        finish,
        out_shape=results,
        in_specs=[vm] * 5,
        out_specs=[hbm] * 5,
        scratch_shapes=[dma((5,))],
    )(*parts)
    return proj.T, out.T, gain, cold, hot


def solution(mesh):
    both = P(("wide", "narrow"))
    in_specs = (both, both, both, both, both, P("wide"), P(), P(), P(), P(), both)
    out_specs = (P(None, "wide"), P(None, "wide"), P(None, "wide"), both, both)
    return jax.shard_map(local, mesh=mesh, in_specs=in_specs, out_specs=out_specs, check_vma=False)
```

```python
import functools

import jax
import jax.numpy as jnp
from jax import lax
from jax.experimental import pallas as pl
from jax.experimental.pallas import tpu as pltpu
from jax.sharding import PartitionSpec as P

WIDE = 64
NARROW = 4
CAP = 24
TOK = 1024
LEN = 512
D = 512
HALF = 256
HEADS = 4
ROWS = 1024
EPS = 1e-05
SCALE = 128 ** (-0.5)
MESH = pl.DeviceIdType.MESH
F32 = jnp.float32
BF16 = jnp.bfloat16


def mm(a, b):
    return jnp.dot(a, b, preferred_element_type=F32)


def mm_nt(a, b):
    return lax.dot_general(a, b, (((1,), (1,)), ((), ())), preferred_element_type=F32)


def mm_tn(a, b):
    return lax.dot_general(a, b, (((0,), (0,)), ((), ())), preferred_element_type=F32)


def iota(shape, dim):
    return lax.broadcasted_iota(jnp.int32, shape, dim).astype(F32)


def sigmoid(x):
    return 0.5 * jnp.tanh(0.5 * x) + 0.5


def onehot(mask):
    return jnp.where(mask, 1.0, 0.0).astype(BF16)


def mean(x):
    return jnp.mean(x, axis=-1, keepdims=True)


def pack(rows):
    half = rows.shape[1] // 2
    blocks = rows.reshape(-1, CAP, rows.shape[1])
    return jnp.concatenate([blocks[:, :, :half], blocks[:, :, half:]], axis=1).astype(BF16)


def kernel(
    owner_in, row_in_in, hot_row_in, hot_flag_in, lens_in, gain_in, table_in, hot_table_in, weight_in, out_weight_in, cot_in,
    proj_hbm, out_hbm, gain_hbm, cold_hbm, hot_hbm,
    proj_out, out_out, gain_out, cold_out, hot_out, store_sem,
    owner, row_in, hot_row, hot_flag, lens, gain, table, hot_table, weight, out_weight, cot, tok, slots, req, want, reply, got, rows_in, place_t, hot_t, emb, normed, xhat, spread, acted, dact,
    attn, dattn, per_head, mixed, masked, mixed_cot, dhead, proj_cot, emb_grad, gain_sum,
    cold_send, cold_got, wsum, core_got, core_sum, x_got, x_on, x_on_got, x_sum, y_got, y_sum, z_got, gathered, cx_send, cx_got, quarter_t, turned,
    load_sem, loc_sem, a2a_send, req_recv, rep_recv, cold_recv, core_ss, core_rs, x_ss, x_rs, y_ss, y_rs, z_ss, z_rs, g_ss, g_rs, cx_ss, cx_rs,
):
    w = lax.axis_index("wide")
    n = lax.axis_index("narrow")
    core = lax.rem(w, 2)
    chip = lax.div(w, 2)
    z = lax.rem(chip, 8)
    y = lax.div(chip, 8)

    loads = [
        pltpu.make_async_copy(src, dst, load_sem.at[i])
        for i, (src, dst) in enumerate(
            [
                (owner_in, owner), (row_in_in, row_in), (hot_row_in, hot_row), (hot_flag_in, hot_flag), (table_in, table),
                (lens_in, lens), (gain_in, gain), (hot_table_in, hot_table), (cot_in, cot), (out_weight_in, out_weight),
                (weight_in, weight),
            ]
        )
    ]
    for load in loads:
        load.start()

    barrier = pltpu.get_barrier_semaphore()

    def greet(d, carry):
        pl.semaphore_signal(barrier, inc=1, device_id=(lax.rem(w + d, WIDE), n), device_id_type=MESH)
        return carry

    lax.fori_loop(1, WIDE, greet, 0)
    for d in range(1, NARROW):
        pl.semaphore_signal(barrier, inc=1, device_id=(w, lax.rem(n + d, NARROW)), device_id_type=MESH)

    for load in loads[:4]:
        load.wait()
    for a in range(8):
        at = (slice(a // 4, a // 4 + 1), slice(a % 4 * 128, a % 4 * 128 + 128))
        tok[a : a + 1, :] = owner[a // 4, :, at[1]].astype(F32)
        tok[8 + a : 9 + a, :] = row_in[at].astype(F32)
        tok[16 + a : 17 + a, :] = jnp.where(hot_flag[at] == 1, hot_row[at], -1).astype(F32)

    upper = onehot(iota((128, 128), 0) < iota((128, 128), 1))
    sub = iota((128, 128), 0)
    carry = jnp.zeros((128, 1), F32)
    req_both = jnp.zeros((128, 256), F32)
    for a in range(8):
        own = tok[a : a + 1, :]
        row = tok[8 + a : 9 + a, :]
        hot = tok[16 + a : 17 + a, :]
        owns = jnp.where(sub == own, 1.0, 0.0)
        owns_b = owns.astype(BF16)
        before = mm(owns_b, upper) + carry
        rank = jnp.sum(owns * before, axis=0, keepdims=True)
        carry = carry + jnp.sum(owns, axis=1, keepdims=True)
        slots[a : a + 1, :] = jnp.where(hot >= 0.0, -1.0, own * CAP + rank)
        high = jnp.floor(row * (1.0 / 32.0))
        low = row - 32.0 * high
        ranked = sub == rank
        both = jnp.concatenate([jnp.where(ranked, high, 0.0), jnp.where(ranked, low, 0.0)], axis=0)
        req_both = req_both + mm_nt(owns_b, both.astype(BF16))
    asked = 32.0 * req_both[:, :128] + req_both[:, 128:]
    for o in range(WIDE):
        req[o] = asked[o : o + 1, :]

    pl.semaphore_wait(barrier, WIDE - 1 + NARROW - 1)

    group = lax.div(w, 8)

    def exchange(src, dst, sends, recv, p):
        return pltpu.make_async_remote_copy(
            src_ref=src, dst_ref=dst, send_sem=a2a_send.at[sends], recv_sem=recv, device_id=(p, n), device_id_type=MESH
        )

    def await_bytes(sem, view):
        pltpu.make_async_copy(view, view, sem).wait()

    others = pl.ds(0, WIDE - 1)

    def ask(d, carry):
        p = lax.rem(w + d, WIDE)
        exchange(req.at[p], want.at[w], 0, req_recv.at[group], p).start()
        return carry

    lax.fori_loop(1, WIDE, ask, 0)
    pltpu.make_async_copy(req.at[w], want.at[w], req_recv.at[group]).start()
    loads[4].wait()

    lanes = iota((CAP, ROWS), 1)

    def answer(i, carry):
        which = lax.rem(group + i, 8)
        first = which * 8
        eight = pl.ds(first, 8)
        await_bytes(req_recv.at[which], want.at[eight])
        asked8 = want[eight].reshape(8, 128).T
        picks = jnp.concatenate([jnp.where(lanes == asked8[:CAP, j : j + 1], 1.0, 0.0) for j in range(8)], axis=0)
        reply[eight] = pack(mm(picks.astype(BF16), table[...]))
        for j in range(8):
            p = first + j

            @pl.when(p != w)
            def _():
                exchange(reply.at[p], got.at[w], 1, rep_recv.at[group], p).start()

        return carry

    lax.fori_loop(0, 8, answer, 0)
    pltpu.make_async_copy(reply.at[w], got.at[w], rep_recv.at[group]).start()

    def build_place(a, carry):
        rows = pl.ds(pl.multiple_of(a * 192, 192), 192)
        at = iota((192, 128), 0) + (a * 192).astype(F32)
        for b in range(8):
            place_t[rows, b * 128 : (b + 1) * 128] = onehot(at == slots[b : b + 1, :])
        return carry

    lax.fori_loop(0, 8, build_place, 0)

    def build_hot(a, carry):
        rows = pl.ds(pl.multiple_of(a * 128, 128), 128)
        at = iota((128, 128), 0) + (a * 128).astype(F32)
        for b in range(8):
            hot_t[rows, b * 128 : (b + 1) * 128] = onehot(at == tok[16 + b : 17 + b, :])
        return carry

    lax.fori_loop(0, 8, build_hot, 0)
    for load in loads[5:]:
        load.wait()
    tok_cols = tok[...].T
    for half in range(2):
        rows = slice(half * LEN, (half + 1) * LEN)
        hots = jnp.concatenate(
            [onehot(iota((128, TOK), 1) == tok_cols[:, 16 + a : 17 + a]) for a in range(half * 4, half * 4 + 4)], axis=0
        )
        emb[rows, :] = mm(hots, hot_table[...]).astype(BF16)
        live = iota((LEN, 1), 0) < lens[half].astype(F32)
        masked[rows, :] = jnp.where(live, cot[rows, :].astype(F32), 0.0).astype(BF16)
        mixed_cot[rows, :] = mm_nt(masked[rows, :], out_weight[...]).astype(BF16)

    slot_cols = slots[...].T

    def place(i, carry):
        which = lax.rem(group - i + 8, 8)
        eight = pl.ds(which * 8, 8)
        await_bytes(rep_recv.at[which], got.at[eight])
        block = got[eight].astype(F32)
        rows_8 = jnp.concatenate([block[:, :CAP].reshape(192, HALF), block[:, CAP:].reshape(192, HALF)], axis=1)
        at = iota((128, 192), 1) + (which * 192).astype(F32)
        picks = jnp.concatenate([onehot(at == slot_cols[:, a : a + 1]) for a in range(8)], axis=0)
        emb[...] = (emb[...].astype(F32) + mm(picks, rows_8.astype(BF16))).astype(BF16)
        return carry

    lax.fori_loop(0, 8, place, 0)

    gain_sum[...] = jnp.zeros_like(gain_sum)

    def layer(s, carry):
        base = s * LEN
        rows = pl.ds(pl.multiple_of(base, LEN), LEN)
        length = lens[s].astype(F32)

        def norm(t, c):
            part = pl.ds(pl.multiple_of(base + t * 256, 256), 256)
            here = pl.ds(pl.multiple_of(t * 256, 256), 256)
            x = emb[part, :].astype(F32)
            center = x - mean(x)
            r = lax.rsqrt(mean(center * center) + EPS)
            hat = center * r
            xhat[here, :] = hat
            spread[here, :] = r
            normed[part, :] = (hat * gain[...]).astype(BF16)
            return c

        lax.fori_loop(0, 2, norm, 0)

        def project(cb, c):
            def raw(i):
                return mm(normed[rows, :], weight[:, i * 256 : i * 256 + 256])

            ahead = raw(0)
            for i in range(8):
                x = 0.5 * ahead
                if i < 7:
                    ahead = raw(i + 1)
                cols = slice(i * 256, i * 256 + 256)
                t = jnp.tanh(x)
                xt = x * t
                acted[:, cols] = (xt + x).astype(BF16)
                dact[:, cols] = ((0.5 * t + 0.5) * (1.0 + x - xt)).astype(BF16)
            return c

        lax.fori_loop(0, 1, project, 0)

        def cols_of(block, h):
            return pl.ds(pl.multiple_of(block * D + h * 128, 128), 128)

        inverse = jnp.where(iota((1, LEN), 1) < length, 1.0 / jnp.full((1, LEN), length), 0.0)

        def attend(pair, c):
            for h in [pair * 4 + i for i in range(4)]:
                for part in range(2):
                    keys = 256 * (part + 1)
                    at = slice(256 * part, 256 * part + 256)
                    k = acted[:keys, cols_of(3, h)]
                    x = mm_nt(acted[at, cols_of(2, h)], k) * (0.5 * SCALE)
                    t = jnp.tanh(x)
                    xt = x * t
                    a = xt + x
                    slope = (t + 1.0) * (1.0 + x - xt)
                    weights = []
                    for block in range(part + 1):
                        these = slice(256 * block, 256 * block + 256)
                        scale = inverse[:, these]
                        if block == part:
                            scale = jnp.where(iota((256, 256), 1) <= iota((256, 256), 0), scale, 0.0)
                        weights.append((a[:, these] * scale).astype(BF16))
                        attn[h, at, these] = weights[-1]
                        dattn[h, at, these] = (slope[:, these] * scale).astype(BF16)
                    w_all = weights[0] if part == 0 else jnp.concatenate(weights, axis=1)
                    per_head[at, pl.ds(pl.multiple_of(h * 128, 128), 128)] = mm(w_all, acted[:keys, cols_of(1, h)])
            return c

        lax.fori_loop(0, 1, attend, 0)

        def gate_step(t, c):
            part = pl.ds(pl.multiple_of(t * 256, 256), 256)
            whole = pl.ds(pl.multiple_of(base + t * 256, 256), 256)
            x = per_head[part, :]
            center = x - mean(x)
            r = lax.rsqrt(mean(center * center) + EPS)
            hat = center * r
            gate = acted[part, :D].astype(F32)
            g = mixed_cot[whole, :].astype(F32)
            mixed[whole, :] = (hat * gate).astype(BF16)
            dgate = (g * hat).astype(BF16)
            proj_cot[whole, :D] = dgate * dact[part, :D]
            dhat = g * gate
            dhead[part, :] = (r * (dhat - mean(dhat) - hat * mean(dhat * hat))).astype(BF16)
            return c

        lax.fori_loop(0, 2, gate_step, 0)

        def attend_back(pair, c):
            for h in [pair * 4 + i for i in range(4)]:
                head_back(h)
            return c

        def head_back(h):
            def put(block, at, to, grad):
                cols = cols_of(block, h)
                proj_cot[to, cols] = grad.astype(BF16) * dact[at, cols]

            dks, dvs = [], []
            for part in range(2):
                keys = 256 * (part + 1)
                at = slice(256 * part, 256 * part + 256)
                q = acted[at, cols_of(2, h)]
                k = acted[:keys, cols_of(3, h)]
                v = acted[:keys, cols_of(1, h)]
                do = dhead[at, pl.ds(pl.multiple_of(h * 128, 128), 128)]
                ds = mm_nt(do, v).astype(BF16) * dattn[h, at, :keys]
                put(2, at, pl.ds(pl.multiple_of(base + 256 * part, 256), 256), mm(ds, k) * (0.5 * SCALE))
                dks.append(mm_tn(ds, q) * (0.5 * SCALE))
                dvs.append(mm_tn(attn[h, at, :keys], do))
            for block, grads in ((3, dks), (1, dvs)):
                put(block, slice(0, 256), pl.ds(pl.multiple_of(base, 256), 256), grads[0] + grads[1][:256])
                put(block, slice(256, 512), pl.ds(pl.multiple_of(base + 256, 256), 256), grads[1][256:])

        lax.fori_loop(0, 1, attend_back, 0)

        for t in range(2):
            here = slice(256 * t, 256 * t + 256)
            part = pl.ds(pl.multiple_of(base + 256 * t, 256), 256)
            ncot = mm_nt(proj_cot[part, :], weight[...])
            hat = xhat[here, :]
            gain_sum[...] += jnp.sum(ncot * hat, axis=0, keepdims=True)
            d = ncot * gain[...]
            ecot = spread[here, :] * (d - mean(d) - hat * mean(d * hat))
            total = masked[part, :].astype(F32) + ecot
            emb_grad[part, :] = jnp.where(iota((256, 1), 0) + 256.0 * t < length, total, 0.0).astype(BF16)
        return carry

    lax.fori_loop(0, 2, layer, 0)

    def give(half):
        def step(i, carry):
            first = lax.rem(group + i, 8) * 8
            rows = pl.ds(pl.multiple_of(first * CAP, 192), 192)
            cold_send[half, pl.ds(first, 8)] = pack(mm(place_t[rows, :], emb_grad[:, half * HALF : (half + 1) * HALF]))
            for j in range(8):
                p = first + j

                @pl.when(p != w)
                def _():
                    give_copy(half, p).start()

            return carry

        lax.fori_loop(0, 8, step, 0)
        own = pltpu.make_async_copy(cold_send.at[half, w], cold_got.at[half, w], loc_sem.at[half])
        own.start()
        return own

    def message(ref, which, block):
        if which == 0:
            return ref.at[0, block]
        return ref.at[1, block, pl.ds(0, 32)] if which == 1 else ref.at[1, block, pl.ds(32, 16)]

    def give_copy(which, p):
        return exchange(message(cold_send, which, p), message(cold_got, which, w), 2 + which, cold_recv.at[which], p)

    def give_rest(d, carry):
        give_copy(2, lax.rem(w + d, WIDE)).start()
        return carry

    def sums_a(half):
        cols = slice(half * HALF, (half + 1) * HALF)
        out_grad = mm_tn(masked[...], mixed[:, cols]).reshape(WIDE, 8, HALF)
        gains = jnp.broadcast_to(gain_sum[:, cols].reshape(1, 1, HALF), (WIDE, 8, HALF))
        both = jnp.concatenate([out_grad, gains], axis=1).reshape(32, 2, 16, HALF).astype(BF16)
        hots = mm(hot_t[...], emb_grad[:, cols]).reshape(32, 2, 16, HALF).astype(BF16)
        for c in range(2):
            wsum[half, c, 2] = both[:, c]
            wsum[half, c, 3] = hots[:, c]

    def sums_b(half):
        cols = slice(half * HALF, (half + 1) * HALF)

        def weight_grad(cb, carry):
            grad = mm_tn(proj_cot[:, pl.ds(pl.multiple_of(cb * D, D), D)], normed[:, cols]).reshape(8, 2, 2, 16, HALF).astype(BF16)
            for c in range(2):
                for part in range(2):
                    wsum[half, c, part, pl.ds(cb * 8, 8)] = grad[:, c, part]
            return carry

        lax.fori_loop(0, 4, weight_grad, 0)

    peer = w + 1 - 2 * core
    sides = (n + 1 - 2 * lax.rem(n, 2), NARROW - 1 - n)
    parts = (lax.rem(n + 2, NARROW), sides[0], sides[1], n)

    def remote(src, dst, sems, index, to):
        return pltpu.make_async_remote_copy(
            src_ref=src, dst_ref=dst, send_sem=sems[0].at[index], recv_sem=sems[1].at[index],
            device_id=to, device_id_type=MESH,
        )

    def core_copy(half, part):
        src = wsum.at[half, 1 - core, part]
        return remote(src, core_got.at[half, part], (core_ss, core_rs), half * 4 + part, (peer, n))

    def chips(side):
        return pl.ds(16 * side, 16)

    def x_copy(half, side, on):
        src = core_sum.at[half, parts[0] if on else sides[side], chips(side)]
        return remote(src, x_got.at[half, side, on], (x_ss, x_rs), half * 6 + side * 3 + on, (w, sides[side]))

    def x_on_copy(half, side):
        dst = x_on_got.at[half, side]
        return remote(x_on.at[half, side], dst, (x_ss, x_rs), half * 6 + side * 3 + 2, (w, sides[1 - side]))

    def y_copy(half, d):
        to = lax.rem(y + d, 4)
        return remote(
            x_sum.at[half, to], y_got.at[half, d - 1], (y_ss, y_rs), half * 3 + d - 1, ((to * 8 + z) * 2 + core, n)
        )

    def z_copy(half, d):
        to = lax.rem(z + d, 8)
        return remote(
            y_sum.at[half, to], z_got.at[half, d - 1], (z_ss, z_rs), half * 7 + d - 1, ((y * 8 + to) * 2 + core, n)
        )

    def g_copy(half, d):
        to = lax.rem(n + d, NARROW)
        return remote(gathered.at[half, n], gathered.at[half, n], (g_ss, g_rs), half * 3 + d - 1, (w, to))

    def cx_copy(piece, d):
        to = lax.rem(n + d, NARROW)
        units = pl.ds(0, 2) if piece == 0 else pl.ds(piece + 1, 1)
        return remote(cx_send.at[units, d - 1], cx_got.at[units, d - 1], (cx_ss, cx_rs), piece * 3 + d - 1, (w, to))

    def core_start(half, first):
        for part in (first, first + 1):
            core_copy(half, part).start()

    def core_step(half):
        for part in range(4):
            core_copy(half, part).wait_recv()
        for j in range(4):
            part = parts[j]
            core_sum[half, part] = (wsum[half, core, part].astype(F32) + core_got[half, part].astype(F32)).astype(BF16)
            if j == 0:
                x_copy(half, 0, 1).start()
                x_copy(half, 1, 1).start()
            elif j < 3:
                x_copy(half, j - 1, 0).start()

    def x_pass(half):
        for side in range(2):
            x_copy(half, side, 1).wait_recv()
            mine = core_sum[half, sides[1 - side], chips(side)].astype(F32)
            x_on[half, side] = (mine + x_got[half, side, 1].astype(F32)).astype(BF16)
            x_on_copy(half, side).start()

    def x_step(half):
        for side in range(2):
            x_copy(half, side, 0).wait_recv()
            x_on_copy(half, side).wait_recv()
            total = core_sum[half, n, chips(side)].astype(F32) + x_got[half, side, 0].astype(F32)
            total = total + x_on_got[half, side].astype(F32)
            x_sum[half, 2 * side : 2 * side + 2] = total.astype(BF16).reshape(2, 8, 16, HALF)
        for d in (2, 1, 3):
            y_copy(half, d).start()

    def y_step(half):
        total = x_sum[half, y].astype(F32)
        for d in (1, 3, 2):
            y_copy(half, d).wait_recv()
            total = total + y_got[half, d - 1].astype(F32)
        y_sum[half] = total.astype(BF16)
        for d in range(1, 8):
            z_copy(half, d).start()

    def z_step(half):
        total = y_sum[half, z].astype(F32)
        for d in range(1, 8):
            z_copy(half, d).wait_recv()
            total = total + z_got[half, d - 1].astype(F32)
        gathered[half, n] = total
        for d in range(1, NARROW):
            g_copy(half, d).start()

    def cold_step(piece):
        await_bytes(cold_recv.at[piece], message(cold_got, piece, others))
        units = (0, 1) if piece == 0 else (piece + 1,)

        def unpack(i, carry):
            rows = pl.ds(pl.multiple_of(i * 192, 192), 192)
            for u in units:
                low = 16 * (u % 2)
                block = cold_got[u // 2, pl.ds(i * 8, 8), low : low + 32].astype(F32)
                part = block[:, low // 2 : low // 2 + CAP].reshape(192, 128)
                rows_in[rows, u * 128 : (u + 1) * 128] = part.astype(BF16)
            return carry

        lax.fori_loop(0, 8, unpack, 0)
        cols = slice(units[0] * 128, units[-1] * 128 + 128)

        def quarter(part):
            return mm(quarter_t[part], rows_in[:, cols])

        for d in (2, 1, 3):
            sums_out = quarter(lax.rem(n + d, NARROW)).astype(BF16)
            for i, u in enumerate(units):
                cx_send[u, d - 1] = sums_out[:, i * 128 : (i + 1) * 128]
            cx_copy(piece, d).start()
        cold_out[:, cols] = quarter(n)

    own0 = give(0)
    sums_a(0)
    core_start(0, 2)
    sums_b(0)
    core_start(0, 0)
    sums_a(1)
    core_start(1, 2)
    core_step(0)
    sums_b(1)
    core_start(1, 0)
    own1 = give(1)
    lax.fori_loop(1, WIDE, give_rest, 0)
    x_pass(0)
    core_step(1)

    asked = want[...].reshape(WIDE, 128)
    high = jnp.floor(asked * (1.0 / 32.0))
    low = asked - 32.0 * high
    line = iota((128, WIDE * CAP), 1)
    within = line - CAP * jnp.floor((line + 0.5) * (1.0 / CAP))
    spot = onehot(within == iota((128, WIDE * CAP), 0))
    spread_out = 32.0 * mm(high.astype(BF16), spot) + mm(low.astype(BF16), spot)
    line64 = iota((WIDE, WIDE * CAP), 1)
    start = iota((WIDE, WIDE * CAP), 0) * CAP
    mine = (line64 >= start) & (line64 < start + CAP)
    asked_line = jnp.sum(jnp.where(mine, spread_out, 0.0), axis=0, keepdims=True)
    for part in range(4):
        quarter_t[part] = onehot(iota((256, WIDE * CAP), 0) + 256.0 * part == asked_line)
    own0.wait()
    own1.wait()

    x_step(0)
    x_pass(1)
    cold_step(0)
    x_step(1)
    y_step(0)
    y_step(1)
    cold_step(1)
    z_step(0)
    cold_step(2)
    z_step(1)
    for half in range(2):
        cols = slice(half * HALF, (half + 1) * HALF)
        for d in range(1, NARROW):
            g_copy(half, d).wait_recv()
        proj_out[:, cols] = gathered[half, 0:2].reshape(32, HALF)
        out_out[:, cols] = gathered[half, 2, 0:8]
        turned[cols, :] = gathered[half, 2, 8:16].T
        for k in range(NARROW):

            @pl.when(n == k)
            def _():
                hot_out[:, cols] = gathered[half, 3, 4 * k : 4 * k + 4]

    gain_out[...] = turned[pl.ds(pl.multiple_of(w * 8, 8), 8), :].T[0:1, :]
    stores = [
        pltpu.make_async_copy(src, dst, store_sem.at[i])
        for i, (src, dst) in enumerate([(proj_out, proj_hbm), (out_out, out_hbm), (gain_out, gain_hbm), (hot_out, hot_hbm)])
    ]
    for store in stores:
        store.start()
    for piece in range(3):
        for d in range(1, NARROW):
            cx_copy(piece, d).wait_recv()
        units = (0, 1) if piece == 0 else (piece + 1,)
        cols = slice(units[0] * 128, units[-1] * 128 + 128)
        for u in units:
            total = cold_out[:, u * 128 : (u + 1) * 128]
            for d in range(NARROW - 1):
                total = total + cx_got[u, d].astype(F32)
            cold_out[:, u * 128 : (u + 1) * 128] = total
        stores.append(pltpu.make_async_copy(cold_out.at[:, cols], cold_hbm.at[:, cols], store_sem.at[4 + piece]))
        stores[-1].start()

    await_bytes(a2a_send.at[0], req.at[others])
    await_bytes(a2a_send.at[1], reply.at[others])
    for piece in range(3):
        await_bytes(a2a_send.at[2 + piece], message(cold_send, piece, others))
        for d in range(1, NARROW):
            cx_copy(piece, d).wait_send()
    for half in range(2):
        for part in range(4):
            core_copy(half, part).wait_send()
        for side in range(2):
            x_copy(half, side, 0).wait_send()
            x_copy(half, side, 1).wait_send()
            x_on_copy(half, side).wait_send()
        for d in range(1, NARROW):
            y_copy(half, d).wait_send()
            g_copy(half, d).wait_send()
        for d in range(1, 8):
            z_copy(half, d).wait_send()
    for store in stores:
        store.wait()


def finish(*refs):
    sems = refs[-1]
    copies = [pltpu.make_async_copy(refs[i], refs[5 + i], sems.at[i]) for i in range(5)]
    for copy in copies:
        copy.start()
    for copy in copies:
        copy.wait()


def local(
    item_owner, item_row, hot_row, hot_flag, seq_length, cold_table, hot_table, proj_weight, out_weight, norm_gain, cotangent
):
    vm = pl.BlockSpec(memory_space=pltpu.VMEM)
    v = pltpu.VMEM
    dma = pltpu.SemaphoreType.DMA
    slots = WIDE * CAP
    block = (WIDE, 48, 256)
    i32 = jnp.int32
    scratch = [
        v((32, D), F32), v((8, D), F32), v((1, 8), F32), v((256, D), F32), v((4, D), F32), dma((7,)),
        v((2, 1, LEN), i32), v((2, LEN), i32), v((2, LEN), i32), v((2, LEN), i32), pltpu.SMEM((2,), i32), v((1, D), F32),
        v((ROWS, D), BF16), v((TOK, D), BF16), v((D, 4 * D), BF16), v((D, D), BF16), v((TOK, D), BF16),
        v((32, 128), F32), v((8, 128), F32), v((WIDE, 1, 128), F32), v((WIDE, 1, 128), F32),
        v(block, BF16), v(block, BF16), v((slots, D), BF16), v((slots, TOK), BF16), v((TOK, TOK), BF16),
        v((TOK, D), BF16), v((TOK, D), BF16), v((LEN, D), F32), v((LEN, 1), F32),
        v((LEN, 4 * D), BF16), v((LEN, 4 * D), BF16), v((HEADS, LEN, LEN), BF16), v((HEADS, LEN, LEN), BF16),
        v((LEN, D), F32), v((TOK, D), BF16), v((TOK, D), BF16), v((TOK, D), BF16), v((LEN, D), BF16),
        v((TOK, 4 * D), BF16), v((TOK, D), BF16), v((1, D), F32),
        v((2, WIDE, 48, 128), BF16), v((2, WIDE, 48, 128), BF16),
        v((2, 2, 4, 32, 16, HALF), BF16), v((2, 4, 32, 16, HALF), BF16), v((2, 4, 32, 16, HALF), BF16),
        v((2, 2, 2, 16, 16, HALF), BF16), v((2, 2, 16, 16, HALF), BF16), v((2, 2, 16, 16, HALF), BF16),
        v((2, 4, 8, 16, HALF), BF16), v((2, 3, 8, 16, HALF), BF16),
        v((2, 8, 16, HALF), BF16), v((2, 7, 16, HALF), BF16), v((2, 4, 16, HALF), F32),
        v((4, 3, 256, 128), BF16), v((4, 3, 256, 128), BF16), v((4, 256, slots), BF16), v((D, 8), F32),
        dma((11,)), dma((2,)), dma((5,)), dma((8,)), dma((8,)), dma((3,)), dma((8,)), dma((8,)), dma((12,)), dma((12,)), dma((6,)), dma((6,)),
        dma((14,)), dma((14,)), dma((6,)), dma((6,)), dma((9,)), dma((9,)),
    ]
    shape = jax.ShapeDtypeStruct
    results = [shape((32, D), F32), shape((8, D), F32), shape((1, 8), F32), shape((256, D), F32), shape((4, D), F32)]
    hbm = pl.BlockSpec(memory_space=pl.ANY)
    parts = pl.pallas_call(
        kernel,
        out_shape=results,
        in_specs=[hbm] * 11,
        out_specs=[hbm] * 5,
        scratch_shapes=scratch,
        compiler_params=pltpu.CompilerParams(collective_id=0, has_side_effects=True, vmem_limit_bytes=62 * 1024 * 1024),
    )(
        item_owner.transpose(0, 2, 1), item_row, hot_row, hot_flag, seq_length, norm_gain,
        cold_table, hot_table, proj_weight, out_weight, cotangent.reshape(TOK, D),
    )
    proj, out, gain, cold, hot = pl.pallas_call(
        finish,
        out_shape=results,
        in_specs=[vm] * 5,
        out_specs=[hbm] * 5,
        scratch_shapes=[dma((5,))],
    )(*parts)
    return proj.T, out.T, gain, cold, hot


def solution(mesh):
    both = P(("wide", "narrow"))
    in_specs = (both, both, both, both, both, P("wide"), P(), P(), P(), P(), both)
    out_specs = (P(None, "wide"), P(None, "wide"), P(None, "wide"), both, both)
    return jax.shard_map(local, mesh=mesh, in_specs=in_specs, out_specs=out_specs, check_vma=False)
```
